256 devices in a mesh: leaf: 256 (over y, z, x, core).
Axes of the slice: x: 4, y: 4, z: 8, core: 2. Of those that a mesh axis runs over, the one named last changes fastest.
Arguments:
- rhs: float32 [16, 524288], P(None, 'leaf'), may hold values from -180 to 180
- box_rows: int32 [1024], P('leaf'), may hold values from 384 to 512, as said below
- dense: float32 [1024, 512, 256], P('leaf'), may hold values from -0.375 to 0.375
- row_basis: float32 [1024, 512, 128], P('leaf'), may hold values from -0.5 to 0.5
- col_basis: float32 [1024, 256, 128], P('leaf'), may hold values from -0.375 to 0.375
- local_col_transfer: float32 [768, 256, 128], P('leaf'), may hold values from -0.4375 to 0.4375
- local_row_transfer: float32 [768, 256, 128], P('leaf'), may hold values from -0.4375 to 0.4375
- local_coupling: float32 [768, 2, 128, 128], P('leaf'), may hold values from -0.5 to 0.5
- upper_col_transfer: float32 [7, 256, 128], replicated, may hold values from -0.4375 to 0.4375
- upper_row_transfer: float32 [7, 256, 128], replicated, may hold values from -0.4375 to 0.4375
- upper_coupling: float32 [8, 2, 128, 128], replicated, may hold values from -0.5 to 0.5
Outputs:
- solution: float32 [16, 262144], P(None, 'leaf')
The draws below stay inside these ranges and needn't reach their ends.
Inputs may be any that keep to these rules, and one draw needn't show every extreme that they name: `box_rows`: 512 in some leaf and 384 in another, in every draw.
All inputs are finite; a program needn't handle non-finite values.
Results may differ from the reference program's by a relative error of at most 0.00017.
Values sent between devices are 32-bit elements; how exact they have to be, the bound alone decides.
No kernel may reach another device: no remote copies, remote signals or barrier semaphores. Data moves between devices by JAX's collectives and lax.ppermute only.
A program may use at most 128 MiB of HBM per device.

```python
import jax
import jax.numpy as jnp
from jax import lax

RANK = 128
LEAF_COLS = 256
LEAF_ROWS = 512
RHS_COUNT = 16
ITERS = 2
LEAF_DEV = 4
LEAVES = 1024
COLS = 262144
ROWS = 524288
LOCAL_LEVELS = 2
UP_LEVELS = 8
N_LEAF = 256


def draw_rhs(key, part):
    key = jax.random.fold_in(key, 11)
    streams = jax.random.split(key, 3)
    position = jnp.arange(ROWS, dtype=jnp.float32) / max(ROWS - 1, 1)
    trend_factor = 1.0 + 2.0 * position
    row_scale = jnp.exp(jax.random.uniform(streams[0], (1, ROWS)) * jnp.log(10.0))
    col_scale = jnp.exp(jax.random.uniform(streams[1], (RHS_COUNT, 1)) * jnp.log(10.0))
    pattern = jnp.clip(jax.random.normal(streams[2], (RHS_COUNT, ROWS)), -4.0, 4.0)
    values = 0.15 * pattern * row_scale * col_scale * trend_factor[None, :]
    return values.astype(jnp.float32)


def draw_box_rows(key, part):
    key = jax.random.fold_in(key, 23)
    streams = jax.random.split(key, 3)
    lowest = LEAF_ROWS - LEAF_ROWS // 4
    counts = jax.random.randint(streams[0], (LEAVES,), lowest, LEAF_ROWS + 1)
    first_leaf = jax.random.randint(streams[1], (), 0, LEAVES)
    second_leaf = (first_leaf + jax.random.randint(streams[2], (), 1, LEAVES)) % LEAVES
    counts = counts.at[first_leaf].set(LEAF_ROWS)
    counts = counts.at[second_leaf].set(lowest)
    return counts.astype(jnp.int32)


def levels(key, shape, pieces, low, top_value):
    def one(dim, shards_of):
        draws = jax.random.uniform(jax.random.fold_in(jax.random.fold_in(key, 6), dim), (shards_of,), jnp.float32, low / len(pieces), top_value / len(pieces))
        return jnp.repeat(jnp.exp(draws), shape[dim] // shards_of).reshape((-1,) + (1,) * (len(shape) - dim - 1))

    gain = one(*pieces[0])
    for cut in pieces[1:]:
        gain = gain * one(*cut)
    return gain


def gaussian(own_key, extent, deviation, limit, pieces=(), kind=jnp.bfloat16):
    values = deviation * jax.random.normal(own_key, extent, jnp.float32)
    if pieces:
        values = values * levels(own_key, extent, pieces, -0.22, 0.18)
    return jnp.clip(values, -limit, limit).astype(kind)


def setup_inputs(seed: int = 0) -> dict:
    key_list = jax.random.split(jax.random.key(seed), 12)
    return {
        "rhs": draw_rhs(jax.random.fold_in(key_list[11], 71), 0),
        "box_rows": draw_box_rows(jax.random.fold_in(key_list[11], 71), 0),
        "dense": gaussian(key_list[2], (LEAVES, LEAF_ROWS, LEAF_COLS), LEAF_COLS ** -0.5, 0.375, ((0, 256),), jnp.float32),
        "row_basis": gaussian(key_list[3], (LEAVES, LEAF_ROWS, RANK), RANK ** -0.5, 0.5, ((0, 256),), jnp.float32),
        "col_basis": gaussian(key_list[4], (LEAVES, LEAF_COLS, RANK), LEAF_COLS ** -0.5, 0.375, ((0, 256),), jnp.float32),
        "local_col_transfer": gaussian(key_list[5], (N_LEAF * (LEAF_DEV - 1), 2 * RANK, RANK), (3 * RANK // 2) ** -0.5, 0.4375, ((0, 256),), jnp.float32),
        "local_row_transfer": gaussian(key_list[6], (N_LEAF * (LEAF_DEV - 1), 2 * RANK, RANK), (3 * RANK // 2) ** -0.5, 0.4375, ((0, 256),), jnp.float32),
        "local_coupling": gaussian(key_list[7], (N_LEAF * (LEAF_DEV - 1), 2, RANK, RANK), RANK ** -0.5, 0.5, ((0, 256),), jnp.float32),
        "upper_col_transfer": gaussian(key_list[8], (UP_LEVELS - 1, 2 * RANK, RANK), (3 * RANK // 2) ** -0.5, 0.4375, (), jnp.float32),
        "upper_row_transfer": gaussian(key_list[9], (UP_LEVELS - 1, 2 * RANK, RANK), (3 * RANK // 2) ** -0.5, 0.4375, (), jnp.float32),
        "upper_coupling": gaussian(key_list[10], (UP_LEVELS, 2, RANK, RANK), RANK ** -0.5, 0.5, (), jnp.float32),
    }


precise = lax.Precision.HIGHEST

def climb(children, transfer):
    node_count = transfer.shape[0]
    paired = children.reshape(node_count, 2, children.shape[1], children.shape[2])
    blocks = transfer.reshape(node_count, 2, children.shape[2], transfer.shape[2])
    return jnp.einsum('minj,mijk->mnk', paired, blocks, precision=precise)

def descend(parent, transfer):
    node_count = transfer.shape[0]
    blocks = transfer.reshape(node_count, 2, transfer.shape[2], transfer.shape[2])
    spread = jnp.einsum('mnk,mijk->minj', parent, blocks, precision=precise)
    return spread.reshape(node_count * 2, parent.shape[1], parent.shape[2])

def couple_forward(children, coupling):
    node_count = coupling.shape[0]
    paired = children.reshape(node_count, 2, children.shape[1], children.shape[2])
    sibling = jnp.flip(paired, 1)
    gained = jnp.einsum('minj,mijk->mink', sibling, coupling, precision=precise)
    return gained.reshape(children.shape)

def couple_adjoint(children, coupling):
    node_count = coupling.shape[0]
    paired = children.reshape(node_count, 2, children.shape[1], children.shape[2])
    gained = jnp.einsum('mink,mijk->minj', paired, coupling, precision=precise)
    return jnp.flip(gained, 1).reshape(children.shape)

def tree_levels(leaf_summary, climbers, descenders, couplers, cross_fn):
    summaries = [leaf_summary]
    coupled = []
    height_total = len(couplers)
    for height in range(height_total):
        coupled.append(cross_fn(summaries[height], couplers[height]))
        if height + 1 < height_total:
            summaries.append(climb(summaries[height], climbers[height]))
    potential = coupled[height_total - 1]
    for height in reversed(range(height_total - 1)):
        potential = coupled[height] + descend(potential, descenders[height])
    return potential

def level_data(local_array, upper_array):
    per_device = local_array.reshape((N_LEAF, LEAF_DEV - 1) + local_array.shape[1:])
    collected = []
    offset = 0
    for height in range(LOCAL_LEVELS):
        node_width = LEAF_DEV // 2 ** (height + 1)
        chosen = per_device[:, offset:offset + node_width]
        collected.append(chosen.reshape((N_LEAF * node_width,) + local_array.shape[1:]))
        offset += node_width
    for height in range(upper_array.shape[0]):
        node_count = N_LEAF // 2 ** (height + 1)
        collected.append(jnp.broadcast_to(upper_array[height], (node_count,) + upper_array.shape[1:]))
    return collected

def reference(rhs, box_rows, dense, row_basis, col_basis, local_col_transfer, local_row_transfer, local_coupling, upper_col_transfer, upper_row_transfer, upper_coupling):
    slots = lax.broadcasted_iota(jnp.int32, (LEAVES, LEAF_ROWS), 1)
    live_rows = (slots < box_rows.astype(jnp.int32)[:, None]).astype(jnp.float32)
    col_levels = level_data(local_col_transfer, upper_col_transfer)
    row_levels = level_data(local_row_transfer, upper_row_transfer)
    couplers = level_data(local_coupling, upper_coupling)

    def forward(vector):
        blocks = vector.reshape(RHS_COUNT, LEAVES, LEAF_COLS)
        summary = jnp.einsum('nqc,qck->qnk', blocks, col_basis, precision=precise)
        potential = tree_levels(summary, col_levels, row_levels, couplers, couple_forward)
        result = jnp.einsum('qrc,nqc->nqr', dense, blocks, precision=precise)
        result = result + jnp.einsum('qrk,qnk->nqr', row_basis, potential, precision=precise)
        return (result * live_rows[None]).reshape(RHS_COUNT, ROWS)

    def adjoint(vector):
        blocks = vector.reshape(RHS_COUNT, LEAVES, LEAF_ROWS) * live_rows[None]
        summary = jnp.einsum('nqr,qrk->qnk', blocks, row_basis, precision=precise)
        potential = tree_levels(summary, row_levels, col_levels, couplers, couple_adjoint)
        result = jnp.einsum('qrc,nqr->nqc', dense, blocks, precision=precise)
        result = result + jnp.einsum('qck,qnk->nqc', col_basis, potential, precision=precise)
        return result.reshape(RHS_COUNT, COLS)

    def column_norm(vector):
        return jnp.sqrt(lax.optimization_barrier(jnp.sum(vector * vector, axis=1)))
    masked_rhs = rhs * live_rows.reshape(1, ROWS)
    beta_norm = column_norm(masked_rhs)
    left_vector = masked_rhs / beta_norm[:, None]
    unscaled = adjoint(left_vector)
    alpha_norm = column_norm(unscaled)
    right_vector = unscaled / alpha_norm[:, None]
    search = right_vector
    solution = jnp.zeros((RHS_COUNT, COLS), jnp.float32)
    phi_bar = beta_norm
    rho_bar = alpha_norm
    for iteration in range(ITERS):
        unscaled = forward(right_vector) - alpha_norm[:, None] * left_vector
        beta_norm = column_norm(unscaled)
        left_vector = unscaled / beta_norm[:, None]
        unscaled = adjoint(left_vector) - beta_norm[:, None] * right_vector
        alpha_norm = column_norm(unscaled)
        right_vector = unscaled / alpha_norm[:, None]
        rho_value = jnp.sqrt(rho_bar * rho_bar + beta_norm * beta_norm)
        cosine = rho_bar / rho_value
        sine_value = beta_norm / rho_value
        theta_value = sine_value * alpha_norm
        rho_bar = -cosine * alpha_norm
        phi_value = cosine * phi_bar
        phi_bar = sine_value * phi_bar
        solution = solution + (phi_value / rho_value)[:, None] * search
        search = right_vector - (theta_value / rho_value)[:, None] * search
    return solution
```

```python
import functools

import jax
import jax.numpy as jnp
from jax import lax
from jax.experimental import pallas as pl
from jax.experimental.pallas import tpu as pltpu
from jax.sharding import PartitionSpec as P

RHS = 16
RANK = 128
LEAF_DEV = 4
LEAF_ROWS = 512
LEAF_COLS = 256
MSG = 24
GROUP = 16
VMEM_LIMIT = 40 * 1024 * 1024

f32 = jnp.float32
bf16 = jnp.bfloat16


def split(v):
    head = v.astype(bf16)
    return head, (v - head.astype(f32)).astype(bf16)


def mm(x, w, transposed=False):
    xh, xl = split(x)
    wh, wl = split(w)
    dims = (((1,), (1 if transposed else 0,)), ((), ()))
    n = x.shape[0]
    both = lax.dot_general(jnp.concatenate([xh, xl], 0), wh, dims, preferred_element_type=f32)
    rest = lax.dot_general(xh, wl, dims, preferred_element_type=f32)
    return both[:n] + (both[n:] + rest)


def eye():
    return (
        lax.broadcasted_iota(jnp.int32, (RHS, RANK), 0)
        == lax.broadcasted_iota(jnp.int32, (RHS, RANK), 1)
    ).astype(f32)


def stat_row(column):
    row = jnp.sum(column * eye(), axis=0, keepdims=True)
    first = (lax.broadcasted_iota(jnp.int32, (8, RANK), 0) == 0).astype(f32)
    return row * first


def stat_column(block):
    row = jnp.sum(block, axis=0, keepdims=True)
    return jnp.sum(row * eye(), axis=1, keepdims=True)


def sum_squares(v):
    return jnp.sum(v * v, axis=1, keepdims=True)


def send(out_ref, value):
    for peer in range(GROUP):
        out_ref[peer] = value


def local_up(parts, basis_ref, climb_ref):
    leaf = [mm(parts[q], basis_ref[q]) for q in range(LEAF_DEV)]
    node = [
        mm(jnp.concatenate([leaf[2 * m], leaf[2 * m + 1]], 1), climb_ref[m]) for m in range(2)
    ]
    root = mm(jnp.concatenate(node, 1), climb_ref[2])
    return leaf, node, root


def couple(sibling, coupling_ref, node, child, adjoint):
    if adjoint:
        return mm(sibling, coupling_ref[node, 1 - child], transposed=True)
    return mm(sibling, coupling_ref[node, child])


def local_down(root, leaf, node, coupling_ref, descend_ref, adjoint):
    spread = mm(root, descend_ref[2], transposed=True)
    out = []
    for m in range(2):
        here = couple(node[1 - m], coupling_ref, 2, m, adjoint)
        here = here + spread[:, m * RANK : (m + 1) * RANK]
        below = mm(here, descend_ref[m], transposed=True)
        for i in range(2):
            gained = couple(leaf[2 * m + 1 - i], coupling_ref, m, i, adjoint)
            out.append(gained + below[:, i * RANK : (i + 1) * RANK])
    return out


def live_mask(rows_ref, q):
    slots = lax.broadcasted_iota(jnp.int32, (RHS, LEAF_ROWS), 1)
    return (slots < rows_ref[q]).astype(f32)


def row_part(v, q):
    return v[:, q * LEAF_ROWS : (q + 1) * LEAF_ROWS]


def col_part(v, q):
    return v[:, q * LEAF_COLS : (q + 1) * LEAF_COLS]


def finish_up(parts, basis_ref, climb_ref, msg_ref, keep_ref, squares):
    leaf, node, root = local_up(parts, basis_ref, climb_ref)
    for k, value in enumerate(leaf + node):
        keep_ref[k] = value
    send(msg_ref, jnp.concatenate([root, stat_row(squares)], 0))


def start_kernel(rows_ref, rhs_ref, row_basis_ref, local_row_ref, z_ref, msg_ref, keep_ref):
    parts = []
    squares = jnp.zeros((RHS, 1), f32)
    for q in range(LEAF_DEV):
        part = rhs_ref[:, q * LEAF_ROWS : (q + 1) * LEAF_ROWS] * live_mask(rows_ref, q)
        z_ref[:, q * LEAF_ROWS : (q + 1) * LEAF_ROWS] = part
        squares = squares + sum_squares(part)
        parts.append(part)
    finish_up(parts, row_basis_ref, local_row_ref, msg_ref, keep_ref, squares)


def lower_kernel(me_ref, recv_ref, climb_ref, msg_ref, sib_ref, scratch_ref):
    place = me_ref[0] % GROUP
    level = [recv_ref[d, :RHS] for d in range(GROUP)]
    sib_ref[0] = recv_ref[place ^ 1, :RHS]
    base = 0
    for height in range(4):
        count = len(level) // 2
        paired = jnp.concatenate(
            [jnp.concatenate([level[2 * m], level[2 * m + 1]], 1) for m in range(count)], 0
        )
        parents = mm(paired, climb_ref[height])
        level = [parents[m * RHS : (m + 1) * RHS] for m in range(count)]
        if height < 3:
            for m in range(count):
                scratch_ref[base + m] = level[m]
            sib_ref[height + 1] = scratch_ref[base + ((place >> (height + 1)) ^ 1)]
            base += count
    stats = recv_ref[0, RHS:]
    for d in range(1, GROUP):
        stats = stats + recv_ref[d, RHS:]
    send(msg_ref, jnp.concatenate([level[0], stats], 0))


def upper_potential(me_ref, recv_ref, sib_ref, climb_ref, descend_ref, coupling_ref, scratch_ref, adjoint):
    me = me_ref[0]
    place = me // GROUP
    level = [recv_ref[d, :RHS] for d in range(GROUP)]
    siblings = [sib_ref[j] for j in range(4)]
    siblings.append(recv_ref[place ^ 1, :RHS])
    base = 0
    for height in range(3):
        count = len(level) // 2
        paired = jnp.concatenate(
            [jnp.concatenate([level[2 * m], level[2 * m + 1]], 1) for m in range(count)], 0
        )
        parents = mm(paired, climb_ref[4 + height])
        level = [parents[m * RHS : (m + 1) * RHS] for m in range(count)]
        for m in range(count):
            scratch_ref[base + m] = level[m]
        siblings.append(scratch_ref[base + ((place >> (height + 1)) ^ 1)])
        base += count
    gained = []
    for j in range(8):
        child = (me >> j) & 1
        if adjoint:
            gained.append(mm(siblings[j], coupling_ref[j, 1 - child], transposed=True))
        else:
            gained.append(mm(siblings[j], coupling_ref[j, child]))
    potential = gained[7]
    for j in reversed(range(7)):
        child = (me >> j) & 1
        half = descend_ref[j, pl.ds(pl.multiple_of(child * RANK, RANK), RANK), :]
        potential = gained[j] + mm(potential, half, transposed=True)
    stats = recv_ref[0, RHS:]
    for d in range(1, GROUP):
        stats = stats + recv_ref[d, RHS:]
    return potential, jnp.sqrt(stat_column(stats))


def adjoint_kernel(
    first,
    me_ref,
    recv_ref,
    sib_ref,
    up_row_ref,
    up_col_ref,
    up_couple_ref,
    keep_ref,
    dense_ref,
    col_basis_ref,
    local_row_ref,
    local_col_ref,
    local_couple_ref,
    z_ref,
    *rest,
):
    if first:
        u_ref, v_ref, norm_ref, msg_ref, next_ref, scratch_ref = rest
    else:
        prev_ref, u_ref, v_ref, norm_ref, msg_ref, next_ref, scratch_ref = rest
    potential, norm = upper_potential(
        me_ref, recv_ref, sib_ref, up_row_ref, up_col_ref, up_couple_ref, scratch_ref, True
    )
    inverse = 1.0 / norm
    norm_ref[...] = jnp.broadcast_to(norm, (RHS, RANK))
    leaf = [keep_ref[q] for q in range(LEAF_DEV)]
    node = [keep_ref[LEAF_DEV + m] for m in range(2)]
    down = local_down(potential, leaf, node, local_couple_ref, local_col_ref, True)
    parts = []
    squares = jnp.zeros((RHS, 1), f32)
    for q in range(LEAF_DEV):
        rows = slice(q * LEAF_ROWS, (q + 1) * LEAF_ROWS)
        cols = slice(q * LEAF_COLS, (q + 1) * LEAF_COLS)
        z = z_ref[:, rows]
        u_ref[:, rows] = z * inverse
        v = mm(z, dense_ref[q]) + mm(down[q], col_basis_ref[q], transposed=True)
        v = v * inverse
        if not first:
            v = v - norm * prev_ref[:, cols]
        v_ref[:, cols] = v
        squares = squares + sum_squares(v)
        parts.append(v)
    finish_up(parts, col_basis_ref, local_col_ref, msg_ref, next_ref, squares)


def forward_kernel(
    last,
    me_ref,
    recv_ref,
    sib_ref,
    up_row_ref,
    up_col_ref,
    up_couple_ref,
    keep_ref,
    dense_ref,
    row_basis_ref,
    local_row_ref,
    local_col_ref,
    local_couple_ref,
    rows_ref,
    x_ref,
    u_ref,
    *rest,
):
    if last:
        v_ref, norm_ref, msg_ref, scratch_ref = rest
    else:
        v_ref, z_ref, norm_ref, msg_ref, next_ref, scratch_ref = rest
    potential, norm = upper_potential(
        me_ref, recv_ref, sib_ref, up_col_ref, up_row_ref, up_couple_ref, scratch_ref, False
    )
    inverse = 1.0 / norm
    norm_ref[...] = jnp.broadcast_to(norm, (RHS, RANK))
    leaf = [keep_ref[q] for q in range(LEAF_DEV)]
    node = [keep_ref[LEAF_DEV + m] for m in range(2)]
    down = local_down(potential, leaf, node, local_couple_ref, local_row_ref, False)
    parts = []
    squares = jnp.zeros((RHS, 1), f32)
    for q in range(LEAF_DEV):
        rows = slice(q * LEAF_ROWS, (q + 1) * LEAF_ROWS)
        cols = slice(q * LEAF_COLS, (q + 1) * LEAF_COLS)
        x = x_ref[:, cols]
        v_ref[:, cols] = x * inverse
        z = mm(x, dense_ref[q], transposed=True) + mm(down[q], row_basis_ref[q], transposed=True)
        z = z * live_mask(rows_ref, q) * inverse - norm * u_ref[:, rows]
        squares = squares + sum_squares(z)
        if not last:
            z_ref[:, rows] = z
            parts.append(z)
    if last:
        send(msg_ref, stat_row(squares))
    else:
        finish_up(parts, row_basis_ref, local_row_ref, msg_ref, next_ref, squares)


def relay_kernel(recv_ref, msg_ref):
    stats = recv_ref[0]
    for d in range(1, GROUP):
        stats = stats + recv_ref[d]
    send(msg_ref, stats)


def final_kernel(recv_ref, beta1_ref, alpha1_ref, beta2_ref, alpha2_ref, v1_ref, v2_ref, out_ref):
    stats = recv_ref[0]
    for d in range(1, GROUP):
        stats = stats + recv_ref[d]
    beta3 = jnp.sqrt(stat_column(stats))
    phi_bar = beta1_ref[:, :1]
    alpha1 = alpha1_ref[:, :1]
    beta2 = beta2_ref[:, :1]
    alpha2 = alpha2_ref[:, :1]
    rho1 = jnp.sqrt(alpha1 * alpha1 + beta2 * beta2)
    cosine = alpha1 / rho1
    sine = beta2 / rho1
    theta = sine * alpha2
    rho_bar = -cosine * alpha2
    phi1 = cosine * phi_bar
    phi_bar = sine * phi_bar
    rho2 = jnp.sqrt(rho_bar * rho_bar + beta3 * beta3)
    phi2 = rho_bar / rho2 * phi_bar
    v1 = v1_ref[...]
    search = v2_ref[...] - (theta / rho1) * v1
    out_ref[...] = (phi1 / rho1) * v1 + (phi2 / rho2) * search


def call(kernel, outs, operands, scalars=0, scratch=()):
    smem = pl.BlockSpec(memory_space=pltpu.SMEM)
    vmem = pl.BlockSpec(memory_space=pltpu.VMEM)
    return pl.pallas_call(
        kernel,
        out_shape=[jax.ShapeDtypeStruct(shape, f32) for shape in outs],
        in_specs=[smem if isinstance(k, Scalar) else vmem for k in operands],
        out_specs=[vmem] * len(outs),
        scratch_shapes=list(scratch),
        compiler_params=pltpu.CompilerParams(vmem_limit_bytes=VMEM_LIMIT),
    )(*[k.value if isinstance(k, Scalar) else k for k in operands])


class Scalar:
    def __init__(self, value):
        self.value = value


def device_groups(devices, stride):
    out = []
    for base in range(devices):
        if (base // stride) % GROUP == 0:
            out.append([base + k * stride for k in range(GROUP)])
    return out


def local(
    devices,
    rhs,
    box_rows,
    dense,
    row_basis,
    col_basis,
    local_col,
    local_row,
    local_couple,
    up_col,
    up_row,
    up_couple,
):
    me = Scalar(lax.axis_index("leaf").astype(jnp.int32).reshape(1))
    rows = Scalar(box_rows)
    near = device_groups(devices, 1)
    far = device_groups(devices, GROUP)

    def swap(message, groups):
        return lax.all_to_all(message, "leaf", 0, 0, axis_index_groups=groups)

    message_shape = (GROUP, MSG, RANK)
    keep_shape = (6, RHS, RANK)
    row_shape = (RHS, LEAF_DEV * LEAF_ROWS)
    col_shape = (RHS, LEAF_DEV * LEAF_COLS)
    norm_shape = (RHS, RANK)
    nodes = pltpu.VMEM((14, RHS, RANK), f32)

    def climb_group(message, climbers):
        received = swap(message, near)
        message, siblings = call(
            lower_kernel,
            [message_shape, (4, RHS, RANK)],
            [me, received, climbers],
            scratch=[nodes],
        )
        return swap(message, far), siblings

    z, message, keep = call(
        start_kernel, [row_shape, message_shape, keep_shape], [rows, rhs, row_basis, local_row]
    )
    prev = None
    norms = []
    vectors = []
    u = None
    for step in range(2):
        received, siblings = climb_group(message, up_row)
        outs = call(
            functools.partial(adjoint_kernel, prev is None),
            [row_shape, col_shape, norm_shape, message_shape, keep_shape],
            [me, received, siblings, up_row, up_col, up_couple, keep]
            + [dense, col_basis, local_row, local_col, local_couple, z]
            + ([] if prev is None else [prev]),
            scratch=[nodes],
        )
        u, x, norm, message, keep = outs
        norms.append(norm)
        received, siblings = climb_group(message, up_col)
        operands = [me, received, siblings, up_row, up_col, up_couple, keep]
        operands += [dense, row_basis, local_row, local_col, local_couple, rows, x, u]
        if step == 0:
            prev, z, norm, message, keep = call(
                functools.partial(forward_kernel, False),
                [col_shape, row_shape, norm_shape, message_shape, keep_shape],
                operands,
                scratch=[nodes],
            )
            vectors.append(prev)
        else:
            v, norm, message = call(
                functools.partial(forward_kernel, True),
                [col_shape, norm_shape, (GROUP, 8, RANK)],
                operands,
                scratch=[nodes],
            )
            vectors.append(v)
        norms.append(norm)
    received = swap(message, near)
    (message,) = call(relay_kernel, [(GROUP, 8, RANK)], [received])
    received = swap(message, far)
    (out,) = call(final_kernel, [col_shape], [received] + norms + vectors)
    return out


def solution(mesh):
    devices = mesh.shape["leaf"]
    return jax.shard_map(
        functools.partial(local, devices),
        mesh=mesh,
        in_specs=(
            P(None, "leaf"),
            P("leaf"),
            P("leaf", None, None),
            P("leaf", None, None),
            P("leaf", None, None),
            P("leaf", None, None),
            P("leaf", None, None),
            P("leaf", None, None, None),
            P(),
            P(),
            P(),
        ),
        out_specs=P(None, "leaf"),
        check_vma=False,
    )
```

```python
import functools

import jax
import jax.numpy as jnp
from jax import lax
from jax.experimental import pallas as pl
from jax.experimental.pallas import tpu as pltpu
from jax.sharding import PartitionSpec as P

RHS = 16
RANK = 128
LEAF_DEV = 4
LEAF_ROWS = 512
LEAF_COLS = 256
TINY = 1.2e-38
GROUP = 16
VMEM_LIMIT = 40 * 1024 * 1024

f32 = jnp.float32
bf16 = jnp.bfloat16


def split(v):
    head = v.astype(bf16)
    return head, (v - head.astype(f32)).astype(bf16)


def mm_inner(a, b):
    ah, al = split(a)
    bh, bl = split(b)
    dims = (((0,), (0,)), ((), ()))
    m = a.shape[1]
    both = lax.dot_general(jnp.concatenate([ah, al], 1), bh, dims, preferred_element_type=f32)
    rest = lax.dot_general(ah, bl, dims, preferred_element_type=f32)
    return both[:m] + (both[m:] + rest)


def mm(x, w, transposed=False):
    xh, xl = split(x)
    wh, wl = split(w)
    dims = (((1,), (1 if transposed else 0,)), ((), ()))
    n = x.shape[0]
    both = lax.dot_general(jnp.concatenate([xh, xl], 0), wh, dims, preferred_element_type=f32)
    rest = lax.dot_general(xh, wl, dims, preferred_element_type=f32)
    return both[:n] + (both[n:] + rest)


def eye():
    return (
        lax.broadcasted_iota(jnp.int32, (RHS, RANK), 0)
        == lax.broadcasted_iota(jnp.int32, (RHS, RANK), 1)
    ).astype(f32)


def stat_block(first, second):
    rows = lax.broadcasted_iota(jnp.int32, (8, RANK), 0)
    return first * (rows == 0).astype(f32) + second * (rows == 1).astype(f32)


def column_of(row):
    return jnp.sum(row * eye(), axis=1, keepdims=True)


def row_of(column):
    return jnp.sum(column * eye(), axis=0, keepdims=True)


def inverse_norm(squares):
    return jnp.where(squares >= TINY, 1.0 / jnp.sqrt(squares), 1.0)


def sum_squares(v):
    return jnp.sum(v * v, axis=1, keepdims=True)


def send(out_ref, value):
    for peer in range(GROUP):
        out_ref[peer] = value


def stack(blocks):
    return jnp.concatenate(blocks, 0)


def unstack(value, count):
    size = value.shape[0] // count
    return [value[k * size : (k + 1) * size] for k in range(count)]


def climb(blocks, transfer):
    count = len(blocks) // 2
    paired = [jnp.concatenate([blocks[2 * m], blocks[2 * m + 1]], 1) for m in range(count)]
    return unstack(mm(stack(paired), transfer), count)


def descend(blocks, transfer):
    spread = unstack(mm(stack(blocks), transfer, transposed=True), len(blocks))
    out = []
    for block in spread:
        out += [block[:, :RANK], block[:, RANK:]]
    return out


def couple_all(blocks, coupling):
    count = len(blocks) // 2
    even = unstack(mm(stack(blocks[1::2]), coupling[0]), count)
    odd = unstack(mm(stack(blocks[0::2]), coupling[1]), count)
    out = []
    for m in range(count):
        out += [even[m], odd[m]]
    return out


def local_up(parts, basis_ref, climb_ref):
    leaf = [mm(parts[q], basis_ref[q]) for q in range(LEAF_DEV)]
    node = [
        mm(jnp.concatenate([leaf[2 * m], leaf[2 * m + 1]], 1), climb_ref[m]) for m in range(2)
    ]
    return leaf, node


def local_root(node, climb_ref):
    return mm(jnp.concatenate(node, 1), climb_ref[2])


def couple(sibling, coupling_ref, node, child, adjoint):
    if adjoint:
        return mm(sibling, coupling_ref[node, 1 - child], transposed=True)
    return mm(sibling, coupling_ref[node, child])


def local_down(root, leaf, node, coupling_ref, descend_ref, adjoint):
    spread = None if root is None else mm(root, descend_ref[2], transposed=True)
    out = []
    for m in range(2):
        here = None if spread is None else spread[:, m * RANK : (m + 1) * RANK]
        if node is not None:
            gained = couple(node[1 - m], coupling_ref, 2, m, adjoint)
            here = gained if here is None else here + gained
        below = mm(here, descend_ref[m], transposed=True)
        for i in range(2):
            value = below[:, i * RANK : (i + 1) * RANK]
            if leaf is not None:
                value = value + couple(leaf[2 * m + 1 - i], coupling_ref, m, i, adjoint)
            out.append(value)
    return out


def live_mask(rows_ref, q):
    slots = lax.broadcasted_iota(jnp.int32, (RHS, LEAF_ROWS), 1)
    return (slots < rows_ref[q]).astype(f32)


def row_part(q):
    return slice(q * LEAF_ROWS, (q + 1) * LEAF_ROWS)


def col_part(q):
    return slice(q * LEAF_COLS, (q + 1) * LEAF_COLS)


def pair_up(parts, local, rows_ref, msg_ref, own_ref, inner_ref):
    dense_ref, row_basis_ref, col_basis_ref, local_row_ref, local_col_ref, couple_ref = local
    squares = sum_squares(parts[0])
    for part in parts[1:]:
        squares = squares + sum_squares(part)
    scale = inverse_norm(squares)
    parts = [part * scale for part in parts]
    leaf, node = local_up(parts, col_basis_ref, local_col_ref)
    root = local_root(node, local_col_ref)
    down = local_down(None, leaf, node, couple_ref, local_row_ref, False)
    result = []
    energy = jnp.zeros((RHS, 1), f32)
    for q in range(LEAF_DEV):
        y = mm(parts[q], dense_ref[q], transposed=True)
        y = y + mm(down[q], row_basis_ref[q], transposed=True)
        y = y * live_mask(rows_ref, q)
        if inner_ref is not None:
            inner_ref[:, row_part(q)] = y
        energy = energy + sum_squares(y)
        result.append(y)
    _, row_node = local_up(result, row_basis_ref, local_row_ref)
    row_root = local_root(row_node, local_row_ref)
    stats = stat_block(row_of(squares), row_of(energy))
    own_ref[...] = stats
    send(msg_ref, stack([root, row_root, stats]))


def start_kernel(rows_ref, rhs_ref, row_basis_ref, local_row_ref, z_ref, msg_ref, keep_ref):
    parts = []
    squares = jnp.zeros((RHS, 1), f32)
    for q in range(LEAF_DEV):
        part = rhs_ref[:, row_part(q)] * live_mask(rows_ref, q)
        z_ref[:, row_part(q)] = part
        squares = squares + sum_squares(part)
        parts.append(part)
    leaf, node = local_up(parts, row_basis_ref, local_row_ref)
    for k, value in enumerate(leaf + node):
        keep_ref[k] = value
    root = local_root(node, local_row_ref)
    row = row_of(squares)
    send(msg_ref, stack([root, stat_block(row, row)]))


def both_sides(grams, half):
    left = mm(jnp.transpose(half), jnp.concatenate(grams, 1))
    columns = [left[:, k * RANK : (k + 1) * RANK] for k in range(len(grams))]
    return unstack(mm(stack(columns), half), len(grams))


def gram_climb(grams, transfer):
    even = both_sides(grams[0::2], transfer[:RANK])
    odd = both_sides(grams[1::2], transfer[RANK:])
    return [a + b for a, b in zip(even, odd)]


def gram_kernel(rows_ref, row_basis_ref, local_row_ref, out_ref):
    grams = []
    for q in range(LEAF_DEV):
        slots = lax.broadcasted_iota(jnp.int32, (LEAF_ROWS, RANK), 0)
        basis = jnp.where(slots < rows_ref[q], row_basis_ref[q], 0.0)
        grams.append(mm_inner(basis, basis))
    nodes = [gram_climb(grams[2 * m : 2 * m + 2], local_row_ref[m])[0] for m in range(2)]
    out_ref[...] = gram_climb(nodes, local_row_ref[2])[0]


def group_gram_kernel(gram_ref, up_row_ref, nodes_ref, out_ref):
    grams = [gram_ref[d] for d in range(GROUP)]
    base = 0
    for height in range(4):
        grams = gram_climb(grams, up_row_ref[height])
        if height < 3:
            for k, value in enumerate(grams):
                nodes_ref[base + k] = value
            base += len(grams)
    out_ref[...] = grams[0]


def lower_kernel(me_ref, recv_ref, climb_ref, msg_ref, sib_ref, scratch_ref):
    place = me_ref[0] % GROUP
    level = [recv_ref[d, :RHS] for d in range(GROUP)]
    sib_ref[0] = recv_ref[place ^ 1, :RHS]
    base = 0
    for height in range(4):
        level = climb(level, climb_ref[height])
        if height < 3:
            for m, value in enumerate(level):
                scratch_ref[base + m] = value
            sib_ref[height + 1] = scratch_ref[base + ((place >> (height + 1)) ^ 1)]
            base += len(level)
    stats = recv_ref[0, RHS:]
    for d in range(1, GROUP):
        stats = stats + recv_ref[d, RHS:]
    send(msg_ref, stack([level[0], stats]))


def first_kernel(
    me_ref,
    rows_ref,
    recv_ref,
    sib_ref,
    up_row_ref,
    up_col_ref,
    up_couple_ref,
    keep_ref,
    dense_ref,
    row_basis_ref,
    col_basis_ref,
    local_row_ref,
    local_col_ref,
    local_couple_ref,
    z_ref,
    x_ref,
    beta_ref,
    msg_ref,
    own_ref,
    inner_ref,
    scratch_ref,
):
    me = me_ref[0]
    place = me // GROUP
    level = [recv_ref[d, :RHS] for d in range(GROUP)]
    siblings = [sib_ref[j] for j in range(4)]
    siblings.append(recv_ref[place ^ 1, :RHS])
    base = 0
    for height in range(3):
        level = climb(level, up_row_ref[4 + height])
        for m, value in enumerate(level):
            scratch_ref[base + m] = value
        siblings.append(scratch_ref[base + ((place >> (height + 1)) ^ 1)])
        base += len(level)
    potential = None
    for j in reversed(range(8)):
        child = (me >> j) & 1
        gained = mm(siblings[j], up_couple_ref[j, 1 - child], transposed=True)
        if potential is not None:
            gained = gained + mm(potential, half_of(up_col_ref, j, child), transposed=True)
        potential = gained
    stats = recv_ref[0, RHS:]
    for d in range(1, GROUP):
        stats = stats + recv_ref[d, RHS:]
    beta = jnp.sqrt(column_of(stats[:1]))
    inverse = 1.0 / beta
    beta_ref[...] = jnp.broadcast_to(beta, (RHS, RANK))
    leaf = [keep_ref[q] for q in range(LEAF_DEV)]
    node = [keep_ref[LEAF_DEV + m] for m in range(2)]
    down = local_down(potential, leaf, node, local_couple_ref, local_col_ref, True)
    parts = []
    for q in range(LEAF_DEV):
        x = mm(z_ref[:, row_part(q)], dense_ref[q])
        x = (x + mm(down[q], col_basis_ref[q], transposed=True)) * inverse
        x_ref[:, col_part(q)] = x
        parts.append(x)
    local = (dense_ref, row_basis_ref, col_basis_ref, local_row_ref, local_col_ref, local_couple_ref)
    pair_up(parts, local, rows_ref, msg_ref, own_ref, inner_ref)


def half_of(table_ref, j, child):
    return table_ref[j, pl.ds(pl.multiple_of(child * RANK, RANK), RANK), :]


def rescale(recv_ref):
    base = 2 * RHS
    squares = stack([recv_ref[d, base : base + 1] for d in range(GROUP)])
    energy = stack([recv_ref[d, base + 1 : base + 2] for d in range(GROUP)])
    total = jnp.sum(squares, axis=0, keepdims=True)
    factor = inverse_norm(total) / inverse_norm(squares)
    energy = jnp.sum(energy * factor * factor, axis=0, keepdims=True)
    first = []
    second = []
    for d in range(GROUP):
        column = column_of(factor[d : d + 1])
        first.append(recv_ref[d, :RHS] * column)
        second.append(recv_ref[d, RHS : 2 * RHS] * column)
    return first, second, factor, total, energy


def lower_pair_kernel(
    me_ref,
    recv_ref,
    up_row_ref,
    up_col_ref,
    up_couple_ref,
    gram_ref,
    nodes_ref,
    msg_ref,
    path_ref,
    gain_ref,
    below_ref,
):
    place = me_ref[0] % GROUP
    first, second, _, total, energy = rescale(recv_ref)
    cross = jnp.zeros((RHS, RANK), f32)
    base = 0
    for j in range(4):
        gained = couple_all(first, (up_couple_ref[j, 0], up_couple_ref[j, 1]))
        summed = []
        for k in range(len(first)):
            gram = gram_ref[k] if j == 0 else nodes_ref[base - GROUP + k]
            moved = mm(gained[k], gram)
            cross = cross + gained[k] * (2.0 * second[k] + moved)
            summed.append(second[k] + moved)
            gain_ref[base + k] = gained[k]
            below_ref[base + k] = second[k]
        own = place >> j
        path_ref[3 * j] = gain_ref[base + own]
        path_ref[3 * j + 1] = gain_ref[base + (own ^ 1)]
        path_ref[3 * j + 2] = below_ref[base + (own ^ 1)]
        base += len(first)
        first = climb(first, up_col_ref[j])
        second = climb(summed, up_row_ref[j])
    energy = energy + row_of(jnp.sum(cross, axis=1, keepdims=True))
    send(msg_ref, stack([first[0], second[0], stat_block(total, energy)]))


def top_levels(recv_ref, up_row_ref, up_col_ref, up_couple_ref, gram_ref):
    first, second, factor, total, energy = rescale(recv_ref)
    gained = []
    for j in range(4, 8):
        gained.append(couple_all(first, (up_couple_ref[j, 0], up_couple_ref[j, 1])))
        if j < 7:
            first = climb(first, up_col_ref[j])
    potential = gained[3]
    for j in (6, 5, 4):
        below = descend(potential, up_row_ref[j])
        potential = [a + b for a, b in zip(gained[j - 4], below)]
    cross = jnp.zeros((RHS, RANK), f32)
    summed = []
    for d in range(GROUP):
        moved = mm(potential[d], gram_ref[d])
        cross = cross + potential[d] * (2.0 * second[d] + moved)
        summed.append(second[d] + moved)
    energy = column_of(energy) + jnp.sum(cross, axis=1, keepdims=True)
    return potential, summed, factor, column_of(total), energy


def middle_kernel(
    me_ref,
    rows_ref,
    recv_ref,
    path_ref,
    up_row_ref,
    up_col_ref,
    up_couple_ref,
    top_gram_ref,
    gram_ref,
    nodes_ref,
    dense_ref,
    row_basis_ref,
    col_basis_ref,
    local_row_ref,
    local_col_ref,
    local_couple_ref,
    x_ref,
    stats_ref,
    inner_ref,
    v_ref,
    next_ref,
    alpha_ref,
    rho_ref,
    msg_ref,
    own_ref,
    a_ref,
    b_ref,
    c_ref,
):
    me = me_ref[0]
    place = me // GROUP
    inside = me % GROUP
    potential, summed, factor, squares, energy = top_levels(
        recv_ref, up_row_ref, up_col_ref, up_couple_ref, top_gram_ref
    )
    alpha = jnp.sqrt(squares)
    rho = jnp.sqrt(energy)
    alpha_ref[...] = jnp.broadcast_to(alpha, (RHS, RANK))
    rho_ref[...] = jnp.broadcast_to(rho, (RHS, RANK))
    scale = inverse_norm(squares)
    for d in range(GROUP):
        a_ref[d] = potential[d]
    c_ref[...] = factor
    forward = a_ref[place]
    group_factor = column_of(c_ref[pl.ds(place, 1), :])
    siblings = {}
    for j in range(4, 8):
        for k, value in enumerate(summed):
            b_ref[k] = value
        siblings[j] = b_ref[(place >> (j - 4)) ^ 1]
        if j < 7:
            summed = climb(summed, up_row_ref[j])
    for j in reversed(range(4)):
        child = (me >> j) & 1
        spread = mm(forward, up_row_ref[j], transposed=True)
        low = spread[:, :RANK]
        high = spread[:, RANK:]
        own = jnp.where(child == 0, low, high)
        other = jnp.where(child == 0, high, low)
        forward = path_ref[3 * j] * group_factor + own
        other = path_ref[3 * j + 1] * group_factor + other
        sibling = (inside >> j) ^ 1
        gram = gram_ref[sibling] if j == 0 else nodes_ref[(0, 0, 8, 12)[j] + sibling]
        siblings[j] = path_ref[3 * j + 2] * group_factor + mm(other, gram)
    backward = None
    for j in reversed(range(8)):
        child = (me >> j) & 1
        gained = mm(siblings[j], up_couple_ref[j, 1 - child], transposed=True)
        if backward is not None:
            gained = gained + mm(backward, half_of(up_col_ref, j, child), transposed=True)
        backward = gained
    own_factor = scale / inverse_norm(column_of(stats_ref[:1]))
    outer = local_down(forward, None, None, local_couple_ref, local_row_ref, False)
    images = []
    for q in range(LEAF_DEV):
        y = mm(outer[q], row_basis_ref[q], transposed=True) * live_mask(rows_ref, q)
        images.append(y + inner_ref[:, row_part(q)] * own_factor)
    leaf, node = local_up(images, row_basis_ref, local_row_ref)
    down = local_down(backward, leaf, node, local_couple_ref, local_col_ref, True)
    inverse = 1.0 / rho
    parts = []
    for q in range(LEAF_DEV):
        v = x_ref[:, col_part(q)] * scale
        v_ref[:, col_part(q)] = v
        x = mm(images[q], dense_ref[q]) + mm(down[q], col_basis_ref[q], transposed=True)
        x = x * inverse - rho * v
        next_ref[:, col_part(q)] = x
        parts.append(x)
    local = (dense_ref, row_basis_ref, col_basis_ref, local_row_ref, local_col_ref, local_couple_ref)
    pair_up(parts, local, rows_ref, msg_ref, own_ref, None)


def final_kernel(
    recv_ref,
    up_row_ref,
    up_col_ref,
    up_couple_ref,
    top_gram_ref,
    beta_ref,
    alpha_ref,
    rho_ref,
    v_ref,
    x_ref,
    out_ref,
):
    _, _, _, squares, energy = top_levels(
        recv_ref, up_row_ref, up_col_ref, up_couple_ref, top_gram_ref
    )
    theta = jnp.sqrt(squares)
    rho2 = jnp.sqrt(energy - squares)
    rho = rho_ref[:, :1]
    phi = alpha_ref[:, :1] / rho * beta_ref[:, :1]
    v = v_ref[...]
    search = x_ref[...] * inverse_norm(squares) - (theta / rho) * v
    out_ref[...] = (phi / rho) * v - (phi * (theta / rho2) / rho2) * search


def call(kernel, outs, operands, scratch=()):
    smem = pl.BlockSpec(memory_space=pltpu.SMEM)
    vmem = pl.BlockSpec(memory_space=pltpu.VMEM)
    return pl.pallas_call(
        kernel,
        out_shape=[jax.ShapeDtypeStruct(shape, f32) for shape in outs],
        in_specs=[smem if k.dtype == jnp.int32 else vmem for k in operands],
        out_specs=[vmem] * len(outs),
        scratch_shapes=[pltpu.VMEM(shape, f32) for shape in scratch],
        compiler_params=pltpu.CompilerParams(vmem_limit_bytes=VMEM_LIMIT),
    )(*operands)


def device_groups(devices, stride, size):
    out = []
    for base in range(devices):
        if (base // stride) % size == 0:
            out.append([base + k * stride for k in range(size)])
    return out


def local_program(
    devices,
    rhs,
    box_rows,
    dense,
    row_basis,
    col_basis,
    local_col,
    local_row,
    local_couple,
    up_col,
    up_row,
    up_couple,
):
    me = lax.axis_index("leaf").astype(jnp.int32).reshape(1)
    near = device_groups(devices, 1, GROUP)
    far = device_groups(devices, GROUP, GROUP)

    def swap(message, groups):
        return lax.all_to_all(message, "leaf", 0, 0, axis_index_groups=groups)

    def collect(value, stride, size):
        groups = device_groups(devices, stride, size)
        return lax.all_gather(value, "leaf", axis_index_groups=groups)

    tile = (RHS, RANK)
    row_shape = (RHS, LEAF_DEV * LEAF_ROWS)
    col_shape = (RHS, LEAF_DEV * LEAF_COLS)
    first_message = (GROUP, RHS + 8, RANK)
    pair_message = (GROUP, 2 * RHS + 8, RANK)
    gram_shape = (RANK, RANK)
    tables = [up_row, up_col, up_couple]
    blocks = [dense, row_basis, col_basis, local_row, local_col, local_couple]

    (gram,) = call(gram_kernel, [gram_shape], [box_rows, row_basis, local_row])
    grams = collect(gram, 1, GROUP)
    z, message, keep = call(
        start_kernel, [row_shape, first_message, (6,) + tile], [box_rows, rhs, row_basis, local_row]
    )
    received = swap(message, near)
    message, siblings = call(
        lower_kernel, [first_message, (4,) + tile], [me, received, up_row], [(14,) + tile]
    )
    received = swap(message, far)
    grams, received = lax.optimization_barrier((grams, received))
    nodes, group_gram = call(group_gram_kernel, [(14,) + gram_shape, gram_shape], [grams, up_row])
    group_gram, received = lax.optimization_barrier((group_gram, received))
    top_grams = collect(group_gram, GROUP, 4)
    x, beta, message, own, inner = call(
        first_kernel,
        [col_shape, tile, pair_message, (8, RANK), row_shape],
        [me, box_rows, received, siblings] + tables + [keep] + blocks + [z],
        [(14,) + tile],
    )

    def lower_pair(message):
        received = swap(message, near)
        return call(
            lower_pair_kernel,
            [pair_message, (12,) + tile],
            [me, received] + tables + [grams, nodes],
            [(30,) + tile, (30,) + tile],
        )

    message, path = lower_pair(message)
    top_grams, message = lax.optimization_barrier((top_grams, message))
    top_grams = collect(top_grams, 4 * GROUP, 4).reshape((GROUP,) + gram_shape)
    received = swap(message, far)
    v, x, alpha, rho, message, _ = call(
        middle_kernel,
        [col_shape, col_shape, tile, tile, pair_message, (8, RANK)],
        [me, box_rows, received, path] + tables + [top_grams, grams, nodes] + blocks + [x, own, inner],
        [(GROUP,) + tile, (GROUP,) + tile, tile],
    )
    message, _ = lower_pair(message)
    received = swap(message, far)
    (out,) = call(
        final_kernel, [col_shape], [received] + tables + [top_grams, beta, alpha, rho, v, x]
    )
    return out


def solution(mesh):
    devices = mesh.shape["leaf"]
    return jax.shard_map(
        functools.partial(local_program, devices),
        mesh=mesh,
        in_specs=(
            P(None, "leaf"),
            P("leaf"),
            P("leaf", None, None),
            P("leaf", None, None),
            P("leaf", None, None),
            P("leaf", None, None),
            P("leaf", None, None),
            P("leaf", None, None, None),
            P(),
            P(),
            P(),
        ),
        out_specs=P(None, "leaf"),
        check_vma=False,
    )
```

```python
import functools

import jax
import jax.numpy as jnp
from jax import lax
from jax.experimental import pallas as pl
from jax.experimental.pallas import tpu as pltpu
from jax.sharding import PartitionSpec as P

RHS = 16
RANK = 128
LEAF_DEV = 4
LEAF_ROWS = 512
LEAF_COLS = 256
PATH = 3
LEVEL_BASE = (0, 8, 12)
PACKED = 72
TINY = 1.2e-38
NEAR = 8
MID = 8
FAR = 4
VMEM_MIB = 24
VMEM_LIMIT = VMEM_MIB * 1024 * 1024

f32 = jnp.float32
bf16 = jnp.bfloat16


def split(v):
    head = v.astype(bf16)
    return head, (v - head.astype(f32)).astype(bf16)


def mm(x, pair, transposed=False):
    xh, xl = split(x)
    wh, wl = pair
    dims = (((1,), (1 if transposed else 0,)), ((), ()))
    n = x.shape[0]
    both = lax.dot_general(jnp.concatenate([xh, xl], 0), wh, dims, preferred_element_type=f32)
    rest = lax.dot_general(xh, wl, dims, preferred_element_type=f32)
    return both[:n] + (both[n:] + rest)


def mm_inner(a, b):
    ah, al = split(a)
    bh, bl = split(b)
    dims = (((0,), (0,)), ((), ()))
    m = a.shape[1]
    both = lax.dot_general(jnp.concatenate([ah, al], 1), bh, dims, preferred_element_type=f32)
    rest = lax.dot_general(ah, bl, dims, preferred_element_type=f32)
    return both[:m] + (both[m:] + rest)


def pair_at(ref, *index):
    if ref.dtype == bf16:
        return ref[(0,) + index], ref[(1,) + index]
    return split(ref[index])


def pairs_of(ref):
    return functools.partial(pair_at, ref)


def half_of(ref, j, child):
    return pair_at(ref, j, pl.ds(pl.multiple_of(child * RANK, RANK), RANK))


def eye():
    return (
        lax.broadcasted_iota(jnp.int32, (RHS, RANK), 0)
        == lax.broadcasted_iota(jnp.int32, (RHS, RANK), 1)
    ).astype(f32)


def stat_block(first, second):
    rows = lax.broadcasted_iota(jnp.int32, (8, RANK), 0)
    return first * (rows == 0).astype(f32) + second * (rows == 1).astype(f32)


def column_of(row):
    return jnp.sum(row * eye(), axis=1, keepdims=True)


def row_of(column):
    return jnp.sum(column * eye(), axis=0, keepdims=True)


def inverse_norm(squares):
    return jnp.where(squares >= TINY, 1.0 / jnp.sqrt(squares), 1.0)


def sum_squares(v):
    return jnp.sum(v * v, axis=1, keepdims=True)


def send(out_ref, value):
    for peer in range(out_ref.shape[0]):
        out_ref[peer] = value


def stack(blocks):
    return jnp.concatenate(blocks, 0)


def unstack(value, count):
    size = value.shape[0] // count
    return [value[k * size : (k + 1) * size] for k in range(count)]


def climb(blocks, transfer):
    count = len(blocks) // 2
    paired = [jnp.concatenate([blocks[2 * m], blocks[2 * m + 1]], 1) for m in range(count)]
    return unstack(mm(stack(paired), transfer), count)


def descend(blocks, transfer):
    spread = unstack(mm(stack(blocks), transfer, transposed=True), len(blocks))
    out = []
    for block in spread:
        out += [block[:, :RANK], block[:, RANK:]]
    return out


def couple_all(blocks, coupling):
    count = len(blocks) // 2
    even = unstack(mm(stack(blocks[1::2]), coupling[0]), count)
    odd = unstack(mm(stack(blocks[0::2]), coupling[1]), count)
    out = []
    for m in range(count):
        out += [even[m], odd[m]]
    return out


def local_up(parts, basis, transfer):
    leaf = [mm(parts[q], basis(q)) for q in range(LEAF_DEV)]
    node = [
        mm(jnp.concatenate([leaf[2 * m], leaf[2 * m + 1]], 1), transfer(m)) for m in range(2)
    ]
    return leaf, node


def local_root(node, transfer):
    return mm(jnp.concatenate(node, 1), transfer(2))


def couple(sibling, coupling, node, child, adjoint):
    if adjoint:
        return mm(sibling, coupling(node, 1 - child), transposed=True)
    return mm(sibling, coupling(node, child))


def local_down(root, leaf, node, coupling, transfer, adjoint):
    spread = None if root is None else mm(root, transfer(2), transposed=True)
    out = []
    for m in range(2):
        here = None if spread is None else spread[:, m * RANK : (m + 1) * RANK]
        if node is not None:
            gained = couple(node[1 - m], coupling, 2, m, adjoint)
            here = gained if here is None else here + gained
        below = mm(here, transfer(m), transposed=True)
        for i in range(2):
            value = below[:, i * RANK : (i + 1) * RANK]
            if leaf is not None:
                value = value + couple(leaf[2 * m + 1 - i], coupling, m, i, adjoint)
            out.append(value)
    return out


def live_mask(rows_ref, q):
    slots = lax.broadcasted_iota(jnp.int32, (RHS, LEAF_ROWS), 1)
    return (slots < rows_ref[q]).astype(f32)


def row_part(q):
    return slice(q * LEAF_ROWS, (q + 1) * LEAF_ROWS)


def col_part(q):
    return slice(q * LEAF_COLS, (q + 1) * LEAF_COLS)


def pair_up(parts, local, rows_ref, msg_ref, own_ref, inner_ref):
    dense, row_basis, col_basis, local_row, local_col, coupling = local
    squares = sum_squares(parts[0])
    for part in parts[1:]:
        squares = squares + sum_squares(part)
    scale = inverse_norm(squares)
    parts = [part * scale for part in parts]
    leaf, node = local_up(parts, col_basis, local_col)
    root = local_root(node, local_col)
    down = local_down(None, leaf, node, coupling, local_row, False)
    result = []
    energy = jnp.zeros((RHS, 1), f32)
    for q in range(LEAF_DEV):
        y = mm(parts[q], dense(q), transposed=True)
        y = y + mm(down[q], row_basis(q), transposed=True)
        y = y * live_mask(rows_ref, q)
        if inner_ref is not None:
            inner_ref[:, row_part(q)] = y
        energy = energy + sum_squares(y)
        result.append(y)
    _, row_node = local_up(result, row_basis, local_row)
    row_root = local_root(row_node, local_row)
    stats = stat_block(row_of(squares), row_of(energy))
    own_ref[...] = stats
    send(msg_ref, stack([root, row_root, stats]))


def both_sides(grams, half):
    full = half[0].astype(f32) + half[1].astype(f32)
    left = mm(jnp.transpose(full), split(jnp.concatenate(grams, 1)))
    columns = [left[:, k * RANK : (k + 1) * RANK] for k in range(len(grams))]
    return unstack(mm(stack(columns), half), len(grams))


def gram_climb(grams, transfer):
    even = both_sides(grams[0::2], (transfer[0][:RANK], transfer[1][:RANK]))
    odd = both_sides(grams[1::2], (transfer[0][RANK:], transfer[1][RANK:]))
    return [a + b for a, b in zip(even, odd)]


def pack(gram):
    half = RANK // 2
    row = lax.broadcasted_iota(jnp.int32, (half, RANK), 0)
    col = lax.broadcasted_iota(jnp.int32, (half, RANK), 1)
    last = gram[half:]
    top = jnp.where((col < half) & (col > row), pltpu.roll(last, half, 1), gram[:half])
    diagonal = jnp.sum(jnp.where(col - half == row, last, 0.0), axis=0, keepdims=True)
    first = (lax.broadcasted_iota(jnp.int32, (8, RANK), 0) == 0).astype(f32)
    return stack([top, diagonal * first])


def unpack(packed):
    half = RANK // 2
    row = lax.broadcasted_iota(jnp.int32, (half, RANK), 0)
    col = lax.broadcasted_iota(jnp.int32, (half, RANK), 1)
    top = packed[:half]
    diagonal = packed[half : half + 1]
    upper = jnp.where((col >= half) | (col < row), top, jnp.where(col == row, 0.5 * top, 0.0))
    lower = jnp.where(
        col - half > row,
        pltpu.roll(top, half, 1),
        jnp.where(col - half == row, 0.5 * diagonal, 0.0),
    )
    part = stack([upper, lower])
    return part + jnp.transpose(part)


def start_kernel(
    me_ref, rows_ref, rhs_ref, row_basis_ref, local_row_ref, z_ref, msg_ref, keep_ref
):
    row_basis = [split(row_basis_ref[q]) for q in range(LEAF_DEV)]
    local_row = [split(local_row_ref[m]) for m in range(3)]
    parts = []
    squares = jnp.zeros((RHS, 1), f32)
    for q in range(LEAF_DEV):
        part = rhs_ref[:, row_part(q)] * live_mask(rows_ref, q)
        z_ref[:, row_part(q)] = part
        squares = squares + sum_squares(part)
        parts.append(part)
    leaf, node = local_up(parts, row_basis.__getitem__, local_row.__getitem__)
    for k, value in enumerate(leaf + node):
        keep_ref[k] = value
    root = local_root(node, local_row.__getitem__)
    row = row_of(squares)
    grams = []
    for q in range(LEAF_DEV):
        slots = lax.broadcasted_iota(jnp.int32, (LEAF_ROWS, RANK), 0)
        basis = jnp.where(slots < rows_ref[q], row_basis_ref[q], 0.0)
        grams.append(mm_inner(basis, basis))
    nodes = [gram_climb(grams[2 * m : 2 * m + 2], local_row[m])[0] for m in range(2)]
    gram = gram_climb(nodes, local_row[2])[0]
    send(msg_ref, stack([root, stat_block(row, row), pack(gram)]))


def sum_stats(recv_ref):
    stats = recv_ref[0, RHS : RHS + 8]
    for d in range(1, recv_ref.shape[0]):
        stats = stats + recv_ref[d, RHS : RHS + 8]
    return stats


def lower_kernel(level, me_ref, recv_ref, climb_ref, msg_ref, sib_ref, nodes_ref, scratch_ref):
    place = (me_ref[0] >> level) % NEAR
    peers = range(recv_ref.shape[0])
    summaries = [recv_ref[d, :RHS] for d in peers]
    grams = [unpack(recv_ref[d, RHS + 8 :]) for d in peers]
    for height in range(PATH):
        base = LEVEL_BASE[height]
        for m, value in enumerate(summaries):
            scratch_ref[base + m] = value
        sib_ref[height] = scratch_ref[base + ((place >> height) ^ 1)]
        for k, value in enumerate(grams):
            high, low = split(value)
            nodes_ref[0, base + k] = high
            nodes_ref[1, base + k] = low
        transfer = pair_at(climb_ref, level + height)
        summaries = climb(summaries, transfer)
        grams = gram_climb(grams, transfer)
    send(msg_ref, stack([summaries[0], sum_stats(recv_ref), pack(grams[0])]))


def readers(local):
    return [pairs_of(ref) for ref in local]


def first_kernel(
    me_ref,
    rows_ref,
    recv_ref,
    near_ref,
    mid_ref,
    up_row_ref,
    up_col_ref,
    up_couple_ref,
    keep_ref,
    dense_ref,
    row_basis_ref,
    col_basis_ref,
    local_row_ref,
    local_col_ref,
    local_couple_ref,
    z_ref,
    x_ref,
    beta_ref,
    msg_ref,
    own_ref,
    inner_ref,
    nodes_ref,
    scratch_ref,
):
    me = me_ref[0]
    place = me >> (2 * PATH)
    summaries = [recv_ref[d, :RHS] for d in range(FAR)]
    siblings = [near_ref[j] for j in range(PATH)] + [mid_ref[j] for j in range(PATH)]
    siblings.append(recv_ref[place ^ 1, :RHS])
    summaries = climb(summaries, pair_at(up_row_ref, 6))
    for m, value in enumerate(summaries):
        scratch_ref[m] = value
    siblings.append(scratch_ref[(place >> 1) ^ 1])
    potential = None
    for j in reversed(range(8)):
        child = (me >> j) & 1
        gained = mm(siblings[j], pair_at(up_couple_ref, j, 1 - child), transposed=True)
        if potential is not None:
            gained = gained + mm(potential, half_of(up_col_ref, j, child), transposed=True)
        potential = gained
    beta = jnp.sqrt(column_of(sum_stats(recv_ref)[:1]))
    for d in range(FAR):
        high, low = split(unpack(recv_ref[d, RHS + 8 :]))
        nodes_ref[0, d] = high
        nodes_ref[1, d] = low
    inverse = 1.0 / beta
    beta_ref[...] = jnp.broadcast_to(beta, (RHS, RANK))
    local = readers(
        (dense_ref, row_basis_ref, col_basis_ref, local_row_ref, local_col_ref, local_couple_ref)
    )
    dense, _, col_basis, _, local_col, coupling = local
    leaf = [keep_ref[q] for q in range(LEAF_DEV)]
    node = [keep_ref[LEAF_DEV + m] for m in range(2)]
    down = local_down(potential, leaf, node, coupling, local_col, True)
    parts = []
    for q in range(LEAF_DEV):
        x = mm(z_ref[:, row_part(q)], dense(q))
        x = (x + mm(down[q], col_basis(q), transposed=True)) * inverse
        x_ref[:, col_part(q)] = x
        parts.append(x)
    pair_up(parts, local, rows_ref, msg_ref, own_ref, inner_ref)


def rescale(recv_ref):
    base = 2 * RHS
    squares = stack([recv_ref[d, base : base + 1] for d in range(recv_ref.shape[0])])
    energy = stack([recv_ref[d, base + 1 : base + 2] for d in range(recv_ref.shape[0])])
    total = jnp.sum(squares, axis=0, keepdims=True)
    factor = inverse_norm(total) / inverse_norm(squares)
    energy = jnp.sum(energy * factor * factor, axis=0, keepdims=True)
    first = []
    second = []
    for d in range(recv_ref.shape[0]):
        column = column_of(factor[d : d + 1])
        first.append(recv_ref[d, :RHS] * column)
        second.append(recv_ref[d, RHS : 2 * RHS] * column)
    return first, second, factor, total, energy


def lower_pair_kernel(
    level,
    me_ref,
    recv_ref,
    up_row_ref,
    up_col_ref,
    up_couple_ref,
    nodes_ref,
    msg_ref,
    path_ref,
    own_ref,
    gain_ref,
    below_ref,
):
    place = (me_ref[0] >> level) % NEAR
    first, second, _, total, energy = rescale(recv_ref)
    cross = jnp.zeros((RHS, RANK), f32)
    for height in range(PATH):
        j = level + height
        base = LEVEL_BASE[height]
        gained = couple_all(first, (pair_at(up_couple_ref, j, 0), pair_at(up_couple_ref, j, 1)))
        summed = []
        for k in range(len(first)):
            moved = mm(gained[k], pair_at(nodes_ref, base + k))
            cross = cross + gained[k] * (2.0 * second[k] + moved)
            summed.append(second[k] + moved)
            gain_ref[base + k] = gained[k]
            below_ref[base + k] = second[k]
        own = base + (place >> height)
        other = base + ((place >> height) ^ 1)
        path_ref[3 * height] = gain_ref[own]
        path_ref[3 * height + 1] = gain_ref[other]
        path_ref[3 * height + 2] = below_ref[other]
        first = climb(first, pair_at(up_col_ref, j))
        second = climb(summed, pair_at(up_row_ref, j))
    energy = energy + row_of(jnp.sum(cross, axis=1, keepdims=True))
    stats = stat_block(total, energy)
    own_ref[...] = stats
    send(msg_ref, stack([first[0], second[0], stats]))


def top_levels(recv_ref, up_row_ref, up_col_ref, up_couple_ref, gram_ref):
    first, second, _, total, energy = rescale(recv_ref)
    gained = couple_all(first, (pair_at(up_couple_ref, 6, 0), pair_at(up_couple_ref, 6, 1)))
    first = climb(first, pair_at(up_col_ref, 6))
    potential = couple_all(first, (pair_at(up_couple_ref, 7, 0), pair_at(up_couple_ref, 7, 1)))
    below = descend(potential, pair_at(up_row_ref, 6))
    potential = [a + b for a, b in zip(gained, below)]
    cross = jnp.zeros((RHS, RANK), f32)
    summed = []
    for d in range(FAR):
        moved = mm(potential[d], pair_at(gram_ref, d))
        cross = cross + potential[d] * (2.0 * second[d] + moved)
        summed.append(second[d] + moved)
    energy = column_of(energy) + jnp.sum(cross, axis=1, keepdims=True)
    return potential, summed, column_of(total), energy


def middle_kernel(
    me_ref,
    rows_ref,
    recv_ref,
    near_path_ref,
    near_own_ref,
    mid_path_ref,
    mid_own_ref,
    up_row_ref,
    up_col_ref,
    up_couple_ref,
    top_gram_ref,
    near_nodes_ref,
    mid_nodes_ref,
    dense_ref,
    row_basis_ref,
    col_basis_ref,
    local_row_ref,
    local_col_ref,
    local_couple_ref,
    x_ref,
    own_in_ref,
    inner_ref,
    v_ref,
    next_ref,
    alpha_ref,
    rho_ref,
    msg_ref,
    own_ref,
    a_ref,
    b_ref,
):
    me = me_ref[0]
    place = me >> (2 * PATH)
    potential, summed, squares, energy = top_levels(
        recv_ref, up_row_ref, up_col_ref, up_couple_ref, top_gram_ref
    )
    alpha = jnp.sqrt(squares)
    rho = jnp.sqrt(energy)
    alpha_ref[...] = jnp.broadcast_to(alpha, (RHS, RANK))
    rho_ref[...] = jnp.broadcast_to(rho, (RHS, RANK))
    scale = inverse_norm(squares)
    for d in range(FAR):
        a_ref[d] = potential[d]
        b_ref[d] = summed[d]
    forward = a_ref[place]
    siblings = {6: b_ref[place ^ 1]}
    for k, value in enumerate(climb(summed, pair_at(up_row_ref, 6))):
        a_ref[FAR + k] = value
    siblings[7] = a_ref[FAR + ((place >> 1) ^ 1)]
    for level, path_ref, part_ref, nodes_ref in (
        (PATH, mid_path_ref, mid_own_ref, mid_nodes_ref),
        (0, near_path_ref, near_own_ref, near_nodes_ref),
    ):
        factor = scale / inverse_norm(column_of(part_ref[:1]))
        inside = (me >> level) % NEAR
        for height in reversed(range(PATH)):
            j = level + height
            child = (me >> j) & 1
            spread = mm(forward, pair_at(up_row_ref, j), transposed=True)
            low = spread[:, :RANK]
            high = spread[:, RANK:]
            forward = path_ref[3 * height] * factor + jnp.where(child == 0, low, high)
            other = path_ref[3 * height + 1] * factor + jnp.where(child == 0, high, low)
            gram = pair_at(nodes_ref, LEVEL_BASE[height] + ((inside >> height) ^ 1))
            siblings[j] = path_ref[3 * height + 2] * factor + mm(other, gram)
    backward = None
    for j in reversed(range(8)):
        child = (me >> j) & 1
        gained = mm(siblings[j], pair_at(up_couple_ref, j, 1 - child), transposed=True)
        if backward is not None:
            gained = gained + mm(backward, half_of(up_col_ref, j, child), transposed=True)
        backward = gained
    local = readers(
        (dense_ref, row_basis_ref, col_basis_ref, local_row_ref, local_col_ref, local_couple_ref)
    )
    dense, row_basis, col_basis, local_row, local_col, coupling = local
    own_factor = scale / inverse_norm(column_of(own_in_ref[:1]))
    outer = local_down(forward, None, None, coupling, local_row, False)
    images = []
    for q in range(LEAF_DEV):
        y = mm(outer[q], row_basis(q), transposed=True) * live_mask(rows_ref, q)
        images.append(y + inner_ref[:, row_part(q)] * own_factor)
    leaf, node = local_up(images, row_basis, local_row)
    down = local_down(backward, leaf, node, coupling, local_col, True)
    inverse = 1.0 / rho
    parts = []
    for q in range(LEAF_DEV):
        v = x_ref[:, col_part(q)] * scale
        v_ref[:, col_part(q)] = v
        x = mm(images[q], dense(q)) + mm(down[q], col_basis(q), transposed=True)
        x = x * inverse - rho * v
        next_ref[:, col_part(q)] = x
        parts.append(x)
    pair_up(parts, local, rows_ref, msg_ref, own_ref, None)


def final_kernel(
    recv_ref,
    up_row_ref,
    up_col_ref,
    up_couple_ref,
    top_gram_ref,
    beta_ref,
    alpha_ref,
    rho_ref,
    v_ref,
    x_ref,
    out_ref,
):
    _, _, squares, energy = top_levels(
        recv_ref, up_row_ref, up_col_ref, up_couple_ref, top_gram_ref
    )
    theta = jnp.sqrt(squares)
    rho2 = jnp.sqrt(energy - squares)
    rho = rho_ref[:, :1]
    phi = alpha_ref[:, :1] / rho * beta_ref[:, :1]
    v = v_ref[...]
    search = x_ref[...] * inverse_norm(squares) - (theta / rho) * v
    out_ref[...] = (phi / rho) * v - (phi * (theta / rho2) / rho2) * search


def call(kernel, outs, operands, scratch=()):
    spaces = [pltpu.SMEM if k.dtype == jnp.int32 else pltpu.VMEM for k in operands]
    outs = [shape if isinstance(shape, jax.ShapeDtypeStruct) else jax.ShapeDtypeStruct(shape, f32) for shape in outs]
    return pl.pallas_call(
        kernel,
        out_shape=outs,
        in_specs=[pl.BlockSpec(memory_space=space) for space in spaces],
        out_specs=[pl.BlockSpec(memory_space=pltpu.VMEM)] * len(outs),
        scratch_shapes=[pltpu.VMEM(shape, f32) for shape in scratch],
        compiler_params=pltpu.CompilerParams(vmem_limit_bytes=VMEM_LIMIT),
    )(*operands)


def device_groups(devices, stride, size):
    out = []
    for base in range(devices):
        if (base // stride) % size == 0:
            out.append([base + k * stride for k in range(size)])
    return out


def local_program(
    devices,
    rhs,
    box_rows,
    dense,
    row_basis,
    col_basis,
    local_col,
    local_row,
    local_couple,
    up_col,
    up_row,
    up_couple,
):
    me = lax.axis_index("leaf").astype(jnp.int32).reshape(1)
    near, mid, far = (1, NEAR), (NEAR, MID), (NEAR * MID, FAR)

    def swap(message, group):
        return lax.all_to_all(message, "leaf", 0, 0, axis_index_groups=device_groups(devices, *group))

    tile = (RHS, RANK)
    row_shape = (RHS, LEAF_DEV * LEAF_ROWS)
    col_shape = (RHS, LEAF_DEV * LEAF_COLS)
    single = (RHS + 8 + PACKED, RANK)
    double = (2 * RHS + 8, RANK)
    stat = (8, RANK)
    gram_shape = (RANK, RANK)
    tables = [up_row, up_col, up_couple]
    blocks = [dense, row_basis, col_basis, local_row, local_col, local_couple]

    def nodes_shape(count):
        return jax.ShapeDtypeStruct((2, count) + gram_shape, bf16)

    def lower(level, message, peers):
        return call(
            functools.partial(lower_kernel, level),
            [(peers,) + single, (PATH,) + tile, nodes_shape(14)],
            [me, message, up_row],
            [(14,) + tile],
        )

    def lower_pair(level, message, peers, nodes):
        return call(
            functools.partial(lower_pair_kernel, level),
            [(peers,) + double, (3 * PATH,) + tile, stat],
            [me, message] + tables + [nodes],
            [(14,) + tile, (14,) + tile],
        )

    z, message, keep = call(
        start_kernel,
        [row_shape, (NEAR,) + single, (6,) + tile],
        [me, box_rows, rhs, row_basis, local_row],
    )
    message, near_sib, near_nodes = lower(0, swap(message, near), MID)
    message, mid_sib, mid_nodes = lower(PATH, swap(message, mid), FAR)
    received = swap(message, far)
    x, beta, message, own, inner, top_nodes = call(
        first_kernel,
        [col_shape, tile, (NEAR,) + double, stat, row_shape, nodes_shape(FAR)],
        [me, box_rows, received, near_sib, mid_sib] + tables + [keep] + blocks + [z],
        [(2,) + tile],
    )
    message, near_path, near_own = lower_pair(0, swap(message, near), MID, near_nodes)
    message, mid_path, mid_own = lower_pair(PATH, swap(message, mid), FAR, mid_nodes)
    received = swap(message, far)
    v, x, alpha, rho, message, _ = call(
        middle_kernel,
        [col_shape, col_shape, tile, tile, (NEAR,) + double, stat],
        [me, box_rows, received, near_path, near_own, mid_path, mid_own]
        + tables
        + [top_nodes, near_nodes, mid_nodes]
        + blocks
        + [x, own, inner],
        [(6,) + tile, (4,) + tile],
    )
    message, _, _ = lower_pair(0, swap(message, near), MID, near_nodes)
    message, _, _ = lower_pair(PATH, swap(message, mid), FAR, mid_nodes)
    received = swap(message, far)
    (out,) = call(
        final_kernel, [col_shape], [received] + tables + [top_nodes, beta, alpha, rho, v, x]
    )
    return out


def solution(mesh):
    devices = mesh.shape["leaf"]
    return jax.shard_map(
        functools.partial(local_program, devices),
        mesh=mesh,
        in_specs=(
            P(None, "leaf"),
            P("leaf"),
            P("leaf", None, None),
            P("leaf", None, None),
            P("leaf", None, None),
            P("leaf", None, None),
            P("leaf", None, None),
            P("leaf", None, None, None),
            P(),
            P(),
            P(),
        ),
        out_specs=P(None, "leaf"),
        check_vma=False,
    )
```

```python
import functools

import jax
import jax.numpy as jnp
from jax import lax
from jax.experimental import pallas as pl
from jax.experimental.pallas import tpu as pltpu
from jax.sharding import PartitionSpec as P

RHS = 16
RANK = 128
LEAF_DEV = 4
LEAF_ROWS = 512
LEAF_COLS = 256
PATH = 3
LEVEL_BASE = (0, 8, 12)
HALF = RANK // 2
SLICE = 8
COST_FLOPS = 6000000000
KEEP = LEAF_DEV * LEAF_ROWS
TINY = 1.2e-38
NEAR = 8
MID = 8
FAR = 4
VMEM_MIB = 24
VMEM_LIMIT = VMEM_MIB * 1024 * 1024
START_LIMIT = 60 * 1024 * 1024

f32 = jnp.float32
bf16 = jnp.bfloat16


def split(v):
    head = v.astype(bf16)
    return head, (v - head.astype(f32)).astype(bf16)


def mm(x, pair, transposed=False):
    xh, xl = split(x)
    wh, wl = pair
    dims = (((1,), (1 if transposed else 0,)), ((), ()))
    n = x.shape[0]
    both = lax.dot_general(jnp.concatenate([xh, xl], 0), wh, dims, preferred_element_type=f32)
    rest = lax.dot_general(xh, wl, dims, preferred_element_type=f32)
    return both[:n] + (both[n:] + rest)


def mm_inner(a, b):
    ah, al = split(a)
    bh, bl = split(b)
    dims = (((0,), (0,)), ((), ()))
    m = a.shape[1]
    both = lax.dot_general(jnp.concatenate([ah, al], 1), bh, dims, preferred_element_type=f32)
    rest = lax.dot_general(ah, bl, dims, preferred_element_type=f32)
    return both[:m] + (both[m:] + rest)


def pair_at(ref, *index):
    if ref.dtype == bf16:
        return ref[(0,) + index], ref[(1,) + index]
    return split(ref[index])


def pairs_of(ref):
    return functools.partial(pair_at, ref)


def half_of(ref, j, child):
    return pair_at(ref, j, pl.ds(pl.multiple_of(child * RANK, RANK), RANK))


def eye():
    return (
        lax.broadcasted_iota(jnp.int32, (RHS, RANK), 0)
        == lax.broadcasted_iota(jnp.int32, (RHS, RANK), 1)
    ).astype(f32)


def stat_block(*values):
    rows = lax.broadcasted_iota(jnp.int32, (8, RANK), 0)
    block = jnp.where(rows == 0, values[0], 0.0)
    for k in range(1, len(values)):
        block = jnp.where(rows == k, values[k], block)
    return block


def column_of(row):
    return jnp.sum(row * eye(), axis=1, keepdims=True)


def row_of(column):
    return jnp.sum(column * eye(), axis=0, keepdims=True)


def inverse_norm(squares):
    return jnp.where(squares >= TINY, 1.0 / jnp.sqrt(squares), 1.0)


def sum_squares(v):
    return jnp.sum(v * v, axis=1, keepdims=True)


def send(out_ref, value):
    for peer in range(out_ref.shape[0]):
        out_ref[peer] = value


def stack(blocks):
    return jnp.concatenate(blocks, 0)


def unstack(value, count):
    size = value.shape[0] // count
    return [value[k * size : (k + 1) * size] for k in range(count)]


def climb(blocks, transfer):
    count = len(blocks) // 2
    paired = [jnp.concatenate([blocks[2 * m], blocks[2 * m + 1]], 1) for m in range(count)]
    return unstack(mm(stack(paired), transfer), count)


def descend(blocks, transfer):
    spread = unstack(mm(stack(blocks), transfer, transposed=True), len(blocks))
    out = []
    for block in spread:
        out += [block[:, :RANK], block[:, RANK:]]
    return out


def couple_all(blocks, coupling):
    count = len(blocks) // 2
    even = unstack(mm(stack(blocks[1::2]), coupling[0]), count)
    odd = unstack(mm(stack(blocks[0::2]), coupling[1]), count)
    out = []
    for m in range(count):
        out += [even[m], odd[m]]
    return out


def local_up(parts, basis, transfer):
    leaf = [mm(parts[q], basis(q)) for q in range(LEAF_DEV)]
    node = [
        mm(jnp.concatenate([leaf[2 * m], leaf[2 * m + 1]], 1), transfer(m)) for m in range(2)
    ]
    return leaf, node


def local_root(node, transfer):
    return mm(jnp.concatenate(node, 1), transfer(2))


def couple(sibling, coupling, node, child, adjoint):
    if adjoint:
        return mm(sibling, coupling(node, 1 - child), transposed=True)
    return mm(sibling, coupling(node, child))


def local_down(root, leaf, node, coupling, transfer, adjoint):
    spread = None if root is None else mm(root, transfer(2), transposed=True)
    out = []
    for m in range(2):
        here = None if spread is None else spread[:, m * RANK : (m + 1) * RANK]
        if node is not None:
            gained = couple(node[1 - m], coupling, 2, m, adjoint)
            here = gained if here is None else here + gained
        below = mm(here, transfer(m), transposed=True)
        for i in range(2):
            value = below[:, i * RANK : (i + 1) * RANK]
            if leaf is not None:
                value = value + couple(leaf[2 * m + 1 - i], coupling, m, i, adjoint)
            out.append(value)
    return out


def live_mask(rows_ref, q):
    slots = lax.broadcasted_iota(jnp.int32, (RHS, LEAF_ROWS), 1)
    return (slots < rows_ref[q]).astype(f32)


def row_part(q):
    return slice(q * LEAF_ROWS, (q + 1) * LEAF_ROWS)


def col_part(q):
    return slice(q * LEAF_COLS, (q + 1) * LEAF_COLS)


def pair_up(parts, local, rows_ref, msg_ref, own_ref, inner_ref, extra):
    dense, row_basis, col_basis, local_row, local_col, coupling = local
    squares = sum_squares(parts[0])
    for part in parts[1:]:
        squares = squares + sum_squares(part)
    scale = inverse_norm(squares)
    parts = [part * scale for part in parts]
    leaf, node = local_up(parts, col_basis, local_col)
    root = local_root(node, local_col)
    down = local_down(None, leaf, node, coupling, local_row, False)
    result = []
    energy = jnp.zeros((RHS, 1), f32)
    for q in range(LEAF_DEV):
        y = mm(parts[q], dense(q), transposed=True)
        y = y + mm(down[q], row_basis(q), transposed=True)
        y = y * live_mask(rows_ref, q)
        if inner_ref is not None:
            inner_ref[:, row_part(q)] = y
        energy = energy + sum_squares(y)
        result.append(y)
    _, row_node = local_up(result, row_basis, local_row)
    row_root = local_root(row_node, local_row)
    stats = stat_block(row_of(squares), row_of(energy))
    if own_ref is not None:
        own_ref[...] = stats
    send(msg_ref, stack([root, row_root, stats] + extra))


def both_sides(grams, half):
    full = half[0].astype(f32) + half[1].astype(f32)
    left = mm(jnp.transpose(full), split(jnp.concatenate(grams, 1)))
    columns = [left[:, k * RANK : (k + 1) * RANK] for k in range(len(grams))]
    return unstack(mm(stack(columns), half), len(grams))


def gram_climb(grams, transfer):
    even = both_sides(grams[0::2], (transfer[0][:RANK], transfer[1][:RANK]))
    odd = both_sides(grams[1::2], (transfer[0][RANK:], transfer[1][RANK:]))
    return [a + b for a, b in zip(even, odd)]


def pack(gram):
    row = lax.broadcasted_iota(jnp.int32, (HALF, RANK), 0)
    col = lax.broadcasted_iota(jnp.int32, (HALF, RANK), 1)
    last = gram[HALF:]
    top = jnp.where((col < HALF) & (col > row), pltpu.roll(last, HALF, 1), gram[:HALF])
    diagonal = jnp.sum(jnp.where(col - HALF == row, last, 0.0), axis=0, keepdims=True)
    return top, diagonal


def unpack(top, diagonal):
    row = lax.broadcasted_iota(jnp.int32, (HALF, RANK), 0)
    col = lax.broadcasted_iota(jnp.int32, (HALF, RANK), 1)
    upper = jnp.where((col >= HALF) | (col < row), top, jnp.where(col == row, 0.5 * top, 0.0))
    lower = jnp.where(
        col - HALF > row,
        pltpu.roll(top, HALF, 1),
        jnp.where(col - HALF == row, 0.5 * diagonal, 0.0),
    )
    part = stack([upper, lower])
    return part + jnp.transpose(part)


def store_pair(ref, index, value):
    high, low = split(value)
    ref[0, index] = high
    ref[1, index] = low


def group_grams(level, grams, up_row_ref, nodes_ref):
    for height in range(PATH):
        for k, value in enumerate(grams):
            store_pair(nodes_ref, LEVEL_BASE[height] + k, value)
        grams = gram_climb(grams, pair_at(up_row_ref, level + height))
    return grams[0]


def start_copies(pairs, sems):
    copies = [
        pltpu.make_async_copy(source, target, sems.at[k])
        for k, (source, target) in enumerate(pairs)
    ]
    for copy in copies:
        copy.start()
    return copies


def start_kernel(
    me_ref,
    rows_hbm,
    rhs_hbm,
    row_basis_hbm,
    local_row_hbm,
    z_ref,
    msg_ref,
    rows_ref,
    rhs_ref,
    row_basis_ref,
    local_row_ref,
    sems,
):
    pairs = [(rows_hbm, rows_ref), (rhs_hbm, rhs_ref)]
    pairs += [(row_basis_hbm, row_basis_ref), (local_row_hbm, local_row_ref)]
    for copy in start_copies(pairs, sems):
        copy.wait()
    squares = jnp.zeros((RHS, 1), f32)
    local_row = [split(local_row_ref[m]) for m in range(3)]
    leaf = []
    grams = []
    for q in range(LEAF_DEV):
        part = rhs_ref[:, row_part(q)] * live_mask(rows_ref, q)
        z_ref[:, row_part(q)] = part
        squares = squares + sum_squares(part)
        leaf.append(mm(part, split(row_basis_ref[q])))
    for q in range(LEAF_DEV):
        slots = lax.broadcasted_iota(jnp.int32, (LEAF_ROWS, RANK), 0)
        basis = jnp.where(slots < rows_ref[q], row_basis_ref[q], 0.0)
        grams.append(mm_inner(basis, basis))
    node = [climb(leaf[2 * m : 2 * m + 2], local_row[m])[0] for m in range(2)]
    for k, value in enumerate(leaf + node):
        z_ref[:, KEEP + k * RANK : KEEP + (k + 1) * RANK] = value
    root = climb(node, local_row[2])[0]
    row = row_of(squares)
    nodes = [gram_climb(grams[2 * m : 2 * m + 2], local_row[m])[0] for m in range(2)]
    gram = gram_climb(nodes, local_row[2])[0]
    top, diagonal = pack(gram)
    send(msg_ref, stack([root, stat_block(row, row, diagonal), top]))


def sum_stats(recv_ref):
    stats = recv_ref[0, RHS : RHS + 8]
    for d in range(1, recv_ref.shape[0]):
        stats = stats + recv_ref[d, RHS : RHS + 8]
    return stats


def climb_group(level, me_ref, recv_ref, climb_ref, sib_ref, scratch_ref):
    place = (me_ref[0] >> level) % NEAR
    summaries = [recv_ref[d, :RHS] for d in range(recv_ref.shape[0])]
    for height in range(PATH):
        base = LEVEL_BASE[height]
        for m, value in enumerate(summaries):
            scratch_ref[base + m] = value
        sib_ref[height] = scratch_ref[base + ((place >> height) ^ 1)]
        summaries = climb(summaries, pair_at(climb_ref, level + height))
    return summaries[0]


def path_product(me, level, path, up_col_ref):
    half = half_of(up_col_ref, level, (me >> level) & 1)
    return mm(path, half)


def sibling_gain(me, level, path, up_couple_ref):
    child = 1 - ((me >> level) & 1)
    return mm(path, pair_at(up_couple_ref, level, child))


def near_kernel(
    me_ref,
    recv_ref,
    up_row_ref,
    up_col_ref,
    up_couple_ref,
    msg_ref,
    sib_ref,
    nodes_ref,
    gain_ref,
    path_ref,
    scratch_ref,
    slice_ref,
):
    me = me_ref[0]
    summary = climb_group(0, me_ref, recv_ref, up_row_ref, sib_ref, scratch_ref)
    base = RHS + 8
    grams = [unpack(recv_ref[d, base:], recv_ref[d, RHS + 2 : RHS + 3]) for d in range(NEAR)]
    gram = group_grams(0, grams, up_row_ref, nodes_ref)
    child = 1 - (me & 1)
    first = up_couple_ref[0, child]
    store_pair(gain_ref, 0, first)
    path = up_col_ref[0, pl.ds(pl.multiple_of((me & 1) * RANK, RANK), RANK), :]
    for j in range(1, PATH):
        store_pair(gain_ref, j, sibling_gain(me, j, path, up_couple_ref))
        path = path_product(me, j, path, up_col_ref)
    path_ref[...] = path
    top, diagonal = pack(gram)
    slice_ref[...] = top
    part = slice_ref[pl.ds(pl.multiple_of((me % NEAR) * SLICE, SLICE), SLICE), :]
    stats = sum_stats(recv_ref)
    send(msg_ref, stack([summary, stat_block(stats[:1], stats[1:2], diagonal), part]))


def mid_kernel(
    me_ref,
    recv_ref,
    up_row_ref,
    up_col_ref,
    up_couple_ref,
    path_ref,
    msg_ref,
    sib_ref,
    gain_ref,
    part_ref,
    diagonal_ref,
    scratch_ref,
):
    me = me_ref[0]
    summary = climb_group(PATH, me_ref, recv_ref, up_row_ref, sib_ref, scratch_ref)
    path = path_ref[...]
    for j in range(PATH, 8):
        store_pair(gain_ref, j - PATH, sibling_gain(me, j, path, up_couple_ref))
        if j < 7:
            path = path_product(me, j, path, up_col_ref)
    for d in range(MID):
        part_ref[d * SLICE : (d + 1) * SLICE] = recv_ref[d, RHS + 8 :]
        diagonal_ref[d : d + 1] = recv_ref[d, RHS + 2 : RHS + 3]
    send(msg_ref, stack([summary, sum_stats(recv_ref)]))


def from_siblings(siblings, near_gain_ref, mid_gain_ref):
    gains = [pair_at(near_gain_ref, j) for j in range(PATH)]
    gains += [pair_at(mid_gain_ref, j) for j in range(8 - PATH)]
    gains = tuple(jnp.concatenate([g[k] for g in gains], 1) for k in range(2))
    return mm(jnp.concatenate(siblings, 1), gains, transposed=True)


def gather_far(me, parts, out_ref):
    place = me >> (2 * PATH)
    for k, part in enumerate(parts):
        out_ref[place ^ k] = part[0]


def readers(local):
    return [pairs_of(ref) for ref in local]


def first_kernel(
    me_ref,
    rows_ref,
    part0_ref,
    part1_ref,
    part2_ref,
    part3_ref,
    near_ref,
    mid_ref,
    near_gain_ref,
    mid_gain_ref,
    part_ref,
    up_row_ref,
    dense_ref,
    row_basis_ref,
    col_basis_ref,
    local_row_ref,
    local_col_ref,
    local_couple_ref,
    z_ref,
    x_ref,
    beta_ref,
    msg_ref,
    own_ref,
    inner_ref,
    scratch_ref,
    recv_ref,
):
    me = me_ref[0]
    gather_far(me, (part0_ref, part1_ref, part2_ref, part3_ref), recv_ref)
    place = me >> (2 * PATH)
    summaries = [recv_ref[d, :RHS] for d in range(FAR)]
    siblings = [near_ref[j] for j in range(PATH)] + [mid_ref[j] for j in range(PATH)]
    siblings.append(recv_ref[place ^ 1, :RHS])
    summaries = climb(summaries, pair_at(up_row_ref, 6))
    for m, value in enumerate(summaries):
        scratch_ref[m] = value
    siblings.append(scratch_ref[(place >> 1) ^ 1])
    potential = from_siblings(siblings, near_gain_ref, mid_gain_ref)
    beta = jnp.sqrt(column_of(sum_stats(recv_ref)[:1]))
    inverse = 1.0 / beta
    beta_ref[...] = jnp.broadcast_to(beta, (RHS, RANK))
    local = readers(
        (dense_ref, row_basis_ref, col_basis_ref, local_row_ref, local_col_ref, local_couple_ref)
    )
    dense, _, col_basis, _, local_col, coupling = local
    keep = [z_ref[:, KEEP + k * RANK : KEEP + (k + 1) * RANK] for k in range(LEAF_DEV + 2)]
    leaf, node = keep[:LEAF_DEV], keep[LEAF_DEV:]
    down = local_down(potential, leaf, node, coupling, local_col, True)
    parts = []
    for q in range(LEAF_DEV):
        x = mm(z_ref[:, row_part(q)], dense(q))
        x = (x + mm(down[q], col_basis(q), transposed=True)) * inverse
        x_ref[:, col_part(q)] = x
        parts.append(x)
    pair_up(parts, local, rows_ref, msg_ref, own_ref, inner_ref, [part_ref[...]])


def rescale(recv_ref):
    base = 2 * RHS
    squares = stack([recv_ref[d, base : base + 1] for d in range(recv_ref.shape[0])])
    energy = stack([recv_ref[d, base + 1 : base + 2] for d in range(recv_ref.shape[0])])
    total = jnp.sum(squares, axis=0, keepdims=True)
    factor = inverse_norm(total) / inverse_norm(squares)
    energy = jnp.sum(energy * factor * factor, axis=0, keepdims=True)
    first = []
    second = []
    for d in range(recv_ref.shape[0]):
        column = column_of(factor[d : d + 1])
        first.append(recv_ref[d, :RHS] * column)
        second.append(recv_ref[d, RHS : 2 * RHS] * column)
    return first, second, factor, total, energy


def pair_group(level, me_ref, recv_ref, up_row_ref, up_col_ref, up_couple_ref, nodes_ref, keep):
    place = (me_ref[0] >> level) % NEAR
    first, second, _, total, energy = rescale(recv_ref)
    cross = jnp.zeros((RHS, RANK), f32)
    for height in range(PATH):
        j = level + height
        base = LEVEL_BASE[height]
        gained = couple_all(first, (pair_at(up_couple_ref, j, 0), pair_at(up_couple_ref, j, 1)))
        summed = []
        for k in range(len(first)):
            moved = mm(gained[k], pair_at(nodes_ref, base + k))
            cross = cross + gained[k] * (2.0 * second[k] + moved)
            summed.append(second[k] + moved)
        if keep is not None:
            path_ref, gain_ref, below_ref = keep
            for k in range(len(first)):
                gain_ref[base + k] = gained[k]
                below_ref[base + k] = second[k]
            own = base + (place >> height)
            other = base + ((place >> height) ^ 1)
            path_ref[3 * height] = gain_ref[own]
            path_ref[3 * height + 1] = gain_ref[other]
            path_ref[3 * height + 2] = below_ref[other]
        first = climb(first, pair_at(up_col_ref, j))
        second = climb(summed, pair_at(up_row_ref, j))
    energy = energy + row_of(jnp.sum(cross, axis=1, keepdims=True))
    return first[0], second[0], stat_block(total, energy)


def near_pair_kernel(
    me_ref,
    recv_ref,
    up_row_ref,
    up_col_ref,
    up_couple_ref,
    nodes_ref,
    diagonal_ref,
    msg_ref,
    path_ref,
    own_ref,
    mid_nodes_ref,
    gram_ref,
    gain_ref,
    below_ref,
):
    keep = (path_ref, gain_ref, below_ref)
    first, second, stats = pair_group(
        0, me_ref, recv_ref, up_row_ref, up_col_ref, up_couple_ref, nodes_ref, keep
    )
    own_ref[...] = stats
    send(msg_ref, stack([first, second, stats]))
    base = 2 * RHS + 8
    grams = []
    for d in range(MID):
        low = base + d * SLICE
        top = stack([recv_ref[p, low : low + SLICE] for p in range(NEAR)])
        grams.append(unpack(top, diagonal_ref[d : d + 1]))
    top, diagonal = pack(group_grams(PATH, grams, up_row_ref, mid_nodes_ref))
    gram_ref[...] = stack([top, stat_block(diagonal)])


def mid_pair_kernel(
    me_ref,
    recv_ref,
    up_row_ref,
    up_col_ref,
    up_couple_ref,
    nodes_ref,
    gram_ref,
    msg_ref,
    path_ref,
    own_ref,
    gain_ref,
    below_ref,
):
    keep = (path_ref, gain_ref, below_ref)
    first, second, stats = pair_group(
        PATH, me_ref, recv_ref, up_row_ref, up_col_ref, up_couple_ref, nodes_ref, keep
    )
    own_ref[...] = stats
    send(msg_ref, stack([first, second, stats, gram_ref[...]]))


def last_pair_kernel(
    level, me_ref, recv_ref, up_row_ref, up_col_ref, up_couple_ref, nodes_ref, msg_ref
):
    parts = pair_group(
        level, me_ref, recv_ref, up_row_ref, up_col_ref, up_couple_ref, nodes_ref, None
    )
    send(msg_ref, stack(parts))


def top_levels(recv_ref, up_row_ref, up_col_ref, up_couple_ref, gram_ref):
    first, second, _, total, energy = rescale(recv_ref)
    gained = couple_all(first, (pair_at(up_couple_ref, 6, 0), pair_at(up_couple_ref, 6, 1)))
    first = climb(first, pair_at(up_col_ref, 6))
    potential = couple_all(first, (pair_at(up_couple_ref, 7, 0), pair_at(up_couple_ref, 7, 1)))
    below = descend(potential, pair_at(up_row_ref, 6))
    potential = [a + b for a, b in zip(gained, below)]
    cross = jnp.zeros((RHS, RANK), f32)
    summed = []
    for d in range(FAR):
        moved = mm(potential[d], pair_at(gram_ref, d))
        cross = cross + potential[d] * (2.0 * second[d] + moved)
        summed.append(second[d] + moved)
    energy = column_of(energy) + jnp.sum(cross, axis=1, keepdims=True)
    return potential, summed, column_of(total), energy


def middle_kernel(
    me_ref,
    rows_ref,
    part0_ref,
    part1_ref,
    part2_ref,
    part3_ref,
    near_path_ref,
    near_own_ref,
    mid_path_ref,
    mid_own_ref,
    near_gain_ref,
    mid_gain_ref,
    up_row_ref,
    up_col_ref,
    up_couple_ref,
    near_nodes_ref,
    mid_nodes_ref,
    dense_ref,
    row_basis_ref,
    col_basis_ref,
    local_row_ref,
    local_col_ref,
    local_couple_ref,
    x_ref,
    own_in_ref,
    inner_ref,
    v_ref,
    next_ref,
    alpha_ref,
    rho_ref,
    msg_ref,
    top_gram_ref,
    a_ref,
    b_ref,
    recv_ref,
):
    me = me_ref[0]
    gather_far(me, (part0_ref, part1_ref, part2_ref, part3_ref), recv_ref)
    place = me >> (2 * PATH)
    base = 2 * RHS + 8
    for d in range(FAR):
        gram = unpack(recv_ref[d, base : base + HALF], recv_ref[d, base + HALF : base + HALF + 1])
        store_pair(top_gram_ref, d, gram)
    potential, summed, squares, energy = top_levels(
        recv_ref, up_row_ref, up_col_ref, up_couple_ref, top_gram_ref
    )
    alpha = jnp.sqrt(squares)
    rho = jnp.sqrt(energy)
    alpha_ref[...] = jnp.broadcast_to(alpha, (RHS, RANK))
    rho_ref[...] = jnp.broadcast_to(rho, (RHS, RANK))
    scale = inverse_norm(squares)
    for d in range(FAR):
        a_ref[d] = potential[d]
        b_ref[d] = summed[d]
    forward = a_ref[place]
    siblings = {6: b_ref[place ^ 1]}
    for k, value in enumerate(climb(summed, pair_at(up_row_ref, 6))):
        a_ref[FAR + k] = value
    siblings[7] = a_ref[FAR + ((place >> 1) ^ 1)]
    for level, path_ref, part_ref, nodes_ref in (
        (PATH, mid_path_ref, mid_own_ref, mid_nodes_ref),
        (0, near_path_ref, near_own_ref, near_nodes_ref),
    ):
        factor = scale / inverse_norm(column_of(part_ref[:1]))
        inside = (me >> level) % NEAR
        for height in reversed(range(PATH)):
            j = level + height
            child = (me >> j) & 1
            spread = mm(forward, pair_at(up_row_ref, j), transposed=True)
            low = spread[:, :RANK]
            high = spread[:, RANK:]
            forward = path_ref[3 * height] * factor + jnp.where(child == 0, low, high)
            other = path_ref[3 * height + 1] * factor + jnp.where(child == 0, high, low)
            gram = pair_at(nodes_ref, LEVEL_BASE[height] + ((inside >> height) ^ 1))
            siblings[j] = path_ref[3 * height + 2] * factor + mm(other, gram)
    backward = from_siblings([siblings[j] for j in range(8)], near_gain_ref, mid_gain_ref)
    local = readers(
        (dense_ref, row_basis_ref, col_basis_ref, local_row_ref, local_col_ref, local_couple_ref)
    )
    dense, row_basis, col_basis, local_row, local_col, coupling = local
    own_factor = scale / inverse_norm(column_of(own_in_ref[:1]))
    outer = local_down(forward, None, None, coupling, local_row, False)
    images = []
    for q in range(LEAF_DEV):
        y = mm(outer[q], row_basis(q), transposed=True) * live_mask(rows_ref, q)
        images.append(y + inner_ref[:, row_part(q)] * own_factor)
    leaf, node = local_up(images, row_basis, local_row)
    down = local_down(backward, leaf, node, coupling, local_col, True)
    inverse = 1.0 / rho
    parts = []
    for q in range(LEAF_DEV):
        v = x_ref[:, col_part(q)] * scale
        v_ref[:, col_part(q)] = v
        x = mm(images[q], dense(q)) + mm(down[q], col_basis(q), transposed=True)
        x = x * inverse - rho * v
        next_ref[:, col_part(q)] = x
        parts.append(x)
    pair_up(parts, local, rows_ref, msg_ref, None, None, [])


def final_kernel(
    me_ref,
    part0_ref,
    part1_ref,
    part2_ref,
    part3_ref,
    up_row_ref,
    up_col_ref,
    up_couple_ref,
    top_gram_ref,
    beta_ref,
    alpha_ref,
    rho_ref,
    v_ref,
    x_ref,
    out_ref,
    recv_ref,
):
    gather_far(me_ref[0], (part0_ref, part1_ref, part2_ref, part3_ref), recv_ref)
    _, _, squares, energy = top_levels(
        recv_ref, up_row_ref, up_col_ref, up_couple_ref, top_gram_ref
    )
    theta = jnp.sqrt(squares)
    rho2 = jnp.sqrt(energy - squares)
    rho = rho_ref[:, :1]
    phi = alpha_ref[:, :1] / rho * beta_ref[:, :1]
    v = v_ref[...]
    search = x_ref[...] * inverse_norm(squares) - (theta / rho) * v
    out_ref[...] = (phi / rho) * v - (phi * (theta / rho2) / rho2) * search


def call(kernel, outs, operands, scratch=(), far=(), limit=VMEM_LIMIT):
    spaces = []
    for index, operand in enumerate(operands):
        space = pltpu.SMEM if operand.dtype == jnp.int32 else pltpu.VMEM
        spaces.append(pl.ANY if index in far else space)
    outs = [shape if isinstance(shape, jax.ShapeDtypeStruct) else jax.ShapeDtypeStruct(shape, f32) for shape in outs]
    return pl.pallas_call(
        kernel,
        out_shape=outs,
        in_specs=[pl.BlockSpec(memory_space=space) for space in spaces],
        out_specs=[pl.BlockSpec(memory_space=pltpu.VMEM)] * len(outs),
        scratch_shapes=[
            pltpu.VMEM(shape, f32) if isinstance(shape, tuple) else shape for shape in scratch
        ],
        compiler_params=pltpu.CompilerParams(vmem_limit_bytes=limit),
        cost_estimate=pl.CostEstimate(flops=COST_FLOPS, bytes_accessed=0, transcendentals=0),
    )(*operands)


def device_groups(devices, stride, size):
    out = []
    for base in range(devices):
        if (base // stride) % size == 0:
            out.append([base + k * stride for k in range(size)])
    return out


def local_program(
    devices,
    rhs,
    box_rows,
    dense,
    row_basis,
    col_basis,
    local_col,
    local_row,
    local_couple,
    up_col,
    up_row,
    up_couple,
):
    me = lax.axis_index("leaf").astype(jnp.int32).reshape(1)
    near, mid = (1, NEAR), (NEAR, MID)

    def swap_far(message):
        parts = [message]
        for k in range(1, FAR):
            pairs = [(i, i ^ (k * NEAR * MID)) for i in range(devices)]
            parts.append(lax.ppermute(message, "leaf", pairs))
        return parts

    def swap(message, group):
        return lax.all_to_all(message, "leaf", 0, 0, axis_index_groups=device_groups(devices, *group))

    tile = (RHS, RANK)
    row_shape = (RHS, LEAF_DEV * LEAF_ROWS)
    col_shape = (RHS, LEAF_DEV * LEAF_COLS)
    single = (RHS + 8, RANK)
    double = (2 * RHS + 8, RANK)

    def longer(shape, rows):
        return (shape[0] + rows, shape[1])

    stat = (8, RANK)
    gram_shape = (RANK, RANK)
    tables = [up_row, up_col, up_couple]

    def nodes_shape(count):
        return jax.ShapeDtypeStruct((2, count) + gram_shape, bf16)

    path_shape = (3 * PATH,) + tile
    pair_scratch = [(14,) + tile, (14,) + tile]

    def last_pair(level, message, peers, nodes):
        return call(
            functools.partial(last_pair_kernel, level),
            [(peers,) + double],
            [me, message] + tables + [nodes],
        )[0]

    z, message = call(
        start_kernel,
        [(RHS, KEEP + 6 * RANK), (NEAR,) + longer(single, HALF)],
        [me, box_rows, rhs, row_basis, local_row],
        [pltpu.SMEM(box_rows.shape, jnp.int32)]
        + [k.shape for k in (rhs, row_basis, local_row)]
        + [pltpu.SemaphoreType.DMA((4,))],
        range(1, 5),
        START_LIMIT,
    )
    blocks = [dense, row_basis, col_basis, local_row, local_col, local_couple]
    message, near_sib, near_nodes, near_gain, path = call(
        near_kernel,
        [(MID,) + longer(single, SLICE), (PATH,) + tile, nodes_shape(14), nodes_shape(PATH), gram_shape],
        [me, swap(message, near)] + tables,
        [(14,) + tile, (HALF, RANK)],
    )
    message, mid_sib, mid_gain, part, diagonal = call(
        mid_kernel,
        [(1,) + single, (PATH,) + tile, nodes_shape(8 - PATH), (HALF, RANK), stat],
        [me, swap(message, mid)] + tables + [path],
        [(14,) + tile],
    )
    gains = [near_gain, mid_gain]
    x, beta, message, own, inner = call(
        first_kernel,
        [col_shape, tile, (NEAR,) + longer(double, HALF), stat, row_shape],
        [me, box_rows]
        + swap_far(message)
        + [near_sib, mid_sib]
        + gains
        + [part, up_row]
        + blocks
        + [z],
        [(2,) + tile, (FAR,) + single],
    )
    message, near_path, near_own, mid_nodes, gram = call(
        near_pair_kernel,
        [(MID,) + double, path_shape, stat, nodes_shape(14), (HALF + 8, RANK)],
        [me, swap(message, near)] + tables + [near_nodes, diagonal],
        pair_scratch,
    )
    message, mid_path, mid_own = call(
        mid_pair_kernel,
        [(1,) + longer(double, HALF + 8), path_shape, stat],
        [me, swap(message, mid)] + tables + [mid_nodes, gram],
        pair_scratch,
    )
    v, x, alpha, rho, message, top_nodes = call(
        middle_kernel,
        [col_shape, col_shape, tile, tile, (NEAR,) + double, nodes_shape(FAR)],
        [me, box_rows]
        + swap_far(message)
        + [near_path, near_own, mid_path, mid_own]
        + gains
        + tables
        + [near_nodes, mid_nodes]
        + blocks
        + [x, own, inner],
        [(6,) + tile, (4,) + tile, (FAR,) + longer(double, HALF + 8)],
    )
    message = last_pair(0, swap(message, near), MID, near_nodes)
    message = last_pair(PATH, swap(message, mid), 1, mid_nodes)
    (out,) = call(
        final_kernel,
        [col_shape],
        [me] + swap_far(message) + tables + [top_nodes, beta, alpha, rho, v, x],
        [(FAR,) + double],
    )
    return out


def solution(mesh):
    devices = mesh.shape["leaf"]
    return jax.shard_map(
        functools.partial(local_program, devices),
        mesh=mesh,
        in_specs=(
            P(None, "leaf"),
            P("leaf"),
            P("leaf", None, None),
            P("leaf", None, None),
            P("leaf", None, None),
            P("leaf", None, None),
            P("leaf", None, None),
            P("leaf", None, None, None),
            P(),
            P(),
            P(),
        ),
        out_specs=P(None, "leaf"),
        check_vma=False,
    )
```

```python
import functools

import jax
import jax.numpy as jnp
from jax import lax
from jax.experimental import pallas as pl
from jax.experimental.pallas import tpu as pltpu
from jax.sharding import PartitionSpec as P

RHS = 16
RANK = 128
LEAF_DEV = 4
LEAF_ROWS = 512
LEAF_COLS = 256
HALF = RANK // 2
SLICE = 8
COST_FLOPS = 6000000000
KEEP = LEAF_DEV * LEAF_ROWS
TINY = 1.2e-38
NEAR = 8
STAGES = {"core": (0, 1), "row": (1, 2), "mid": (3, 3), "far": (6, 2)}
VMEM_MIB = 24
VMEM_LIMIT = VMEM_MIB * 1024 * 1024
START_LIMIT = 60 * 1024 * 1024

f32 = jnp.float32
bf16 = jnp.bfloat16


def split(v):
    head = v.astype(bf16)
    return head, (v - head.astype(f32)).astype(bf16)


def mm(x, pair, transposed=False):
    xh, xl = split(x)
    wh, wl = pair
    dims = (((1,), (1 if transposed else 0,)), ((), ()))
    n = x.shape[0]
    both = lax.dot_general(jnp.concatenate([xh, xl], 0), wh, dims, preferred_element_type=f32)
    rest = lax.dot_general(xh, wl, dims, preferred_element_type=f32)
    return both[:n] + (both[n:] + rest)


def mm_inner(a, b):
    ah, al = split(a)
    bh, bl = split(b)
    dims = (((0,), (0,)), ((), ()))
    m = a.shape[1]
    both = lax.dot_general(jnp.concatenate([ah, al], 1), bh, dims, preferred_element_type=f32)
    rest = lax.dot_general(ah, bl, dims, preferred_element_type=f32)
    return both[:m] + (both[m:] + rest)


def pair_at(ref, *index):
    if ref.dtype == bf16:
        return ref[(0,) + index], ref[(1,) + index]
    return split(ref[index])


def pairs_of(ref):
    return functools.partial(pair_at, ref)


def half_of(ref, j, child):
    return pair_at(ref, j, pl.ds(pl.multiple_of(child * RANK, RANK), RANK))


def eye():
    return (
        lax.broadcasted_iota(jnp.int32, (RHS, RANK), 0)
        == lax.broadcasted_iota(jnp.int32, (RHS, RANK), 1)
    ).astype(f32)


def stat_block(*values):
    rows = lax.broadcasted_iota(jnp.int32, (8, RANK), 0)
    block = jnp.where(rows == 0, values[0], 0.0)
    for k in range(1, len(values)):
        block = jnp.where(rows == k, values[k], block)
    return block


def column_of(row):
    return jnp.sum(row * eye(), axis=1, keepdims=True)


def row_of(column):
    return jnp.sum(column * eye(), axis=0, keepdims=True)


def inverse_norm(squares):
    return jnp.where(squares >= TINY, 1.0 / jnp.sqrt(squares), 1.0)


def sum_squares(v):
    return jnp.sum(v * v, axis=1, keepdims=True)


def send(out_ref, value):
    for peer in range(out_ref.shape[0]):
        out_ref[peer] = value


def stack(blocks):
    return jnp.concatenate(blocks, 0)


def unstack(value, count):
    size = value.shape[0] // count
    return [value[k * size : (k + 1) * size] for k in range(count)]


def climb(blocks, transfer):
    count = len(blocks) // 2
    paired = [jnp.concatenate([blocks[2 * m], blocks[2 * m + 1]], 1) for m in range(count)]
    return unstack(mm(stack(paired), transfer), count)


def descend(blocks, transfer):
    spread = unstack(mm(stack(blocks), transfer, transposed=True), len(blocks))
    out = []
    for block in spread:
        out += [block[:, :RANK], block[:, RANK:]]
    return out


def couple_all(blocks, coupling):
    count = len(blocks) // 2
    even = unstack(mm(stack(blocks[1::2]), coupling[0]), count)
    odd = unstack(mm(stack(blocks[0::2]), coupling[1]), count)
    out = []
    for m in range(count):
        out += [even[m], odd[m]]
    return out


def local_up(parts, basis, transfer):
    leaf = [mm(parts[q], basis(q)) for q in range(LEAF_DEV)]
    node = [
        mm(jnp.concatenate([leaf[2 * m], leaf[2 * m + 1]], 1), transfer(m)) for m in range(2)
    ]
    return leaf, node


def local_root(node, transfer):
    return mm(jnp.concatenate(node, 1), transfer(2))


def couple(sibling, coupling, node, child, adjoint):
    if adjoint:
        return mm(sibling, coupling(node, 1 - child), transposed=True)
    return mm(sibling, coupling(node, child))


def local_down(root, leaf, node, coupling, transfer, adjoint):
    spread = None if root is None else mm(root, transfer(2), transposed=True)
    out = []
    for m in range(2):
        here = None if spread is None else spread[:, m * RANK : (m + 1) * RANK]
        if node is not None:
            gained = couple(node[1 - m], coupling, 2, m, adjoint)
            here = gained if here is None else here + gained
        below = mm(here, transfer(m), transposed=True)
        for i in range(2):
            value = below[:, i * RANK : (i + 1) * RANK]
            if leaf is not None:
                value = value + couple(leaf[2 * m + 1 - i], coupling, m, i, adjoint)
            out.append(value)
    return out


def live_mask(rows_ref, q):
    slots = lax.broadcasted_iota(jnp.int32, (RHS, LEAF_ROWS), 1)
    return (slots < rows_ref[q]).astype(f32)


def row_part(q):
    return slice(q * LEAF_ROWS, (q + 1) * LEAF_ROWS)


def col_part(q):
    return slice(q * LEAF_COLS, (q + 1) * LEAF_COLS)


def pair_up(parts, local, rows_ref, msg_ref, own_ref, inner_ref, extra):
    dense, row_basis, col_basis, local_row, local_col, coupling = local
    squares = sum_squares(parts[0])
    for part in parts[1:]:
        squares = squares + sum_squares(part)
    scale = inverse_norm(squares)
    parts = [part * scale for part in parts]
    leaf, node = local_up(parts, col_basis, local_col)
    root = local_root(node, local_col)
    down = local_down(None, leaf, node, coupling, local_row, False)
    result = []
    energy = jnp.zeros((RHS, 1), f32)
    for q in range(LEAF_DEV):
        y = mm(parts[q], dense(q), transposed=True)
        y = y + mm(down[q], row_basis(q), transposed=True)
        y = y * live_mask(rows_ref, q)
        if inner_ref is not None:
            inner_ref[:, row_part(q)] = y
        energy = energy + sum_squares(y)
        result.append(y)
    _, row_node = local_up(result, row_basis, local_row)
    row_root = local_root(row_node, local_row)
    stats = stat_block(row_of(squares), row_of(energy))
    if own_ref is not None:
        own_ref[...] = stats
    send(msg_ref, stack([root, row_root, stats] + extra))


def both_sides(grams, half):
    full = half[0].astype(f32) + half[1].astype(f32)
    left = mm(jnp.transpose(full), split(jnp.concatenate(grams, 1)))
    columns = [left[:, k * RANK : (k + 1) * RANK] for k in range(len(grams))]
    return unstack(mm(stack(columns), half), len(grams))


def gram_climb(grams, transfer):
    even = both_sides(grams[0::2], (transfer[0][:RANK], transfer[1][:RANK]))
    odd = both_sides(grams[1::2], (transfer[0][RANK:], transfer[1][RANK:]))
    return [a + b for a, b in zip(even, odd)]


def pack(gram):
    row = lax.broadcasted_iota(jnp.int32, (HALF, RANK), 0)
    col = lax.broadcasted_iota(jnp.int32, (HALF, RANK), 1)
    last = gram[HALF:]
    top = jnp.where((col < HALF) & (col > row), pltpu.roll(last, HALF, 1), gram[:HALF])
    diagonal = jnp.sum(jnp.where(col - HALF == row, last, 0.0), axis=0, keepdims=True)
    return top, diagonal


def unpack(top, diagonal):
    row = lax.broadcasted_iota(jnp.int32, (HALF, RANK), 0)
    col = lax.broadcasted_iota(jnp.int32, (HALF, RANK), 1)
    upper = jnp.where((col >= HALF) | (col < row), top, jnp.where(col == row, 0.5 * top, 0.0))
    lower = jnp.where(
        col - HALF > row,
        pltpu.roll(top, HALF, 1),
        jnp.where(col - HALF == row, 0.5 * diagonal, 0.0),
    )
    part = stack([upper, lower])
    return part + jnp.transpose(part)


def stage(name):
    level, heights = STAGES[name]
    return level, heights, 1 << heights


def place_of(me, name):
    level, _, count = stage(name)
    return (me >> level) % count


def bases(name):
    _, heights, count = stage(name)
    return [sum(count >> k for k in range(height)) for height in range(heights)]


def node_count(name):
    return 2 * stage(name)[2] - 2


def gather_parts(me, name, parts, out_ref):
    for k, part in enumerate(parts):
        out_ref[place_of(me, name) ^ k] = part[0]


def store_pair(ref, index, value):
    high, low = split(value)
    ref[0, index] = high
    ref[1, index] = low


def group_grams(name, grams, up_row_ref, nodes_ref):
    for height, base in enumerate(bases(name)):
        for k, value in enumerate(grams):
            store_pair(nodes_ref, base + k, value)
        grams = gram_climb(grams, pair_at(up_row_ref, stage(name)[0] + height))
    return grams[0]


def start_copies(pairs, sems):
    copies = [
        pltpu.make_async_copy(source, target, sems.at[k])
        for k, (source, target) in enumerate(pairs)
    ]
    for copy in copies:
        copy.start()
    return copies


def start_kernel(
    me_ref,
    rows_hbm,
    rhs_hbm,
    row_basis_hbm,
    local_row_hbm,
    z_ref,
    msg_ref,
    rows_ref,
    rhs_ref,
    row_basis_ref,
    local_row_ref,
    sems,
):
    pairs = [(rows_hbm, rows_ref), (rhs_hbm, rhs_ref)]
    pairs += [(row_basis_hbm, row_basis_ref), (local_row_hbm, local_row_ref)]
    for copy in start_copies(pairs, sems):
        copy.wait()
    squares = jnp.zeros((RHS, 1), f32)
    local_row = [split(local_row_ref[m]) for m in range(3)]
    leaf = []
    grams = []
    for q in range(LEAF_DEV):
        part = rhs_ref[:, row_part(q)] * live_mask(rows_ref, q)
        z_ref[:, row_part(q)] = part
        squares = squares + sum_squares(part)
        leaf.append(mm(part, split(row_basis_ref[q])))
    for q in range(LEAF_DEV):
        slots = lax.broadcasted_iota(jnp.int32, (LEAF_ROWS, RANK), 0)
        basis = jnp.where(slots < rows_ref[q], row_basis_ref[q], 0.0)
        grams.append(mm_inner(basis, basis))
    node = [climb(leaf[2 * m : 2 * m + 2], local_row[m])[0] for m in range(2)]
    for k, value in enumerate(leaf + node):
        z_ref[:, KEEP + k * RANK : KEEP + (k + 1) * RANK] = value
    root = climb(node, local_row[2])[0]
    row = row_of(squares)
    nodes = [gram_climb(grams[2 * m : 2 * m + 2], local_row[m])[0] for m in range(2)]
    gram = gram_climb(nodes, local_row[2])[0]
    top, diagonal = pack(gram)
    send(msg_ref, stack([root, stat_block(row, row, diagonal), top]))


def sum_stats(recv_ref):
    stats = recv_ref[0, RHS : RHS + 8]
    for d in range(1, recv_ref.shape[0]):
        stats = stats + recv_ref[d, RHS : RHS + 8]
    return stats


def climb_group(name, me_ref, recv_ref, climb_ref, sib_ref, scratch_ref):
    level = stage(name)[0]
    place = place_of(me_ref[0], name)
    summaries = [recv_ref[d, :RHS] for d in range(recv_ref.shape[0])]
    for height, base in enumerate(bases(name)):
        for m, value in enumerate(summaries):
            scratch_ref[base + m] = value
        sib_ref[height] = scratch_ref[base + ((place >> height) ^ 1)]
        summaries = climb(summaries, pair_at(climb_ref, level + height))
    return summaries[0]


def received_grams(recv_ref):
    base = RHS + 8
    count = recv_ref.shape[0]
    return [unpack(recv_ref[d, base:], recv_ref[d, RHS + 2 : RHS + 3]) for d in range(count)]


def path_product(me, level, path, up_col_ref):
    half = half_of(up_col_ref, level, (me >> level) & 1)
    return mm(path, half)


def sibling_gain(me, level, path, up_couple_ref):
    child = 1 - ((me >> level) & 1)
    return mm(path, pair_at(up_couple_ref, level, child))


def core_kernel(
    me_ref,
    part0_ref,
    part1_ref,
    up_row_ref,
    msg_ref,
    sib_ref,
    nodes_ref,
    recv_ref,
    scratch_ref,
):
    gather_parts(me_ref[0], "core", (part0_ref, part1_ref), recv_ref)
    summary = climb_group("core", me_ref, recv_ref, up_row_ref, sib_ref, scratch_ref)
    top, diagonal = pack(group_grams("core", received_grams(recv_ref), up_row_ref, nodes_ref))
    stats = sum_stats(recv_ref)
    send(msg_ref, stack([summary, stat_block(stats[:1], stats[1:2], diagonal), top]))


def row_kernel(
    me_ref,
    part0_ref,
    part1_ref,
    part2_ref,
    part3_ref,
    up_row_ref,
    up_col_ref,
    up_couple_ref,
    msg_ref,
    sib_ref,
    nodes_ref,
    gain_ref,
    path_ref,
    recv_ref,
    scratch_ref,
    slice_ref,
):
    me = me_ref[0]
    gather_parts(me, "row", (part0_ref, part1_ref, part2_ref, part3_ref), recv_ref)
    summary = climb_group("row", me_ref, recv_ref, up_row_ref, sib_ref, scratch_ref)
    gram = group_grams("row", received_grams(recv_ref), up_row_ref, nodes_ref)
    child = 1 - (me & 1)
    store_pair(gain_ref, 0, up_couple_ref[0, child])
    path = up_col_ref[0, pl.ds(pl.multiple_of((me & 1) * RANK, RANK), RANK), :]
    for j in range(1, 3):
        store_pair(gain_ref, j, sibling_gain(me, j, path, up_couple_ref))
        path = path_product(me, j, path, up_col_ref)
    path_ref[...] = path
    top, diagonal = pack(gram)
    slice_ref[...] = top
    part = slice_ref[pl.ds(pl.multiple_of((me % NEAR) * SLICE, SLICE), SLICE), :]
    stats = sum_stats(recv_ref)
    send(msg_ref, stack([summary, stat_block(stats[:1], stats[1:2], diagonal), part]))


def mid_kernel(
    me_ref,
    recv_ref,
    up_row_ref,
    up_col_ref,
    up_couple_ref,
    path_ref,
    msg_ref,
    sib_ref,
    gain_ref,
    part_ref,
    diagonal_ref,
    scratch_ref,
):
    me = me_ref[0]
    level, _, count = stage("mid")
    summary = climb_group("mid", me_ref, recv_ref, up_row_ref, sib_ref, scratch_ref)
    path = path_ref[...]
    for j in range(level, 8):
        store_pair(gain_ref, j - level, sibling_gain(me, j, path, up_couple_ref))
        if j < 7:
            path = path_product(me, j, path, up_col_ref)
    for d in range(count):
        part_ref[d * SLICE : (d + 1) * SLICE] = recv_ref[d, RHS + 8 :]
        diagonal_ref[d : d + 1] = recv_ref[d, RHS + 2 : RHS + 3]
    send(msg_ref, stack([summary, sum_stats(recv_ref)]))


def from_siblings(siblings, near_gain_ref, mid_gain_ref):
    gains = [pair_at(near_gain_ref, j) for j in range(3)]
    gains += [pair_at(mid_gain_ref, j) for j in range(5)]
    gains = tuple(jnp.concatenate([g[k] for g in gains], 1) for k in range(2))
    return mm(jnp.concatenate(siblings, 1), gains, transposed=True)


def readers(local):
    return [pairs_of(ref) for ref in local]


def first_kernel(
    me_ref,
    rows_ref,
    part0_ref,
    part1_ref,
    part2_ref,
    part3_ref,
    core_sib_ref,
    row_sib_ref,
    mid_sib_ref,
    near_gain_ref,
    mid_gain_ref,
    part_ref,
    up_row_ref,
    dense_ref,
    row_basis_ref,
    col_basis_ref,
    local_row_ref,
    local_col_ref,
    local_couple_ref,
    z_ref,
    x_ref,
    beta_ref,
    msg_ref,
    own_ref,
    inner_ref,
    scratch_ref,
    recv_ref,
):
    me = me_ref[0]
    gather_parts(me, "far", (part0_ref, part1_ref, part2_ref, part3_ref), recv_ref)
    place = place_of(me, "far")
    summaries = [recv_ref[d, :RHS] for d in range(recv_ref.shape[0])]
    siblings = [core_sib_ref[0]] + [row_sib_ref[j] for j in range(2)] + [mid_sib_ref[j] for j in range(3)]
    siblings.append(recv_ref[place ^ 1, :RHS])
    summaries = climb(summaries, pair_at(up_row_ref, 6))
    for m, value in enumerate(summaries):
        scratch_ref[m] = value
    siblings.append(scratch_ref[(place >> 1) ^ 1])
    potential = from_siblings(siblings, near_gain_ref, mid_gain_ref)
    beta = jnp.sqrt(column_of(sum_stats(recv_ref)[:1]))
    inverse = 1.0 / beta
    beta_ref[...] = jnp.broadcast_to(beta, (RHS, RANK))
    local = readers(
        (dense_ref, row_basis_ref, col_basis_ref, local_row_ref, local_col_ref, local_couple_ref)
    )
    dense, _, col_basis, _, local_col, coupling = local
    keep = [z_ref[:, KEEP + k * RANK : KEEP + (k + 1) * RANK] for k in range(LEAF_DEV + 2)]
    leaf, node = keep[:LEAF_DEV], keep[LEAF_DEV:]
    down = local_down(potential, leaf, node, coupling, local_col, True)
    parts = []
    for q in range(LEAF_DEV):
        x = mm(z_ref[:, row_part(q)], dense(q))
        x = (x + mm(down[q], col_basis(q), transposed=True)) * inverse
        x_ref[:, col_part(q)] = x
        parts.append(x)
    pair_up(parts, local, rows_ref, msg_ref, own_ref, inner_ref, [part_ref[...]])


def rescale(recv_ref):
    base = 2 * RHS
    squares = stack([recv_ref[d, base : base + 1] for d in range(recv_ref.shape[0])])
    energy = stack([recv_ref[d, base + 1 : base + 2] for d in range(recv_ref.shape[0])])
    total = jnp.sum(squares, axis=0, keepdims=True)
    factor = inverse_norm(total) / inverse_norm(squares)
    energy = jnp.sum(energy * factor * factor, axis=0, keepdims=True)
    first = []
    second = []
    for d in range(recv_ref.shape[0]):
        column = column_of(factor[d : d + 1])
        first.append(recv_ref[d, :RHS] * column)
        second.append(recv_ref[d, RHS : 2 * RHS] * column)
    return first, second, factor, total, energy


def pair_group(name, me_ref, recv_ref, tables, nodes_ref, keep):
    up_row_ref, up_col_ref, up_couple_ref = tables
    level = stage(name)[0]
    place = place_of(me_ref[0], name)
    first, second, _, total, energy = rescale(recv_ref)
    cross = jnp.zeros((RHS, RANK), f32)
    for height, base in enumerate(bases(name)):
        j = level + height
        gained = couple_all(first, (pair_at(up_couple_ref, j, 0), pair_at(up_couple_ref, j, 1)))
        summed = []
        for k in range(len(first)):
            moved = mm(gained[k], pair_at(nodes_ref, base + k))
            cross = cross + gained[k] * (2.0 * second[k] + moved)
            summed.append(second[k] + moved)
        if keep is not None:
            path_ref, gain_ref, below_ref = keep
            for k in range(len(first)):
                gain_ref[base + k] = gained[k]
                below_ref[base + k] = second[k]
            own = base + (place >> height)
            other = base + ((place >> height) ^ 1)
            path_ref[3 * height] = gain_ref[own]
            path_ref[3 * height + 1] = gain_ref[other]
            path_ref[3 * height + 2] = below_ref[other]
        first = climb(first, pair_at(up_col_ref, j))
        second = climb(summed, pair_at(up_row_ref, j))
    energy = energy + row_of(jnp.sum(cross, axis=1, keepdims=True))
    return first[0], second[0], stat_block(total, energy)


def core_pair_kernel(
    me_ref,
    part0_ref,
    part1_ref,
    up_row_ref,
    up_col_ref,
    up_couple_ref,
    nodes_ref,
    msg_ref,
    path_ref,
    own_ref,
    recv_ref,
    gain_ref,
    below_ref,
):
    gather_parts(me_ref[0], "core", (part0_ref, part1_ref), recv_ref)
    tables = (up_row_ref, up_col_ref, up_couple_ref)
    keep = (path_ref, gain_ref, below_ref)
    first, second, stats = pair_group("core", me_ref, recv_ref, tables, nodes_ref, keep)
    own_ref[...] = stats
    base = 2 * RHS + 8
    send(msg_ref, stack([first, second, stats, recv_ref[0, base:], recv_ref[1, base:]]))


def row_pair_kernel(
    me_ref,
    part0_ref,
    part1_ref,
    part2_ref,
    part3_ref,
    up_row_ref,
    up_col_ref,
    up_couple_ref,
    nodes_ref,
    diagonal_ref,
    msg_ref,
    path_ref,
    own_ref,
    mid_nodes_ref,
    gram_ref,
    recv_ref,
    gain_ref,
    below_ref,
):
    gather_parts(me_ref[0], "row", (part0_ref, part1_ref, part2_ref, part3_ref), recv_ref)
    tables = (up_row_ref, up_col_ref, up_couple_ref)
    keep = (path_ref, gain_ref, below_ref)
    first, second, stats = pair_group("row", me_ref, recv_ref, tables, nodes_ref, keep)
    own_ref[...] = stats
    send(msg_ref, stack([first, second, stats]))
    base = 2 * RHS + 8
    grams = []
    for d in range(stage("mid")[2]):
        slices = []
        for p in range(NEAR):
            low = base + (p % 2) * HALF + d * SLICE
            slices.append(recv_ref[p // 2, low : low + SLICE])
        grams.append(unpack(stack(slices), diagonal_ref[d : d + 1]))
    top, diagonal = pack(group_grams("mid", grams, up_row_ref, mid_nodes_ref))
    gram_ref[...] = stack([top, stat_block(diagonal)])


def mid_pair_kernel(
    me_ref,
    recv_ref,
    up_row_ref,
    up_col_ref,
    up_couple_ref,
    nodes_ref,
    gram_ref,
    msg_ref,
    path_ref,
    own_ref,
    gain_ref,
    below_ref,
):
    tables = (up_row_ref, up_col_ref, up_couple_ref)
    keep = (path_ref, gain_ref, below_ref)
    first, second, stats = pair_group("mid", me_ref, recv_ref, tables, nodes_ref, keep)
    own_ref[...] = stats
    send(msg_ref, stack([first, second, stats, gram_ref[...]]))


def last_pair_kernel(name, me_ref, *refs):
    if name == "mid":
        recv_ref, up_row_ref, up_col_ref, up_couple_ref, nodes_ref, msg_ref = refs
    else:
        count = stage(name)[2]
        up_row_ref, up_col_ref, up_couple_ref, nodes_ref, msg_ref, recv_ref = refs[count:]
        gather_parts(me_ref[0], name, refs[:count], recv_ref)
    tables = (up_row_ref, up_col_ref, up_couple_ref)
    send(msg_ref, stack(pair_group(name, me_ref, recv_ref, tables, nodes_ref, None)))


def top_levels(recv_ref, up_row_ref, up_col_ref, up_couple_ref, gram_ref):
    first, second, _, total, energy = rescale(recv_ref)
    gained = couple_all(first, (pair_at(up_couple_ref, 6, 0), pair_at(up_couple_ref, 6, 1)))
    first = climb(first, pair_at(up_col_ref, 6))
    potential = couple_all(first, (pair_at(up_couple_ref, 7, 0), pair_at(up_couple_ref, 7, 1)))
    below = descend(potential, pair_at(up_row_ref, 6))
    potential = [a + b for a, b in zip(gained, below)]
    cross = jnp.zeros((RHS, RANK), f32)
    summed = []
    for d in range(recv_ref.shape[0]):
        moved = mm(potential[d], pair_at(gram_ref, d))
        cross = cross + potential[d] * (2.0 * second[d] + moved)
        summed.append(second[d] + moved)
    energy = column_of(energy) + jnp.sum(cross, axis=1, keepdims=True)
    return potential, summed, column_of(total), energy


def middle_kernel(
    me_ref,
    rows_ref,
    part0_ref,
    part1_ref,
    part2_ref,
    part3_ref,
    core_path_ref,
    core_own_ref,
    row_path_ref,
    row_own_ref,
    mid_path_ref,
    mid_own_ref,
    near_gain_ref,
    mid_gain_ref,
    up_row_ref,
    up_col_ref,
    up_couple_ref,
    core_nodes_ref,
    row_nodes_ref,
    mid_nodes_ref,
    dense_ref,
    row_basis_ref,
    col_basis_ref,
    local_row_ref,
    local_col_ref,
    local_couple_ref,
    x_ref,
    own_in_ref,
    inner_ref,
    v_ref,
    next_ref,
    alpha_ref,
    rho_ref,
    msg_ref,
    top_gram_ref,
    a_ref,
    b_ref,
    recv_ref,
):
    me = me_ref[0]
    gather_parts(me, "far", (part0_ref, part1_ref, part2_ref, part3_ref), recv_ref)
    place = place_of(me, "far")
    base = 2 * RHS + 8
    for d in range(recv_ref.shape[0]):
        gram = unpack(recv_ref[d, base : base + HALF], recv_ref[d, base + HALF : base + HALF + 1])
        store_pair(top_gram_ref, d, gram)
    potential, summed, squares, energy = top_levels(
        recv_ref, up_row_ref, up_col_ref, up_couple_ref, top_gram_ref
    )
    alpha = jnp.sqrt(squares)
    rho = jnp.sqrt(energy)
    alpha_ref[...] = jnp.broadcast_to(alpha, (RHS, RANK))
    rho_ref[...] = jnp.broadcast_to(rho, (RHS, RANK))
    scale = inverse_norm(squares)
    for d in range(recv_ref.shape[0]):
        a_ref[d] = potential[d]
        b_ref[d] = summed[d]
    forward = a_ref[place]
    siblings = {6: b_ref[place ^ 1]}
    for k, value in enumerate(climb(summed, pair_at(up_row_ref, 6))):
        a_ref[4 + k] = value
    siblings[7] = a_ref[4 + ((place >> 1) ^ 1)]
    for name, path_ref, part_ref, nodes_ref in (
        ("mid", mid_path_ref, mid_own_ref, mid_nodes_ref),
        ("row", row_path_ref, row_own_ref, row_nodes_ref),
        ("core", core_path_ref, core_own_ref, core_nodes_ref),
    ):
        level, heights, _ = stage(name)
        factor = scale / inverse_norm(column_of(part_ref[:1]))
        inside = place_of(me, name)
        for height in reversed(range(heights)):
            j = level + height
            child = (me >> j) & 1
            spread = mm(forward, pair_at(up_row_ref, j), transposed=True)
            low = spread[:, :RANK]
            high = spread[:, RANK:]
            forward = path_ref[3 * height] * factor + jnp.where(child == 0, low, high)
            other = path_ref[3 * height + 1] * factor + jnp.where(child == 0, high, low)
            gram = pair_at(nodes_ref, bases(name)[height] + ((inside >> height) ^ 1))
            siblings[j] = path_ref[3 * height + 2] * factor + mm(other, gram)
    backward = from_siblings([siblings[j] for j in range(8)], near_gain_ref, mid_gain_ref)
    local = readers(
        (dense_ref, row_basis_ref, col_basis_ref, local_row_ref, local_col_ref, local_couple_ref)
    )
    dense, row_basis, col_basis, local_row, local_col, coupling = local
    own_factor = scale / inverse_norm(column_of(own_in_ref[:1]))
    outer = local_down(forward, None, None, coupling, local_row, False)
    images = []
    for q in range(LEAF_DEV):
        y = mm(outer[q], row_basis(q), transposed=True) * live_mask(rows_ref, q)
        images.append(y + inner_ref[:, row_part(q)] * own_factor)
    leaf, node = local_up(images, row_basis, local_row)
    down = local_down(backward, leaf, node, coupling, local_col, True)
    inverse = 1.0 / rho
    parts = []
    for q in range(LEAF_DEV):
        v = x_ref[:, col_part(q)] * scale
        v_ref[:, col_part(q)] = v
        x = mm(images[q], dense(q)) + mm(down[q], col_basis(q), transposed=True)
        x = x * inverse - rho * v
        next_ref[:, col_part(q)] = x
        parts.append(x)
    pair_up(parts, local, rows_ref, msg_ref, None, None, [])


def final_kernel(
    me_ref,
    part0_ref,
    part1_ref,
    part2_ref,
    part3_ref,
    up_row_ref,
    up_col_ref,
    up_couple_ref,
    top_gram_ref,
    beta_ref,
    alpha_ref,
    rho_ref,
    v_ref,
    x_ref,
    out_ref,
    recv_ref,
):
    gather_parts(me_ref[0], "far", (part0_ref, part1_ref, part2_ref, part3_ref), recv_ref)
    _, _, squares, energy = top_levels(
        recv_ref, up_row_ref, up_col_ref, up_couple_ref, top_gram_ref
    )
    theta = jnp.sqrt(squares)
    rho2 = jnp.sqrt(energy - squares)
    rho = rho_ref[:, :1]
    phi = alpha_ref[:, :1] / rho * beta_ref[:, :1]
    v = v_ref[...]
    search = x_ref[...] * inverse_norm(squares) - (theta / rho) * v
    out_ref[...] = (phi / rho) * v - (phi * (theta / rho2) / rho2) * search


def call(kernel, outs, operands, scratch=(), far=(), limit=VMEM_LIMIT):
    spaces = []
    for index, operand in enumerate(operands):
        space = pltpu.SMEM if operand.dtype == jnp.int32 else pltpu.VMEM
        spaces.append(pl.ANY if index in far else space)
    outs = [shape if isinstance(shape, jax.ShapeDtypeStruct) else jax.ShapeDtypeStruct(shape, f32) for shape in outs]
    return pl.pallas_call(
        kernel,
        out_shape=outs,
        in_specs=[pl.BlockSpec(memory_space=space) for space in spaces],
        out_specs=[pl.BlockSpec(memory_space=pltpu.VMEM)] * len(outs),
        scratch_shapes=[
            pltpu.VMEM(shape, f32) if isinstance(shape, tuple) else shape for shape in scratch
        ],
        compiler_params=pltpu.CompilerParams(vmem_limit_bytes=limit),
        cost_estimate=pl.CostEstimate(flops=COST_FLOPS, bytes_accessed=0, transcendentals=0),
    )(*operands)


def device_groups(devices, stride, size):
    out = []
    for base in range(devices):
        if (base // stride) % size == 0:
            out.append([base + k * stride for k in range(size)])
    return out


def local_program(
    devices,
    rhs,
    box_rows,
    dense,
    row_basis,
    col_basis,
    local_col,
    local_row,
    local_couple,
    up_col,
    up_row,
    up_couple,
):
    me = lax.axis_index("leaf").astype(jnp.int32).reshape(1)

    def swap_parts(message, name):
        level, _, count = stage(name)
        parts = [message]
        for k in range(1, count):
            pairs = [(i, i ^ (k << level)) for i in range(devices)]
            parts.append(lax.ppermute(message, "leaf", pairs))
        return parts

    def swap_mid(message):
        level, _, count = stage("mid")
        groups = device_groups(devices, 1 << level, count)
        return lax.all_to_all(message, "leaf", 0, 0, axis_index_groups=groups)

    tile = (RHS, RANK)
    row_shape = (RHS, LEAF_DEV * LEAF_ROWS)
    col_shape = (RHS, LEAF_DEV * LEAF_COLS)
    single = (RHS + 8, RANK)
    double = (2 * RHS + 8, RANK)

    def longer(shape, rows):
        return (shape[0] + rows, shape[1])

    stat = (8, RANK)
    gram_shape = (RANK, RANK)
    tables = [up_row, up_col, up_couple]

    def nodes_shape(count):
        return jax.ShapeDtypeStruct((2, count) + gram_shape, bf16)

    def path_shape(name):
        return (3 * stage(name)[1],) + tile

    def sibling_shape(name):
        return (stage(name)[1],) + tile

    def nodes_of(name):
        return nodes_shape(node_count(name))

    def node_scratch(name, count=1):
        return [(node_count(name),) + tile] * count

    def received(name, shape):
        return [(stage(name)[2],) + shape]

    groups = stage("mid")[2]

    z, message = call(
        start_kernel,
        [(RHS, KEEP + 6 * RANK), (1,) + longer(single, HALF)],
        [me, box_rows, rhs, row_basis, local_row],
        [pltpu.SMEM(box_rows.shape, jnp.int32)]
        + [k.shape for k in (rhs, row_basis, local_row)]
        + [pltpu.SemaphoreType.DMA((4,))],
        range(1, 5),
        START_LIMIT,
    )
    blocks = [dense, row_basis, col_basis, local_row, local_col, local_couple]
    message, core_sib, core_nodes = call(
        core_kernel,
        [(1,) + longer(single, HALF), sibling_shape("core"), nodes_of("core")],
        [me] + swap_parts(message, "core") + [up_row],
        received("core", longer(single, HALF)) + node_scratch("core"),
    )
    message, row_sib, row_nodes, near_gain, path = call(
        row_kernel,
        [(groups,) + longer(single, SLICE), sibling_shape("row"), nodes_of("row"), nodes_shape(3), gram_shape],
        [me] + swap_parts(message, "row") + tables,
        received("row", longer(single, HALF)) + node_scratch("row") + [(HALF, RANK)],
    )
    message, mid_sib, mid_gain, part, diagonal = call(
        mid_kernel,
        [(1,) + single, sibling_shape("mid"), nodes_shape(5), (HALF, RANK), stat],
        [me, swap_mid(message)] + tables + [path],
        node_scratch("mid"),
    )
    gains = [near_gain, mid_gain]
    x, beta, message, own, inner = call(
        first_kernel,
        [col_shape, tile, (1,) + longer(double, HALF), stat, row_shape],
        [me, box_rows]
        + swap_parts(message, "far")
        + [core_sib, row_sib, mid_sib]
        + gains
        + [part, up_row]
        + blocks
        + [z],
        [(2,) + tile] + received("far", single),
    )
    message, core_path, core_own = call(
        core_pair_kernel,
        [(1,) + longer(double, 2 * HALF), path_shape("core"), stat],
        [me] + swap_parts(message, "core") + tables + [core_nodes],
        received("core", longer(double, HALF)) + node_scratch("core", 2),
    )
    message, row_path, row_own, mid_nodes, gram = call(
        row_pair_kernel,
        [(groups,) + double, path_shape("row"), stat, nodes_of("mid"), (HALF + 8, RANK)],
        [me] + swap_parts(message, "row") + tables + [row_nodes, diagonal],
        received("row", longer(double, 2 * HALF)) + node_scratch("row", 2),
    )
    message, mid_path, mid_own = call(
        mid_pair_kernel,
        [(1,) + longer(double, HALF + 8), path_shape("mid"), stat],
        [me, swap_mid(message)] + tables + [mid_nodes, gram],
        node_scratch("mid", 2),
    )
    v, x, alpha, rho, message, top_nodes = call(
        middle_kernel,
        [col_shape, col_shape, tile, tile, (1,) + double, nodes_shape(4)],
        [me, box_rows]
        + swap_parts(message, "far")
        + [core_path, core_own, row_path, row_own, mid_path, mid_own]
        + gains
        + tables
        + [core_nodes, row_nodes, mid_nodes]
        + blocks
        + [x, own, inner],
        [(6,) + tile, (4,) + tile] + received("far", longer(double, HALF + 8)),
    )
    for name, nodes, peers in (
        ("core", core_nodes, 1),
        ("row", row_nodes, groups),
        ("mid", mid_nodes, 1),
    ):
        parts = [swap_mid(message)] if name == "mid" else swap_parts(message, name)
        (message,) = call(
            functools.partial(last_pair_kernel, name),
            [(peers,) + double],
            [me] + parts + tables + [nodes],
            [] if name == "mid" else received(name, double),
        )
    (out,) = call(
        final_kernel,
        [col_shape],
        [me] + swap_parts(message, "far") + tables + [top_nodes, beta, alpha, rho, v, x],
        received("far", double),
    )
    return out


def solution(mesh):
    devices = mesh.shape["leaf"]
    return jax.shard_map(
        functools.partial(local_program, devices),
        mesh=mesh,
        in_specs=(
            P(None, "leaf"),
            P("leaf"),
            P("leaf", None, None),
            P("leaf", None, None),
            P("leaf", None, None),
            P("leaf", None, None),
            P("leaf", None, None),
            P("leaf", None, None, None),
            P(),
            P(),
            P(),
        ),
        out_specs=P(None, "leaf"),
        check_vma=False,
    )
```

```python
import functools

import jax
import jax.numpy as jnp
from jax import lax
from jax.experimental import pallas as pl
from jax.experimental.pallas import tpu as pltpu
from jax.sharding import PartitionSpec as P

RHS = 16
RANK = 128
LEAF_DEV = 4
LEAF_ROWS = 512
LEAF_COLS = 256
HALF = RANK // 2
SLICE = 8
COST_FLOPS = 6000000000
TINY = 1.2e-38
ORDER = (0, 1, 3, 2)
NEAR = 8
STAGES = {"core": (0, 1), "row": (1, 2), "mid": (3, 3), "far": (6, 2)}
VMEM_MIB = 24
VMEM_LIMIT = VMEM_MIB * 1024 * 1024
START_LIMIT = 60 * 1024 * 1024

f32 = jnp.float32
bf16 = jnp.bfloat16


def split(v):
    head = v.astype(bf16)
    return head, (v - head.astype(f32)).astype(bf16)


def mm(x, pair, transposed=False):
    xh, xl = split(x)
    wh, wl = pair
    dims = (((1,), (1 if transposed else 0,)), ((), ()))
    n = x.shape[0]
    both = lax.dot_general(jnp.concatenate([xh, xl], 0), wh, dims, preferred_element_type=f32)
    rest = lax.dot_general(xh, wl, dims, preferred_element_type=f32)
    return both[:n] + (both[n:] + rest)


def mm_inner(a, b):
    ah, al = split(a)
    bh, bl = split(b)
    dims = (((0,), (0,)), ((), ()))
    m = a.shape[1]
    both = lax.dot_general(jnp.concatenate([ah, al], 1), bh, dims, preferred_element_type=f32)
    rest = lax.dot_general(ah, bl, dims, preferred_element_type=f32)
    return both[:m] + (both[m:] + rest)


def gram_of(a):
    high, low = split(a)
    dims = (((0,), (0,)), ((), ()))
    rest = lax.dot_general(high, low, dims, preferred_element_type=f32)
    return lax.dot_general(high, high, dims, preferred_element_type=f32) + (rest + jnp.transpose(rest))


def pair_at(ref, *index):
    if ref.dtype == bf16:
        return ref[(0,) + index], ref[(1,) + index]
    return split(ref[index])


def half_of(ref, j, child):
    return pair_at(ref, j, pl.ds(pl.multiple_of(child * RANK, RANK), RANK))


def eye():
    return (
        lax.broadcasted_iota(jnp.int32, (RHS, RANK), 0)
        == lax.broadcasted_iota(jnp.int32, (RHS, RANK), 1)
    ).astype(f32)


def stat_block(*values):
    rows = lax.broadcasted_iota(jnp.int32, (8, RANK), 0)
    block = jnp.where(rows == 0, values[0], 0.0)
    for k in range(1, len(values)):
        block = jnp.where(rows == k, values[k], block)
    return block


def column_of(row):
    return jnp.sum(row * eye(), axis=1, keepdims=True)


def row_of(column):
    return jnp.sum(column * eye(), axis=0, keepdims=True)


def inverse_norm(squares):
    return jnp.where(squares >= TINY, 1.0 / jnp.sqrt(squares), 1.0)


def sum_squares(v):
    return jnp.sum(v * v, axis=1, keepdims=True)


def send(out_ref, value):
    for peer in range(out_ref.shape[0]):
        out_ref[peer] = value


def stack(blocks):
    return jnp.concatenate(blocks, 0)


def unstack(value, count):
    size = value.shape[0] // count
    return [value[k * size : (k + 1) * size] for k in range(count)]


def climb(blocks, transfer):
    count = len(blocks) // 2
    paired = [jnp.concatenate([blocks[2 * m], blocks[2 * m + 1]], 1) for m in range(count)]
    return unstack(mm(stack(paired), transfer), count)


def descend(blocks, transfer):
    spread = unstack(mm(stack(blocks), transfer, transposed=True), len(blocks))
    out = []
    for block in spread:
        out += [block[:, :RANK], block[:, RANK:]]
    return out


def couple_all(blocks, coupling):
    count = len(blocks) // 2
    even = unstack(mm(stack(blocks[1::2]), coupling[0]), count)
    odd = unstack(mm(stack(blocks[0::2]), coupling[1]), count)
    out = []
    for m in range(count):
        out += [even[m], odd[m]]
    return out


def lanes(value, k):
    return value[:, k * RANK : (k + 1) * RANK]


def live_mask(rows_ref, q):
    slots = lax.broadcasted_iota(jnp.int32, (RHS, LEAF_ROWS), 1)
    return (slots < rows_ref[q]).astype(f32)


def row_part(q):
    return slice(q * LEAF_ROWS, (q + 1) * LEAF_ROWS)


def col_part(q):
    return slice(q * LEAF_COLS, (q + 1) * LEAF_COLS)


def pair_up(parts, local, rows_ref, msg_ref, own_ref, inner_ref, extra):
    dense_ref, row_basis_ref, col_basis_ref, cross_ref, columns_ref, paths_ref, images_ref = local
    squares = sum_squares(parts[0])
    for part in parts[1:]:
        squares = squares + sum_squares(part)
    scale = inverse_norm(squares)
    whole = jnp.concatenate(parts, 1)
    root = mm(whole, pair_at(columns_ref)) * scale
    leaf = [mm(parts[q], pair_at(col_basis_ref, q)) for q in range(LEAF_DEV)]
    down = mm(jnp.concatenate(leaf, 1), pair_at(cross_ref))
    energy = jnp.zeros((RHS, 1), f32)
    rows = []
    for q in range(LEAF_DEV):
        y = mm(parts[q], pair_at(dense_ref, q), transposed=True)
        y = y + mm(lanes(down, q), pair_at(row_basis_ref, q), transposed=True)
        y = y * (live_mask(rows_ref, q) * scale)
        if inner_ref is not None:
            inner_ref[:, row_part(q)] = y
        energy = energy + sum_squares(y)
        if images_ref is None:
            rows.append(mm(y, pair_at(row_basis_ref, q)))
    if images_ref is None:
        row_root = mm(jnp.concatenate(rows, 1), pair_at(paths_ref))
    else:
        row_root = mm(whole * scale, pair_at(images_ref), transposed=True)
    stats = stat_block(row_of(squares), row_of(energy))
    if own_ref is not None:
        own_ref[...] = stats
    send(msg_ref, stack([root, row_root, stats] + extra))


def paths_kernel(
    order_ref,
    col_basis_ref,
    local_row_ref,
    local_col_ref,
    local_couple_ref,
    cross_ref,
    columns_ref,
    paths_ref,
):
    del order_ref
    halves = [slice(0, RANK), slice(RANK, 2 * RANK)]

    def store(ref, index, value):
        high, low = split(value)
        ref[(0,) + index] = high
        ref[(1,) + index] = low

    def part(q, size=RANK):
        return slice(q * size, (q + 1) * size)

    for q in range(LEAF_DEV):
        m, i = q // 2, q % 2
        store(cross_ref, (part(q), part(q)), jnp.zeros((RANK, RANK), f32))
        store(cross_ref, (part(q), part(q ^ 1)), local_couple_ref[m, 1 - i])
        gained = mm(local_col_ref[m, halves[i]], pair_at(local_couple_ref, 2, 1 - m))
        spread = mm(gained, pair_at(local_row_ref, 1 - m), transposed=True)
        store(cross_ref, (part(q), slice(2 * (1 - m) * RANK, 2 * (2 - m) * RANK)), spread)
        store(paths_ref, (part(q),), mm(local_row_ref[m, halves[i]], split(local_row_ref[2, halves[m]])))
        path = mm(local_col_ref[m, halves[i]], split(local_col_ref[2, halves[m]]))
        store(columns_ref, (part(q, LEAF_COLS),), mm(col_basis_ref[q], split(path)))


def images_kernel(
    order_ref, rows_ref, dense_ref, row_basis_ref, col_basis_ref, cross_ref, paths_ref, images_ref
):
    del order_ref
    turned = []
    images = []
    moved = []
    for q in range(LEAF_DEV):
        path = pair_at(paths_ref, slice(q * RANK, (q + 1) * RANK))
        turned.append(jnp.transpose(path[0].astype(f32) + path[1].astype(f32)))
        slots = lax.broadcasted_iota(jnp.int32, (LEAF_ROWS, RANK), 0)
        basis = jnp.where(slots < rows_ref[q], row_basis_ref[q], 0.0)
        images.append(mm_inner(basis, dense_ref[q]))
        moved.append(mm(turned[q], split(gram_of(basis))))
    inner = mm(jnp.concatenate(moved, 1), pair_at(cross_ref), transposed=True)
    for q in range(LEAF_DEV):
        image = mm(turned[q], split(images[q]))
        image = image + mm(lanes(inner, q), pair_at(col_basis_ref, q), transposed=True)
        high, low = split(image)
        images_ref[0, :, col_part(q)] = high
        images_ref[1, :, col_part(q)] = low


def inner_kernel(order_ref, y_ref, dense_ref, row_basis_ref, col_basis_ref, cross_ref, x_ref):
    del order_ref
    leaf = [mm(y_ref[:, row_part(q)], pair_at(row_basis_ref, q)) for q in range(LEAF_DEV)]
    down = mm(jnp.concatenate(leaf, 1), pair_at(cross_ref), transposed=True)
    for q in range(LEAF_DEV):
        x = mm(y_ref[:, row_part(q)], pair_at(dense_ref, q))
        x_ref[:, col_part(q)] = x + mm(lanes(down, q), pair_at(col_basis_ref, q), transposed=True)


def both_sides(grams, half):
    full = half[0].astype(f32) + half[1].astype(f32)
    left = mm(jnp.transpose(full), split(jnp.concatenate(grams, 1)))
    columns = [left[:, k * RANK : (k + 1) * RANK] for k in range(len(grams))]
    return unstack(mm(stack(columns), half), len(grams))


def gram_climb(grams, transfer):
    even = both_sides(grams[0::2], (transfer[0][:RANK], transfer[1][:RANK]))
    odd = both_sides(grams[1::2], (transfer[0][RANK:], transfer[1][RANK:]))
    return [a + b for a, b in zip(even, odd)]


def pack(gram):
    row = lax.broadcasted_iota(jnp.int32, (HALF, RANK), 0)
    col = lax.broadcasted_iota(jnp.int32, (HALF, RANK), 1)
    last = gram[HALF:]
    top = jnp.where((col < HALF) & (col > row), pltpu.roll(last, HALF, 1), gram[:HALF])
    diagonal = jnp.sum(jnp.where(col - HALF == row, last, 0.0), axis=0, keepdims=True)
    return top, diagonal


def unpack(top, diagonal):
    row = lax.broadcasted_iota(jnp.int32, (HALF, RANK), 0)
    col = lax.broadcasted_iota(jnp.int32, (HALF, RANK), 1)
    upper = jnp.where((col >= HALF) | (col < row), top, jnp.where(col == row, 0.5 * top, 0.0))
    lower = jnp.where(
        col - HALF > row,
        pltpu.roll(top, HALF, 1),
        jnp.where(col - HALF == row, 0.5 * diagonal, 0.0),
    )
    part = stack([upper, lower])
    return part + jnp.transpose(part)


def stage(name):
    level, heights = STAGES[name]
    return level, heights, 1 << heights


def place_of(me, name):
    level, _, count = stage(name)
    return (me >> level) % count


def bases(name):
    _, heights, count = stage(name)
    return [sum(count >> k for k in range(height)) for height in range(heights)]


def node_count(name):
    return 2 * stage(name)[2] - 2


def gather_parts(me, name, parts, out_ref):
    for k, part in zip(ORDER, parts):
        out_ref[place_of(me, name) ^ k] = part[0]


def store_pair(ref, index, value):
    high, low = split(value)
    ref[0, index] = high
    ref[1, index] = low


def group_grams(name, grams, up_row_ref, nodes_ref):
    for height, base in enumerate(bases(name)):
        for k, value in enumerate(grams):
            store_pair(nodes_ref, base + k, value)
        grams = gram_climb(grams, pair_at(up_row_ref, stage(name)[0] + height))
    return grams[0]


def start_copies(pairs, sems):
    copies = [
        pltpu.make_async_copy(source, target, sems.at[k])
        for k, (source, target) in enumerate(pairs)
    ]
    for copy in copies:
        copy.start()
    return copies


def start_kernel(
    me_ref,
    rows_hbm,
    rhs_hbm,
    row_basis_hbm,
    local_row_hbm,
    z_ref,
    msg_ref,
    rows_ref,
    rhs_ref,
    row_basis_ref,
    local_row_ref,
    sems,
):
    pairs = [(rows_hbm, rows_ref), (rhs_hbm, rhs_ref)]
    pairs += [(row_basis_hbm, row_basis_ref), (local_row_hbm, local_row_ref)]
    for copy in start_copies(pairs, sems):
        copy.wait()
    squares = jnp.zeros((RHS, 1), f32)
    paths = []
    for q in range(LEAF_DEV):
        m, i = q // 2, q % 2
        top = split(local_row_ref[2, m * RANK : (m + 1) * RANK])
        paths.append(mm(local_row_ref[m, i * RANK : (i + 1) * RANK], top))
    leaf = []
    grams = []
    for q in range(LEAF_DEV):
        part = rhs_ref[:, row_part(q)] * live_mask(rows_ref, q)
        z_ref[:, row_part(q)] = part
        squares = squares + sum_squares(part)
        leaf.append(mm(part, split(row_basis_ref[q])))
    for q in range(LEAF_DEV):
        slots = lax.broadcasted_iota(jnp.int32, (LEAF_ROWS, RANK), 0)
        basis = jnp.where(slots < rows_ref[q], row_basis_ref[q], 0.0)
        grams.append(gram_of(basis))
    root = mm(jnp.concatenate(leaf, 1), split(stack(paths)))
    row = row_of(squares)
    left = [mm(jnp.transpose(paths[q]), split(grams[q])) for q in range(LEAF_DEV)]
    gram = mm(jnp.concatenate(left, 1), split(stack(paths)))
    top, diagonal = pack(gram)
    send(msg_ref, stack([root, stat_block(row, row, diagonal), top]))


def sum_stats(recv_ref):
    stats = recv_ref[0, RHS : RHS + 8]
    for d in range(1, recv_ref.shape[0]):
        stats = stats + recv_ref[d, RHS : RHS + 8]
    return stats


def climb_group(name, me_ref, recv_ref, climb_ref, sib_ref, scratch_ref):
    level = stage(name)[0]
    place = place_of(me_ref[0], name)
    summaries = [recv_ref[d, :RHS] for d in range(recv_ref.shape[0])]
    for height, base in enumerate(bases(name)):
        for m, value in enumerate(summaries):
            scratch_ref[base + m] = value
        sib_ref[height] = scratch_ref[base + ((place >> height) ^ 1)]
        summaries = climb(summaries, pair_at(climb_ref, level + height))
    return summaries[0]


def received_grams(recv_ref):
    base = RHS + 8
    count = recv_ref.shape[0]
    return [unpack(recv_ref[d, base:], recv_ref[d, RHS + 2 : RHS + 3]) for d in range(count)]


def path_product(me, level, path, up_col_ref):
    half = half_of(up_col_ref, level, (me >> level) & 1)
    return mm(path, half)


def sibling_gain(me, level, path, up_couple_ref):
    child = 1 - ((me >> level) & 1)
    return mm(path, pair_at(up_couple_ref, level, child))


def core_kernel(
    me_ref,
    part0_ref,
    part1_ref,
    up_row_ref,
    msg_ref,
    sib_ref,
    nodes_ref,
    recv_ref,
    scratch_ref,
):
    gather_parts(me_ref[0], "core", (part0_ref, part1_ref), recv_ref)
    summary = climb_group("core", me_ref, recv_ref, up_row_ref, sib_ref, scratch_ref)
    top, diagonal = pack(group_grams("core", received_grams(recv_ref), up_row_ref, nodes_ref))
    stats = sum_stats(recv_ref)
    send(msg_ref, stack([summary, stat_block(stats[:1], stats[1:2], diagonal), top]))


def row_kernel(
    me_ref,
    order_ref,
    part0_ref,
    part1_ref,
    part2_ref,
    part3_ref,
    up_row_ref,
    up_col_ref,
    up_couple_ref,
    msg_ref,
    sib_ref,
    nodes_ref,
    gain_ref,
    path_ref,
    recv_ref,
    scratch_ref,
    slice_ref,
):
    del order_ref
    me = me_ref[0]
    gather_parts(me, "row", (part0_ref, part1_ref, part2_ref, part3_ref), recv_ref)
    summary = climb_group("row", me_ref, recv_ref, up_row_ref, sib_ref, scratch_ref)
    gram = group_grams("row", received_grams(recv_ref), up_row_ref, nodes_ref)
    child = 1 - (me & 1)
    store_pair(gain_ref, 0, up_couple_ref[0, child])
    path = up_col_ref[0, pl.ds(pl.multiple_of((me & 1) * RANK, RANK), RANK), :]
    for j in range(1, 3):
        store_pair(gain_ref, j, sibling_gain(me, j, path, up_couple_ref))
        path = path_product(me, j, path, up_col_ref)
    path_ref[...] = path
    top, diagonal = pack(gram)
    slice_ref[...] = top
    part = slice_ref[pl.ds(pl.multiple_of((me % NEAR) * SLICE, SLICE), SLICE), :]
    stats = sum_stats(recv_ref)
    send(msg_ref, stack([summary, stat_block(stats[:1], stats[1:2], diagonal), part]))


def mid_kernel(
    me_ref,
    recv_ref,
    up_row_ref,
    msg_ref,
    sib_ref,
    part_ref,
    diagonal_ref,
    scratch_ref,
):
    count = stage("mid")[2]
    summary = climb_group("mid", me_ref, recv_ref, up_row_ref, sib_ref, scratch_ref)
    for d in range(count):
        part_ref[d * SLICE : (d + 1) * SLICE] = recv_ref[d, RHS + 8 :]
        diagonal_ref[d : d + 1] = recv_ref[d, RHS + 2 : RHS + 3]
    send(msg_ref, stack([summary, sum_stats(recv_ref)]))


def gains_kernel(me_ref, order_ref, up_col_ref, up_couple_ref, path_ref, gain_ref):
    del order_ref
    me = me_ref[0]
    path = path_ref[...]
    for k, j in enumerate(range(stage("mid")[0], 8)):
        store_pair(gain_ref, k, sibling_gain(me, j, path, up_couple_ref))
        if j < 7:
            path = path_product(me, j, path, up_col_ref)


def from_siblings(siblings, near_gain_ref, mid_gain_ref):
    gains = [pair_at(near_gain_ref, j) for j in range(3)]
    gains += [pair_at(mid_gain_ref, j) for j in range(5)]
    gains = tuple(jnp.concatenate([g[k] for g in gains], 1) for k in range(2))
    return mm(jnp.concatenate(siblings, 1), gains, transposed=True)


def first_kernel(
    me_ref,
    rows_ref,
    part0_ref,
    part1_ref,
    part2_ref,
    part3_ref,
    core_sib_ref,
    row_sib_ref,
    mid_sib_ref,
    near_gain_ref,
    mid_gain_ref,
    part_ref,
    up_row_ref,
    dense_ref,
    row_basis_ref,
    col_basis_ref,
    cross_ref,
    columns_ref,
    paths_ref,
    within_ref,
    x_ref,
    beta_ref,
    msg_ref,
    own_ref,
    inner_ref,
    scratch_ref,
    recv_ref,
):
    me = me_ref[0]
    gather_parts(me, "far", (part0_ref, part1_ref, part2_ref, part3_ref), recv_ref)
    place = place_of(me, "far")
    summaries = [recv_ref[d, :RHS] for d in range(recv_ref.shape[0])]
    siblings = [core_sib_ref[0]] + [row_sib_ref[j] for j in range(2)] + [mid_sib_ref[j] for j in range(3)]
    siblings.append(recv_ref[place ^ 1, :RHS])
    summaries = climb(summaries, pair_at(up_row_ref, 6))
    for m, value in enumerate(summaries):
        scratch_ref[m] = value
    siblings.append(scratch_ref[(place >> 1) ^ 1])
    potential = from_siblings(siblings, near_gain_ref, mid_gain_ref)
    beta = jnp.sqrt(column_of(sum_stats(recv_ref)[:1]))
    inverse = 1.0 / beta
    beta_ref[...] = jnp.broadcast_to(beta, (RHS, RANK))
    spread = mm(potential, pair_at(columns_ref), transposed=True)
    parts = []
    for q in range(LEAF_DEV):
        x = (within_ref[:, col_part(q)] + spread[:, col_part(q)]) * inverse
        x_ref[:, col_part(q)] = x
        parts.append(x)
    local = (dense_ref, row_basis_ref, col_basis_ref, cross_ref, columns_ref, paths_ref, None)
    pair_up(parts, local, rows_ref, msg_ref, own_ref, inner_ref, [part_ref[...]])


def rescale(recv_ref):
    base = 2 * RHS
    squares = stack([recv_ref[d, base : base + 1] for d in range(recv_ref.shape[0])])
    energy = stack([recv_ref[d, base + 1 : base + 2] for d in range(recv_ref.shape[0])])
    total = jnp.sum(squares, axis=0, keepdims=True)
    factor = inverse_norm(total) / inverse_norm(squares)
    energy = jnp.sum(energy * factor * factor, axis=0, keepdims=True)
    first = []
    second = []
    for d in range(recv_ref.shape[0]):
        column = column_of(factor[d : d + 1])
        first.append(recv_ref[d, :RHS] * column)
        second.append(recv_ref[d, RHS : 2 * RHS] * column)
    return first, second, factor, total, energy


def pair_group(name, me_ref, recv_ref, tables, nodes_ref, keep):
    up_row_ref, up_col_ref, up_couple_ref = tables
    level = stage(name)[0]
    place = place_of(me_ref[0], name)
    first, second, _, total, energy = rescale(recv_ref)
    cross = jnp.zeros((RHS, RANK), f32)
    for height, base in enumerate(bases(name)):
        j = level + height
        gained = couple_all(first, (pair_at(up_couple_ref, j, 0), pair_at(up_couple_ref, j, 1)))
        summed = []
        for k in range(len(first)):
            moved = mm(gained[k], pair_at(nodes_ref, base + k))
            cross = cross + gained[k] * (2.0 * second[k] + moved)
            summed.append(second[k] + moved)
        if keep is not None:
            path_ref, gain_ref, below_ref = keep
            for k in range(len(first)):
                gain_ref[base + k] = gained[k]
                below_ref[base + k] = second[k]
            own = base + (place >> height)
            other = base + ((place >> height) ^ 1)
            path_ref[3 * height] = gain_ref[own]
            path_ref[3 * height + 1] = gain_ref[other]
            path_ref[3 * height + 2] = below_ref[other]
        first = climb(first, pair_at(up_col_ref, j))
        second = climb(summed, pair_at(up_row_ref, j))
    energy = energy + row_of(jnp.sum(cross, axis=1, keepdims=True))
    return first[0], second[0], stat_block(total, energy)


def core_pair_kernel(
    me_ref,
    part0_ref,
    part1_ref,
    up_row_ref,
    up_col_ref,
    up_couple_ref,
    nodes_ref,
    msg_ref,
    path_ref,
    own_ref,
    recv_ref,
    gain_ref,
    below_ref,
):
    gather_parts(me_ref[0], "core", (part0_ref, part1_ref), recv_ref)
    tables = (up_row_ref, up_col_ref, up_couple_ref)
    keep = (path_ref, gain_ref, below_ref)
    first, second, stats = pair_group("core", me_ref, recv_ref, tables, nodes_ref, keep)
    own_ref[...] = stats
    base = 2 * RHS + 8
    send(msg_ref, stack([first, second, stats, recv_ref[0, base:], recv_ref[1, base:]]))


def row_pair_kernel(
    me_ref,
    order_ref,
    part0_ref,
    part1_ref,
    part2_ref,
    part3_ref,
    up_row_ref,
    up_col_ref,
    up_couple_ref,
    nodes_ref,
    diagonal_ref,
    msg_ref,
    path_ref,
    own_ref,
    mid_nodes_ref,
    gram_ref,
    recv_ref,
    gain_ref,
    below_ref,
):
    del order_ref
    gather_parts(me_ref[0], "row", (part0_ref, part1_ref, part2_ref, part3_ref), recv_ref)
    tables = (up_row_ref, up_col_ref, up_couple_ref)
    keep = (path_ref, gain_ref, below_ref)
    first, second, stats = pair_group("row", me_ref, recv_ref, tables, nodes_ref, keep)
    own_ref[...] = stats
    send(msg_ref, stack([first, second, stats]))
    base = 2 * RHS + 8
    grams = []
    for d in range(stage("mid")[2]):
        slices = []
        for p in range(NEAR):
            low = base + (p % 2) * HALF + d * SLICE
            slices.append(recv_ref[p // 2, low : low + SLICE])
        grams.append(unpack(stack(slices), diagonal_ref[d : d + 1]))
    top, diagonal = pack(group_grams("mid", grams, up_row_ref, mid_nodes_ref))
    gram_ref[...] = stack([top, stat_block(diagonal)])


def mid_pair_kernel(
    me_ref,
    recv_ref,
    up_row_ref,
    up_col_ref,
    up_couple_ref,
    nodes_ref,
    gram_ref,
    msg_ref,
    path_ref,
    own_ref,
    gain_ref,
    below_ref,
):
    tables = (up_row_ref, up_col_ref, up_couple_ref)
    keep = (path_ref, gain_ref, below_ref)
    first, second, stats = pair_group("mid", me_ref, recv_ref, tables, nodes_ref, keep)
    own_ref[...] = stats
    send(msg_ref, stack([first, second, stats, gram_ref[...]]))


def last_pair_kernel(name, me_ref, *refs):
    if name == "mid":
        recv_ref, up_row_ref, up_col_ref, up_couple_ref, nodes_ref, msg_ref = refs
    else:
        count = stage(name)[2]
        up_row_ref, up_col_ref, up_couple_ref, nodes_ref, msg_ref, recv_ref = refs[count:]
        gather_parts(me_ref[0], name, refs[:count], recv_ref)
    tables = (up_row_ref, up_col_ref, up_couple_ref)
    send(msg_ref, stack(pair_group(name, me_ref, recv_ref, tables, nodes_ref, None)))


def top_levels(recv_ref, up_row_ref, up_col_ref, up_couple_ref, gram_ref):
    first, second, _, total, energy = rescale(recv_ref)
    gained = couple_all(first, (pair_at(up_couple_ref, 6, 0), pair_at(up_couple_ref, 6, 1)))
    first = climb(first, pair_at(up_col_ref, 6))
    potential = couple_all(first, (pair_at(up_couple_ref, 7, 0), pair_at(up_couple_ref, 7, 1)))
    below = descend(potential, pair_at(up_row_ref, 6))
    potential = [a + b for a, b in zip(gained, below)]
    cross = jnp.zeros((RHS, RANK), f32)
    summed = []
    for d in range(recv_ref.shape[0]):
        moved = mm(potential[d], pair_at(gram_ref, d))
        cross = cross + potential[d] * (2.0 * second[d] + moved)
        summed.append(second[d] + moved)
    energy = column_of(energy) + jnp.sum(cross, axis=1, keepdims=True)
    return potential, summed, column_of(total), energy


def middle_kernel(
    me_ref,
    rows_ref,
    part0_ref,
    part1_ref,
    part2_ref,
    part3_ref,
    core_path_ref,
    core_own_ref,
    row_path_ref,
    row_own_ref,
    mid_path_ref,
    mid_own_ref,
    near_gain_ref,
    mid_gain_ref,
    up_row_ref,
    up_col_ref,
    up_couple_ref,
    core_nodes_ref,
    row_nodes_ref,
    mid_nodes_ref,
    dense_ref,
    row_basis_ref,
    col_basis_ref,
    cross_ref,
    columns_ref,
    images_ref,
    x_ref,
    own_in_ref,
    within_ref,
    v_ref,
    next_ref,
    alpha_ref,
    rho_ref,
    msg_ref,
    top_gram_ref,
    a_ref,
    b_ref,
    recv_ref,
):
    me = me_ref[0]
    gather_parts(me, "far", (part0_ref, part1_ref, part2_ref, part3_ref), recv_ref)
    place = place_of(me, "far")
    base = 2 * RHS + 8
    for d in range(recv_ref.shape[0]):
        gram = unpack(recv_ref[d, base : base + HALF], recv_ref[d, base + HALF : base + HALF + 1])
        store_pair(top_gram_ref, d, gram)
    potential, summed, squares, energy = top_levels(
        recv_ref, up_row_ref, up_col_ref, up_couple_ref, top_gram_ref
    )
    alpha = jnp.sqrt(squares)
    rho = jnp.sqrt(energy)
    alpha_ref[...] = jnp.broadcast_to(alpha, (RHS, RANK))
    rho_ref[...] = jnp.broadcast_to(rho, (RHS, RANK))
    scale = inverse_norm(squares)
    for d in range(recv_ref.shape[0]):
        a_ref[d] = potential[d]
        b_ref[d] = summed[d]
    forward = a_ref[place]
    siblings = {6: b_ref[place ^ 1]}
    for k, value in enumerate(climb(summed, pair_at(up_row_ref, 6))):
        a_ref[4 + k] = value
    siblings[7] = a_ref[4 + ((place >> 1) ^ 1)]
    for name, path_ref, part_ref, nodes_ref in (
        ("mid", mid_path_ref, mid_own_ref, mid_nodes_ref),
        ("row", row_path_ref, row_own_ref, row_nodes_ref),
        ("core", core_path_ref, core_own_ref, core_nodes_ref),
    ):
        level, heights, _ = stage(name)
        factor = scale / inverse_norm(column_of(part_ref[:1]))
        inside = place_of(me, name)
        for height in reversed(range(heights)):
            j = level + height
            child = (me >> j) & 1
            spread = mm(forward, pair_at(up_row_ref, j), transposed=True)
            low = spread[:, :RANK]
            high = spread[:, RANK:]
            forward = path_ref[3 * height] * factor + jnp.where(child == 0, low, high)
            other = path_ref[3 * height + 1] * factor + jnp.where(child == 0, high, low)
            gram = pair_at(nodes_ref, bases(name)[height] + ((inside >> height) ^ 1))
            siblings[j] = path_ref[3 * height + 2] * factor + mm(other, gram)
    backward = from_siblings([siblings[j] for j in range(8)], near_gain_ref, mid_gain_ref)
    own_factor = scale / inverse_norm(column_of(own_in_ref[:1]))
    inverse = 1.0 / rho
    spread = mm(backward, pair_at(columns_ref), transposed=True)
    spread = spread + mm(forward, pair_at(images_ref))
    parts = []
    for q in range(LEAF_DEV):
        v = x_ref[:, col_part(q)] * scale
        v_ref[:, col_part(q)] = v
        x = spread[:, col_part(q)] + within_ref[:, col_part(q)] * own_factor
        x = x * inverse - rho * v
        next_ref[:, col_part(q)] = x
        parts.append(x)
    local = (dense_ref, row_basis_ref, col_basis_ref, cross_ref, columns_ref, None, images_ref)
    pair_up(parts, local, rows_ref, msg_ref, None, None, [])


def final_kernel(
    me_ref,
    part0_ref,
    part1_ref,
    part2_ref,
    part3_ref,
    up_row_ref,
    up_col_ref,
    up_couple_ref,
    top_gram_ref,
    beta_ref,
    alpha_ref,
    rho_ref,
    v_ref,
    x_ref,
    out_ref,
    recv_ref,
):
    gather_parts(me_ref[0], "far", (part0_ref, part1_ref, part2_ref, part3_ref), recv_ref)
    _, _, squares, energy = top_levels(
        recv_ref, up_row_ref, up_col_ref, up_couple_ref, top_gram_ref
    )
    theta = jnp.sqrt(squares)
    rho2 = jnp.sqrt(energy - squares)
    rho = rho_ref[:, :1]
    phi = alpha_ref[:, :1] / rho * beta_ref[:, :1]
    v = v_ref[...]
    search = x_ref[...] * inverse_norm(squares) - (theta / rho) * v
    out_ref[...] = (phi / rho) * v - (phi * (theta / rho2) / rho2) * search


def call(kernel, outs, operands, scratch=(), far=(), limit=VMEM_LIMIT):
    spaces = []
    for index, operand in enumerate(operands):
        space = pltpu.SMEM if operand.dtype == jnp.int32 else pltpu.VMEM
        spaces.append(pl.ANY if index in far else space)
    outs = [shape if isinstance(shape, jax.ShapeDtypeStruct) else jax.ShapeDtypeStruct(shape, f32) for shape in outs]
    return pl.pallas_call(
        kernel,
        out_shape=outs,
        in_specs=[pl.BlockSpec(memory_space=space) for space in spaces],
        out_specs=[pl.BlockSpec(memory_space=pltpu.VMEM)] * len(outs),
        scratch_shapes=[
            pltpu.VMEM(shape, f32) if isinstance(shape, tuple) else shape for shape in scratch
        ],
        compiler_params=pltpu.CompilerParams(vmem_limit_bytes=limit),
        cost_estimate=pl.CostEstimate(flops=COST_FLOPS, bytes_accessed=0, transcendentals=0),
    )(*operands)


def device_groups(devices, stride, size):
    out = []
    for base in range(devices):
        if (base // stride) % size == 0:
            out.append([base + k * stride for k in range(size)])
    return out


def local_program(
    devices,
    rhs,
    box_rows,
    dense,
    row_basis,
    col_basis,
    local_col,
    local_row,
    local_couple,
    up_col,
    up_row,
    up_couple,
):
    me = lax.axis_index("leaf").astype(jnp.int32).reshape(1)

    def swap_parts(message, name):
        level, _, count = stage(name)
        parts = [message]
        for k in ORDER[1:count]:
            pairs = [(i, i ^ (k << level)) for i in range(devices)]
            parts.append(lax.ppermute(message, "leaf", pairs))
        return parts

    def swap_mid(message):
        level, _, count = stage("mid")
        groups = device_groups(devices, 1 << level, count)
        return lax.all_to_all(message, "leaf", 0, 0, axis_index_groups=groups)

    tile = (RHS, RANK)
    row_shape = (RHS, LEAF_DEV * LEAF_ROWS)
    col_shape = (RHS, LEAF_DEV * LEAF_COLS)
    single = (RHS + 8, RANK)
    double = (2 * RHS + 8, RANK)

    def longer(shape, rows):
        return (shape[0] + rows, shape[1])

    stat = (8, RANK)
    gram_shape = (RANK, RANK)
    tables = [up_row, up_col, up_couple]

    def nodes_shape(count):
        return jax.ShapeDtypeStruct((2, count) + gram_shape, bf16)

    def path_shape(name):
        return (3 * stage(name)[1],) + tile

    def sibling_shape(name):
        return (stage(name)[1],) + tile

    def nodes_of(name):
        return nodes_shape(node_count(name))

    def node_scratch(name, count=1):
        return [(node_count(name),) + tile] * count

    def received(name, shape):
        return [(stage(name)[2],) + shape]

    groups = stage("mid")[2]

    z, message = call(
        start_kernel,
        [row_shape, (1,) + longer(single, HALF)],
        [me, box_rows, rhs, row_basis, local_row],
        [pltpu.SMEM(box_rows.shape, jnp.int32)]
        + [k.shape for k in (rhs, row_basis, local_row)]
        + [pltpu.SemaphoreType.DMA((4,))],
        range(1, 5),
        START_LIMIT,
    )
    def pair_shape(*shape):
        return jax.ShapeDtypeStruct((2,) + shape, bf16)

    def within(y, earlier):
        operands = [earlier, y, dense, row_basis, col_basis, cross]
        return call(inner_kernel, [col_shape], operands, (), (0,))[0]

    message, core_sib, core_nodes = call(
        core_kernel,
        [(1,) + longer(single, HALF), sibling_shape("core"), nodes_of("core")],
        [me] + swap_parts(message, "core") + [up_row],
        received("core", longer(single, HALF)) + node_scratch("core"),
    )
    cross, columns, paths = call(
        paths_kernel,
        [
            pair_shape(LEAF_DEV * RANK, LEAF_DEV * RANK),
            pair_shape(LEAF_DEV * LEAF_COLS, RANK),
            pair_shape(LEAF_DEV * RANK, RANK),
        ],
        [message, col_basis, local_row, local_col, local_couple],
        (),
        (0,),
    )
    message, row_sib, row_nodes, near_gain, path = call(
        row_kernel,
        [(groups,) + longer(single, SLICE), sibling_shape("row"), nodes_of("row"), nodes_shape(3), gram_shape],
        [me, paths] + swap_parts(message, "row") + tables,
        received("row", longer(single, HALF)) + node_scratch("row") + [(HALF, RANK)],
        (1,),
    )
    message, mid_sib, part, diagonal = call(
        mid_kernel,
        [(1,) + single, sibling_shape("mid"), (HALF, RANK), stat],
        [me, swap_mid(message), up_row],
        node_scratch("mid"),
    )
    (mid_gain,) = call(
        gains_kernel, [nodes_shape(5)], [me, message, up_col, up_couple, path], (), (1,)
    )
    gains = [near_gain, mid_gain]
    x, beta, message, own, inner = call(
        first_kernel,
        [col_shape, tile, (1,) + longer(double, HALF), stat, row_shape],
        [me, box_rows]
        + swap_parts(message, "far")
        + [core_sib, row_sib, mid_sib]
        + gains
        + [part, up_row, dense, row_basis, col_basis, cross, columns, paths, within(z, message)],
        [(2,) + tile] + received("far", single),
    )
    message, core_path, core_own = call(
        core_pair_kernel,
        [(1,) + longer(double, 2 * HALF), path_shape("core"), stat],
        [me] + swap_parts(message, "core") + tables + [core_nodes],
        received("core", longer(double, HALF)) + node_scratch("core", 2),
    )
    (images,) = call(
        images_kernel,
        [pair_shape(RANK, LEAF_DEV * LEAF_COLS)],
        [message, box_rows, dense, row_basis, col_basis, cross, paths],
        (),
        (0,),
    )
    message, row_path, row_own, mid_nodes, gram = call(
        row_pair_kernel,
        [(groups,) + double, path_shape("row"), stat, nodes_of("mid"), (HALF + 8, RANK)],
        [me, images] + swap_parts(message, "row") + tables + [row_nodes, diagonal],
        received("row", longer(double, 2 * HALF)) + node_scratch("row", 2),
        (1,),
    )
    message, mid_path, mid_own = call(
        mid_pair_kernel,
        [(1,) + longer(double, HALF + 8), path_shape("mid"), stat],
        [me, swap_mid(message)] + tables + [mid_nodes, gram],
        node_scratch("mid", 2),
    )
    v, x, alpha, rho, message, top_nodes = call(
        middle_kernel,
        [col_shape, col_shape, tile, tile, (1,) + double, nodes_shape(4)],
        [me, box_rows]
        + swap_parts(message, "far")
        + [core_path, core_own, row_path, row_own, mid_path, mid_own]
        + gains
        + tables
        + [core_nodes, row_nodes, mid_nodes]
        + [dense, row_basis, col_basis, cross, columns, images, x, own, within(inner, message)],
        [(6,) + tile, (4,) + tile] + received("far", longer(double, HALF + 8)),
    )
    for name, nodes, peers in (
        ("core", core_nodes, 1),
        ("row", row_nodes, groups),
        ("mid", mid_nodes, 1),
    ):
        parts = [swap_mid(message)] if name == "mid" else swap_parts(message, name)
        (message,) = call(
            functools.partial(last_pair_kernel, name),
            [(peers,) + double],
            [me] + parts + tables + [nodes],
            [] if name == "mid" else received(name, double),
        )
    (out,) = call(
        final_kernel,
        [col_shape],
        [me] + swap_parts(message, "far") + tables + [top_nodes, beta, alpha, rho, v, x],
        received("far", double),
    )
    return out


def solution(mesh):
    devices = mesh.shape["leaf"]
    return jax.shard_map(
        functools.partial(local_program, devices),
        mesh=mesh,
        in_specs=(
            P(None, "leaf"),
            P("leaf"),
            P("leaf", None, None),
            P("leaf", None, None),
            P("leaf", None, None),
            P("leaf", None, None),
            P("leaf", None, None),
            P("leaf", None, None, None),
            P(),
            P(),
            P(),
        ),
        out_specs=P(None, "leaf"),
        check_vma=False,
    )
```

```python
import functools

import jax
import jax.numpy as jnp
from jax import lax
from jax.experimental import pallas as pl
from jax.experimental.pallas import tpu as pltpu
from jax.sharding import PartitionSpec as P

RHS = 16
RANK = 128
LEAF_DEV = 4
LEAF_ROWS = 512
LEAF_COLS = 256
HALF = RANK // 2
SLICE = 8
COST_FLOPS = 6000000000
TINY = 1.2e-38
ORDER = (0, 1, 3, 2)
NEAR = 8
STAGES = {"core": (0, 1), "row": (1, 2), "mid": (3, 3), "far": (6, 2)}
VMEM_MIB = 24
VMEM_LIMIT = VMEM_MIB * 1024 * 1024
START_LIMIT = 60 * 1024 * 1024

f32 = jnp.float32
bf16 = jnp.bfloat16


def split(v):
    head = v.astype(bf16)
    return head, (v - head.astype(f32)).astype(bf16)


def mm(x, pair, transposed=False):
    xh, xl = split(x)
    wh, wl = pair
    dims = (((1,), (1 if transposed else 0,)), ((), ()))
    n = x.shape[0]
    both = lax.dot_general(jnp.concatenate([xh, xl], 0), wh, dims, preferred_element_type=f32)
    rest = lax.dot_general(xh, wl, dims, preferred_element_type=f32)
    return both[:n] + (both[n:] + rest)


def mm_inner(a, b):
    ah, al = split(a)
    bh, bl = split(b)
    dims = (((0,), (0,)), ((), ()))
    m = a.shape[1]
    both = lax.dot_general(jnp.concatenate([ah, al], 1), bh, dims, preferred_element_type=f32)
    rest = lax.dot_general(ah, bl, dims, preferred_element_type=f32)
    return both[:m] + (both[m:] + rest)


def gram_of(a):
    high, low = split(a)
    dims = (((0,), (0,)), ((), ()))
    rest = lax.dot_general(high, low, dims, preferred_element_type=f32)
    return lax.dot_general(high, high, dims, preferred_element_type=f32) + (rest + jnp.transpose(rest))


def pair_at(ref, *index):
    if ref.dtype == bf16:
        return ref[(0,) + index], ref[(1,) + index]
    return split(ref[index])


def half_of(ref, j, child):
    return pair_at(ref, j, pl.ds(pl.multiple_of(child * RANK, RANK), RANK))


def eye():
    return (
        lax.broadcasted_iota(jnp.int32, (RHS, RANK), 0)
        == lax.broadcasted_iota(jnp.int32, (RHS, RANK), 1)
    ).astype(f32)


def stat_block(*values):
    rows = lax.broadcasted_iota(jnp.int32, (8, RANK), 0)
    block = jnp.where(rows == 0, values[0], 0.0)
    for k in range(1, len(values)):
        block = jnp.where(rows == k, values[k], block)
    return block


def column_of(row):
    return jnp.sum(row * eye(), axis=1, keepdims=True)


def row_of(column):
    return jnp.sum(column * eye(), axis=0, keepdims=True)


def inverse_norm(squares):
    return jnp.where(squares >= TINY, 1.0 / jnp.sqrt(squares), 1.0)


def sum_squares(v):
    return jnp.sum(v * v, axis=1, keepdims=True)


def send(out_ref, value):
    for peer in range(out_ref.shape[0]):
        out_ref[peer] = value


def stack(blocks):
    return jnp.concatenate(blocks, 0)


def unstack(value, count):
    size = value.shape[0] // count
    return [value[k * size : (k + 1) * size] for k in range(count)]


def climb(blocks, transfer):
    count = len(blocks) // 2
    paired = [jnp.concatenate([blocks[2 * m], blocks[2 * m + 1]], 1) for m in range(count)]
    return unstack(mm(stack(paired), transfer), count)


def descend(blocks, transfer):
    spread = unstack(mm(stack(blocks), transfer, transposed=True), len(blocks))
    out = []
    for block in spread:
        out += [block[:, :RANK], block[:, RANK:]]
    return out


def couple_all(blocks, coupling):
    count = len(blocks) // 2
    even = unstack(mm(stack(blocks[1::2]), coupling[0]), count)
    odd = unstack(mm(stack(blocks[0::2]), coupling[1]), count)
    out = []
    for m in range(count):
        out += [even[m], odd[m]]
    return out


def lanes(value, k):
    return value[:, k * RANK : (k + 1) * RANK]


def live_mask(rows_ref, q):
    slots = lax.broadcasted_iota(jnp.int32, (RHS, LEAF_ROWS), 1)
    return (slots < rows_ref[q]).astype(f32)


def row_part(q):
    return slice(q * LEAF_ROWS, (q + 1) * LEAF_ROWS)


def col_part(q):
    return slice(q * LEAF_COLS, (q + 1) * LEAF_COLS)


def pair_up(parts, local, rows_ref, msg_ref, own_ref, inner_ref, extra):
    dense_ref, row_basis_ref, col_basis_ref, cross_ref, columns_ref, paths_ref, images_ref = local
    squares = sum_squares(parts[0])
    for part in parts[1:]:
        squares = squares + sum_squares(part)
    scale = inverse_norm(squares)
    whole = jnp.concatenate(parts, 1)
    root = mm(whole, pair_at(columns_ref)) * scale
    leaf = [mm(parts[q], pair_at(col_basis_ref, q)) for q in range(LEAF_DEV)]
    down = mm(jnp.concatenate(leaf, 1), pair_at(cross_ref))
    energy = jnp.zeros((RHS, 1), f32)
    rows = []
    for q in range(LEAF_DEV):
        y = mm(parts[q], pair_at(dense_ref, q), transposed=True)
        y = y + mm(lanes(down, q), pair_at(row_basis_ref, q), transposed=True)
        y = y * (live_mask(rows_ref, q) * scale)
        if inner_ref is not None:
            inner_ref[:, row_part(q)] = y
        energy = energy + sum_squares(y)
        if images_ref is None:
            rows.append(mm(y, pair_at(row_basis_ref, q)))
    if images_ref is None:
        row_root = mm(jnp.concatenate(rows, 1), pair_at(paths_ref))
    else:
        row_root = mm(whole * scale, pair_at(images_ref), transposed=True)
    stats = stat_block(row_of(squares), row_of(energy))
    if own_ref is not None:
        own_ref[...] = stats
    send(msg_ref, stack([root, row_root, stats] + extra))


def paths_kernel(
    order_ref,
    col_basis_ref,
    local_row_ref,
    local_col_ref,
    local_couple_ref,
    up_row_ref,
    cross_ref,
    columns_ref,
    paths_ref,
    products_ref,
    turned_ref,
):
    del order_ref
    store_products("row", up_row_ref, products_ref, turned_ref)
    halves = [slice(0, RANK), slice(RANK, 2 * RANK)]

    def store(ref, index, value):
        high, low = split(value)
        ref[(0,) + index] = high
        ref[(1,) + index] = low

    def part(q, size=RANK):
        return slice(q * size, (q + 1) * size)

    for q in range(LEAF_DEV):
        m, i = q // 2, q % 2
        store(cross_ref, (part(q), part(q)), jnp.zeros((RANK, RANK), f32))
        store(cross_ref, (part(q), part(q ^ 1)), local_couple_ref[m, 1 - i])
        gained = mm(local_col_ref[m, halves[i]], pair_at(local_couple_ref, 2, 1 - m))
        spread = mm(gained, pair_at(local_row_ref, 1 - m), transposed=True)
        store(cross_ref, (part(q), slice(2 * (1 - m) * RANK, 2 * (2 - m) * RANK)), spread)
        store(paths_ref, (part(q),), mm(local_row_ref[m, halves[i]], split(local_row_ref[2, halves[m]])))
        path = mm(local_col_ref[m, halves[i]], split(local_col_ref[2, halves[m]]))
        store(columns_ref, (part(q, LEAF_COLS),), mm(col_basis_ref[q], split(path)))


def store_top(up_row_ref, up_col_ref, up_couple_ref, top_ref):
    def store(source, target, value):
        high, low = split(value)
        rows = slice(source * RANK, (source + 1) * RANK)
        cols = slice(target * RANK, target * RANK + value.shape[1])
        top_ref[0, rows, cols] = high
        top_ref[1, rows, cols] = low

    for p in range(4):
        m, i = p // 2, p % 2
        store(p, p, jnp.zeros((RANK, RANK), f32))
        store(p, p ^ 1, up_couple_ref[6, 1 - i])
        half = up_col_ref[6, i * RANK : (i + 1) * RANK]
        gained = mm(half, pair_at(up_couple_ref, 7, 1 - m))
        store(p, 2 * (1 - m), mm(gained, pair_at(up_row_ref, 6), transposed=True))


def images_kernel(
    order_ref,
    rows_ref,
    dense_ref,
    row_basis_ref,
    col_basis_ref,
    cross_ref,
    paths_ref,
    up_row_ref,
    up_col_ref,
    up_couple_ref,
    images_ref,
    top_ref,
    products_ref,
    turned_ref,
):
    del order_ref
    store_products("mid", up_row_ref, products_ref, turned_ref)
    store_top(up_row_ref, up_col_ref, up_couple_ref, top_ref)
    turned = []
    images = []
    moved = []
    for q in range(LEAF_DEV):
        path = pair_at(paths_ref, slice(q * RANK, (q + 1) * RANK))
        turned.append(jnp.transpose(path[0].astype(f32) + path[1].astype(f32)))
        slots = lax.broadcasted_iota(jnp.int32, (LEAF_ROWS, RANK), 0)
        basis = jnp.where(slots < rows_ref[q], row_basis_ref[q], 0.0)
        images.append(mm_inner(basis, dense_ref[q]))
        moved.append(mm(turned[q], split(gram_of(basis))))
    inner = mm(jnp.concatenate(moved, 1), pair_at(cross_ref), transposed=True)
    for q in range(LEAF_DEV):
        image = mm(turned[q], split(images[q]))
        image = image + mm(lanes(inner, q), pair_at(col_basis_ref, q), transposed=True)
        high, low = split(image)
        images_ref[0, :, col_part(q)] = high
        images_ref[1, :, col_part(q)] = low


def inner_kernel(order_ref, y_ref, dense_ref, row_basis_ref, col_basis_ref, cross_ref, x_ref):
    del order_ref
    leaf = [mm(y_ref[:, row_part(q)], pair_at(row_basis_ref, q)) for q in range(LEAF_DEV)]
    down = mm(jnp.concatenate(leaf, 1), pair_at(cross_ref), transposed=True)
    for q in range(LEAF_DEV):
        x = mm(y_ref[:, row_part(q)], pair_at(dense_ref, q))
        x_ref[:, col_part(q)] = x + mm(lanes(down, q), pair_at(col_basis_ref, q), transposed=True)


def both_sides(grams, half):
    full = half[0].astype(f32) + half[1].astype(f32)
    left = mm(jnp.transpose(full), split(jnp.concatenate(grams, 1)))
    columns = [left[:, k * RANK : (k + 1) * RANK] for k in range(len(grams))]
    return unstack(mm(stack(columns), half), len(grams))


def gram_climb(grams, transfer):
    even = both_sides(grams[0::2], (transfer[0][:RANK], transfer[1][:RANK]))
    odd = both_sides(grams[1::2], (transfer[0][RANK:], transfer[1][RANK:]))
    return [a + b for a, b in zip(even, odd)]


def pack(gram):
    row = lax.broadcasted_iota(jnp.int32, (HALF, RANK), 0)
    col = lax.broadcasted_iota(jnp.int32, (HALF, RANK), 1)
    last = gram[HALF:]
    top = jnp.where((col < HALF) & (col > row), pltpu.roll(last, HALF, 1), gram[:HALF])
    diagonal = jnp.sum(jnp.where(col - HALF == row, last, 0.0), axis=0, keepdims=True)
    return top, diagonal


def unpack(top, diagonal):
    row = lax.broadcasted_iota(jnp.int32, (HALF, RANK), 0)
    col = lax.broadcasted_iota(jnp.int32, (HALF, RANK), 1)
    upper = jnp.where((col >= HALF) | (col < row), top, jnp.where(col == row, 0.5 * top, 0.0))
    lower = jnp.where(
        col - HALF > row,
        pltpu.roll(top, HALF, 1),
        jnp.where(col - HALF == row, 0.5 * diagonal, 0.0),
    )
    part = stack([upper, lower])
    return part + jnp.transpose(part)


def stage(name):
    level, heights = STAGES[name]
    return level, heights, 1 << heights


def place_of(me, name):
    level, _, count = stage(name)
    return (me >> level) % count


def bases(name):
    _, heights, count = stage(name)
    return [sum(count >> k for k in range(height)) for height in range(heights)]


def node_count(name):
    return 2 * stage(name)[2] - 2


def gather_parts(me, name, parts, out_ref):
    for k, part in zip(ORDER, parts):
        out_ref[place_of(me, name) ^ k] = part[0]


def store_pair(ref, index, value):
    high, low = split(value)
    ref[0, index] = high
    ref[1, index] = low


def group_grams(name, grams, up_row_ref, nodes_ref):
    for height, base in enumerate(bases(name)):
        for k, value in enumerate(grams):
            store_pair(nodes_ref, base + k, value)
        grams = gram_climb(grams, pair_at(up_row_ref, stage(name)[0] + height))
    return grams[0]


def product_base(height):
    return (2 << height) - 2


def store_products(name, up_row_ref, products_ref, turned_ref):
    level, heights, _ = stage(name)
    products = None
    for height in range(heights):
        halves = [half_of(up_row_ref, level + height, child) for child in range(2)]
        if products is None:
            products = [half[0].astype(f32) + half[1].astype(f32) for half in halves]
        else:
            products = [mm(product, half) for half in halves for product in products]
        for k, product in enumerate(products):
            store_pair(products_ref, product_base(height) + k, product)
            turned_ref[product_base(height) + k] = jnp.transpose(product)


def member_grams(name, grams, products_ref, turned_ref, nodes_ref):
    _, heights, count = stage(name)
    left = []
    for d in range(count):
        store_pair(nodes_ref, d, grams[d])
        turned = [turned_ref[product_base(h) + d % (2 << h)] for h in range(heights)]
        left.append(unstack(mm(stack(turned), split(grams[d])), heights))
    for height in range(heights):
        size = 2 << height
        base = product_base(height)
        terms = [pair_at(products_ref, base + t) for t in range(size)]
        table = tuple(stack([term[k] for term in terms]) for k in range(2))
        rows = []
        for n in range(count // size):
            rows.append(jnp.concatenate([left[n * size + t][height] for t in range(size)], 1))
        nodes = unstack(mm(stack(rows), table), len(rows))
        if height + 1 < heights:
            for k, value in enumerate(nodes):
                store_pair(nodes_ref, bases(name)[height + 1] + k, value)
    return nodes[0]


def start_copies(pairs, sems):
    copies = [
        pltpu.make_async_copy(source, target, sems.at[k])
        for k, (source, target) in enumerate(pairs)
    ]
    for copy in copies:
        copy.start()
    return copies


def start_kernel(
    me_ref,
    rows_hbm,
    rhs_hbm,
    row_basis_hbm,
    local_row_hbm,
    z_ref,
    msg_ref,
    rows_ref,
    rhs_ref,
    row_basis_ref,
    local_row_ref,
    sems,
):
    pairs = [(rows_hbm, rows_ref), (rhs_hbm, rhs_ref)]
    pairs += [(row_basis_hbm, row_basis_ref), (local_row_hbm, local_row_ref)]
    for copy in start_copies(pairs, sems):
        copy.wait()
    squares = jnp.zeros((RHS, 1), f32)
    paths = []
    for q in range(LEAF_DEV):
        m, i = q // 2, q % 2
        top = split(local_row_ref[2, m * RANK : (m + 1) * RANK])
        paths.append(mm(local_row_ref[m, i * RANK : (i + 1) * RANK], top))
    leaf = []
    grams = []
    for q in range(LEAF_DEV):
        part = rhs_ref[:, row_part(q)] * live_mask(rows_ref, q)
        z_ref[:, row_part(q)] = part
        squares = squares + sum_squares(part)
        leaf.append(mm(part, split(row_basis_ref[q])))
    for q in range(LEAF_DEV):
        slots = lax.broadcasted_iota(jnp.int32, (LEAF_ROWS, RANK), 0)
        basis = jnp.where(slots < rows_ref[q], row_basis_ref[q], 0.0)
        grams.append(gram_of(basis))
    root = mm(jnp.concatenate(leaf, 1), split(stack(paths)))
    row = row_of(squares)
    left = [mm(jnp.transpose(paths[q]), split(grams[q])) for q in range(LEAF_DEV)]
    gram = mm(jnp.concatenate(left, 1), split(stack(paths)))
    top, diagonal = pack(gram)
    send(msg_ref, stack([root, stat_block(row, row, diagonal), top]))


def sum_stats(recv_ref):
    stats = recv_ref[0, RHS : RHS + 8]
    for d in range(1, recv_ref.shape[0]):
        stats = stats + recv_ref[d, RHS : RHS + 8]
    return stats


def climb_group(name, me_ref, recv_ref, climb_ref, sib_ref, scratch_ref):
    level = stage(name)[0]
    place = place_of(me_ref[0], name)
    summaries = [recv_ref[d, :RHS] for d in range(recv_ref.shape[0])]
    for height, base in enumerate(bases(name)):
        for m, value in enumerate(summaries):
            scratch_ref[base + m] = value
        sib_ref[height] = scratch_ref[base + ((place >> height) ^ 1)]
        summaries = climb(summaries, pair_at(climb_ref, level + height))
    return summaries[0]


def received_grams(recv_ref):
    base = RHS + 8
    count = recv_ref.shape[0]
    return [unpack(recv_ref[d, base:], recv_ref[d, RHS + 2 : RHS + 3]) for d in range(count)]


def own_kernel(message_ref, out_ref):
    out_ref[...] = message_ref[...]


def path_product(me, level, path, up_col_ref):
    half = half_of(up_col_ref, level, (me >> level) & 1)
    return mm(path, half)


def sibling_gain(me, level, path, up_couple_ref):
    child = 1 - ((me >> level) & 1)
    return mm(path, pair_at(up_couple_ref, level, child))


def core_kernel(
    me_ref,
    part0_ref,
    part1_ref,
    up_row_ref,
    msg_ref,
    sib_ref,
    nodes_ref,
    recv_ref,
    scratch_ref,
):
    gather_parts(me_ref[0], "core", (part0_ref, part1_ref), recv_ref)
    summary = climb_group("core", me_ref, recv_ref, up_row_ref, sib_ref, scratch_ref)
    top, diagonal = pack(group_grams("core", received_grams(recv_ref), up_row_ref, nodes_ref))
    stats = sum_stats(recv_ref)
    send(msg_ref, stack([summary, stat_block(stats[:1], stats[1:2], diagonal), top]))


def row_kernel(
    me_ref,
    products_ref,
    turned_ref,
    part0_ref,
    part1_ref,
    part2_ref,
    part3_ref,
    up_row_ref,
    up_col_ref,
    up_couple_ref,
    msg_ref,
    sib_ref,
    nodes_ref,
    gain_ref,
    path_ref,
    recv_ref,
    scratch_ref,
    slice_ref,
):
    me = me_ref[0]
    gather_parts(me, "row", (part0_ref, part1_ref, part2_ref, part3_ref), recv_ref)
    summary = climb_group("row", me_ref, recv_ref, up_row_ref, sib_ref, scratch_ref)
    gram = member_grams("row", received_grams(recv_ref), products_ref, turned_ref, nodes_ref)
    child = 1 - (me & 1)
    store_pair(gain_ref, 0, up_couple_ref[0, child])
    path = up_col_ref[0, pl.ds(pl.multiple_of((me & 1) * RANK, RANK), RANK), :]
    for j in range(1, 3):
        store_pair(gain_ref, j, sibling_gain(me, j, path, up_couple_ref))
        path = path_product(me, j, path, up_col_ref)
    path_ref[...] = path
    top, diagonal = pack(gram)
    slice_ref[...] = top
    part = slice_ref[pl.ds(pl.multiple_of((me % NEAR) * SLICE, SLICE), SLICE), :]
    stats = sum_stats(recv_ref)
    send(msg_ref, stack([summary, stat_block(stats[:1], stats[1:2], diagonal), part]))


def mid_kernel(
    me_ref,
    recv_ref,
    up_row_ref,
    msg_ref,
    sib_ref,
    part_ref,
    diagonal_ref,
    scratch_ref,
):
    count = stage("mid")[2]
    summary = climb_group("mid", me_ref, recv_ref, up_row_ref, sib_ref, scratch_ref)
    for d in range(count):
        part_ref[d * SLICE : (d + 1) * SLICE] = recv_ref[d, RHS + 8 :]
        diagonal_ref[d : d + 1] = recv_ref[d, RHS + 2 : RHS + 3]
    send(msg_ref, stack([summary, sum_stats(recv_ref)]))


def gains_kernel(me_ref, order_ref, up_col_ref, up_couple_ref, path_ref, gain_ref):
    del order_ref
    me = me_ref[0]
    path = path_ref[...]
    for k, j in enumerate(range(stage("mid")[0], 8)):
        store_pair(gain_ref, k, sibling_gain(me, j, path, up_couple_ref))
        if j < 7:
            path = path_product(me, j, path, up_col_ref)


def from_siblings(siblings, near_gain_ref, mid_gain_ref):
    gains = [pair_at(near_gain_ref, j) for j in range(3)]
    gains += [pair_at(mid_gain_ref, j) for j in range(5)]
    gains = tuple(jnp.concatenate([g[k] for g in gains], 1) for k in range(2))
    return mm(jnp.concatenate(siblings, 1), gains, transposed=True)


def first_kernel(
    me_ref,
    rows_ref,
    part0_ref,
    part1_ref,
    part2_ref,
    part3_ref,
    core_sib_ref,
    row_sib_ref,
    mid_sib_ref,
    near_gain_ref,
    mid_gain_ref,
    part_ref,
    up_row_ref,
    dense_ref,
    row_basis_ref,
    col_basis_ref,
    cross_ref,
    columns_ref,
    paths_ref,
    within_ref,
    x_ref,
    beta_ref,
    msg_ref,
    own_ref,
    inner_ref,
    scratch_ref,
    recv_ref,
):
    me = me_ref[0]
    gather_parts(me, "far", (part0_ref, part1_ref, part2_ref, part3_ref), recv_ref)
    place = place_of(me, "far")
    summaries = [recv_ref[d, :RHS] for d in range(recv_ref.shape[0])]
    siblings = [core_sib_ref[0]] + [row_sib_ref[j] for j in range(2)] + [mid_sib_ref[j] for j in range(3)]
    siblings.append(recv_ref[place ^ 1, :RHS])
    summaries = climb(summaries, pair_at(up_row_ref, 6))
    for m, value in enumerate(summaries):
        scratch_ref[m] = value
    siblings.append(scratch_ref[(place >> 1) ^ 1])
    potential = from_siblings(siblings, near_gain_ref, mid_gain_ref)
    beta = jnp.sqrt(column_of(sum_stats(recv_ref)[:1]))
    inverse = 1.0 / beta
    beta_ref[...] = jnp.broadcast_to(beta, (RHS, RANK))
    spread = mm(potential, pair_at(columns_ref), transposed=True)
    parts = []
    for q in range(LEAF_DEV):
        x = (within_ref[:, col_part(q)] + spread[:, col_part(q)]) * inverse
        x_ref[:, col_part(q)] = x
        parts.append(x)
    local = (dense_ref, row_basis_ref, col_basis_ref, cross_ref, columns_ref, paths_ref, None)
    pair_up(parts, local, rows_ref, msg_ref, own_ref, inner_ref, [part_ref[...]])


def rescale(recv_ref):
    base = 2 * RHS
    squares = stack([recv_ref[d, base : base + 1] for d in range(recv_ref.shape[0])])
    energy = stack([recv_ref[d, base + 1 : base + 2] for d in range(recv_ref.shape[0])])
    total = jnp.sum(squares, axis=0, keepdims=True)
    factor = inverse_norm(total) / inverse_norm(squares)
    energy = jnp.sum(energy * factor * factor, axis=0, keepdims=True)
    first = []
    second = []
    for d in range(recv_ref.shape[0]):
        column = column_of(factor[d : d + 1])
        first.append(recv_ref[d, :RHS] * column)
        second.append(recv_ref[d, RHS : 2 * RHS] * column)
    return first, second, factor, total, energy


def pair_group(name, me_ref, recv_ref, tables, nodes_ref, keep):
    up_row_ref, up_col_ref, up_couple_ref = tables
    level = stage(name)[0]
    place = place_of(me_ref[0], name)
    first, second, _, total, energy = rescale(recv_ref)
    cross = jnp.zeros((RHS, RANK), f32)
    for height, base in enumerate(bases(name)):
        j = level + height
        gained = couple_all(first, (pair_at(up_couple_ref, j, 0), pair_at(up_couple_ref, j, 1)))
        summed = []
        for k in range(len(first)):
            moved = mm(gained[k], pair_at(nodes_ref, base + k))
            cross = cross + gained[k] * (2.0 * second[k] + moved)
            summed.append(second[k] + moved)
        if keep is not None:
            path_ref, gain_ref, below_ref = keep
            for k in range(len(first)):
                gain_ref[base + k] = gained[k]
                below_ref[base + k] = second[k]
            own = base + (place >> height)
            other = base + ((place >> height) ^ 1)
            path_ref[3 * height] = gain_ref[own]
            path_ref[3 * height + 1] = gain_ref[other]
            path_ref[3 * height + 2] = below_ref[other]
        first = climb(first, pair_at(up_col_ref, j))
        second = climb(summed, pair_at(up_row_ref, j))
    energy = energy + row_of(jnp.sum(cross, axis=1, keepdims=True))
    return first[0], second[0], stat_block(total, energy)


def core_pair_kernel(
    me_ref,
    part0_ref,
    part1_ref,
    up_row_ref,
    up_col_ref,
    up_couple_ref,
    nodes_ref,
    msg_ref,
    path_ref,
    own_ref,
    recv_ref,
    gain_ref,
    below_ref,
):
    gather_parts(me_ref[0], "core", (part0_ref, part1_ref), recv_ref)
    tables = (up_row_ref, up_col_ref, up_couple_ref)
    keep = (path_ref, gain_ref, below_ref)
    first, second, stats = pair_group("core", me_ref, recv_ref, tables, nodes_ref, keep)
    own_ref[...] = stats
    base = 2 * RHS + 8
    send(msg_ref, stack([first, second, stats, recv_ref[0, base:], recv_ref[1, base:]]))


def row_pair_kernel(
    me_ref,
    products_ref,
    turned_ref,
    part0_ref,
    part1_ref,
    part2_ref,
    part3_ref,
    up_row_ref,
    up_col_ref,
    up_couple_ref,
    nodes_ref,
    diagonal_ref,
    msg_ref,
    path_ref,
    own_ref,
    mid_nodes_ref,
    gram_ref,
    recv_ref,
    gain_ref,
    below_ref,
):
    gather_parts(me_ref[0], "row", (part0_ref, part1_ref, part2_ref, part3_ref), recv_ref)
    tables = (up_row_ref, up_col_ref, up_couple_ref)
    keep = (path_ref, gain_ref, below_ref)
    first, second, stats = pair_group("row", me_ref, recv_ref, tables, nodes_ref, keep)
    own_ref[...] = stats
    send(msg_ref, stack([first, second, stats]))
    base = 2 * RHS + 8
    grams = []
    for d in range(stage("mid")[2]):
        slices = []
        for p in range(NEAR):
            low = base + (p % 2) * HALF + d * SLICE
            slices.append(recv_ref[p // 2, low : low + SLICE])
        grams.append(unpack(stack(slices), diagonal_ref[d : d + 1]))
    top, diagonal = pack(member_grams("mid", grams, products_ref, turned_ref, mid_nodes_ref))
    gram_ref[...] = stack([top, stat_block(diagonal)])


def mid_pair_kernel(
    me_ref,
    recv_ref,
    up_row_ref,
    up_col_ref,
    up_couple_ref,
    nodes_ref,
    gram_ref,
    msg_ref,
    path_ref,
    own_ref,
    gain_ref,
    below_ref,
):
    tables = (up_row_ref, up_col_ref, up_couple_ref)
    keep = (path_ref, gain_ref, below_ref)
    first, second, stats = pair_group("mid", me_ref, recv_ref, tables, nodes_ref, keep)
    own_ref[...] = stats
    send(msg_ref, stack([first, second, stats, gram_ref[...]]))


def last_pair_kernel(name, me_ref, *refs):
    if name == "mid":
        recv_ref, up_row_ref, up_col_ref, up_couple_ref, nodes_ref, msg_ref = refs
    else:
        count = stage(name)[2]
        up_row_ref, up_col_ref, up_couple_ref, nodes_ref, msg_ref, recv_ref = refs[count:]
        gather_parts(me_ref[0], name, refs[:count], recv_ref)
    tables = (up_row_ref, up_col_ref, up_couple_ref)
    send(msg_ref, stack(pair_group(name, me_ref, recv_ref, tables, nodes_ref, None)))


def top_levels(recv_ref, top_ref, gram_ref):
    first, second, _, total, energy = rescale(recv_ref)
    potential = mm(jnp.concatenate(first, 1), pair_at(top_ref))
    potential = [lanes(potential, d) for d in range(recv_ref.shape[0])]
    cross = jnp.zeros((RHS, RANK), f32)
    summed = []
    for d in range(recv_ref.shape[0]):
        moved = mm(potential[d], pair_at(gram_ref, d))
        cross = cross + potential[d] * (2.0 * second[d] + moved)
        summed.append(second[d] + moved)
    energy = column_of(energy) + jnp.sum(cross, axis=1, keepdims=True)
    return potential, summed, column_of(total), energy


def middle_kernel(
    me_ref,
    rows_ref,
    part0_ref,
    part1_ref,
    part2_ref,
    part3_ref,
    core_path_ref,
    core_own_ref,
    row_path_ref,
    row_own_ref,
    mid_path_ref,
    mid_own_ref,
    near_gain_ref,
    mid_gain_ref,
    up_row_ref,
    top_ref,
    core_nodes_ref,
    row_nodes_ref,
    mid_nodes_ref,
    dense_ref,
    row_basis_ref,
    col_basis_ref,
    cross_ref,
    columns_ref,
    images_ref,
    x_ref,
    own_in_ref,
    within_ref,
    v_ref,
    next_ref,
    alpha_ref,
    rho_ref,
    msg_ref,
    top_gram_ref,
    a_ref,
    b_ref,
    recv_ref,
):
    me = me_ref[0]
    gather_parts(me, "far", (part0_ref, part1_ref, part2_ref, part3_ref), recv_ref)
    place = place_of(me, "far")
    base = 2 * RHS + 8
    for d in range(recv_ref.shape[0]):
        gram = unpack(recv_ref[d, base : base + HALF], recv_ref[d, base + HALF : base + HALF + 1])
        store_pair(top_gram_ref, d, gram)
    potential, summed, squares, energy = top_levels(recv_ref, top_ref, top_gram_ref)
    alpha = jnp.sqrt(squares)
    rho = jnp.sqrt(energy)
    alpha_ref[...] = jnp.broadcast_to(alpha, (RHS, RANK))
    rho_ref[...] = jnp.broadcast_to(rho, (RHS, RANK))
    scale = inverse_norm(squares)
    for d in range(recv_ref.shape[0]):
        a_ref[d] = potential[d]
        b_ref[d] = summed[d]
    forward = a_ref[place]
    siblings = {6: b_ref[place ^ 1]}
    for k, value in enumerate(climb(summed, pair_at(up_row_ref, 6))):
        a_ref[4 + k] = value
    siblings[7] = a_ref[4 + ((place >> 1) ^ 1)]
    for name, path_ref, part_ref, nodes_ref in (
        ("mid", mid_path_ref, mid_own_ref, mid_nodes_ref),
        ("row", row_path_ref, row_own_ref, row_nodes_ref),
        ("core", core_path_ref, core_own_ref, core_nodes_ref),
    ):
        level, heights, _ = stage(name)
        factor = scale / inverse_norm(column_of(part_ref[:1]))
        inside = place_of(me, name)
        for height in reversed(range(heights)):
            j = level + height
            child = (me >> j) & 1
            spread = mm(forward, pair_at(up_row_ref, j), transposed=True)
            low = spread[:, :RANK]
            high = spread[:, RANK:]
            forward = path_ref[3 * height] * factor + jnp.where(child == 0, low, high)
            other = path_ref[3 * height + 1] * factor + jnp.where(child == 0, high, low)
            gram = pair_at(nodes_ref, bases(name)[height] + ((inside >> height) ^ 1))
            siblings[j] = path_ref[3 * height + 2] * factor + mm(other, gram)
    backward = from_siblings([siblings[j] for j in range(8)], near_gain_ref, mid_gain_ref)
    own_factor = scale / inverse_norm(column_of(own_in_ref[:1]))
    inverse = 1.0 / rho
    spread = mm(backward, pair_at(columns_ref), transposed=True)
    spread = spread + mm(forward, pair_at(images_ref))
    parts = []
    for q in range(LEAF_DEV):
        v = x_ref[:, col_part(q)] * scale
        v_ref[:, col_part(q)] = v
        x = spread[:, col_part(q)] + within_ref[:, col_part(q)] * own_factor
        x = x * inverse - rho * v
        next_ref[:, col_part(q)] = x
        parts.append(x)
    local = (dense_ref, row_basis_ref, col_basis_ref, cross_ref, columns_ref, None, images_ref)
    pair_up(parts, local, rows_ref, msg_ref, None, None, [])


def final_kernel(
    me_ref,
    part0_ref,
    part1_ref,
    part2_ref,
    part3_ref,
    top_ref,
    top_gram_ref,
    beta_ref,
    alpha_ref,
    rho_ref,
    v_ref,
    x_ref,
    out_ref,
    recv_ref,
):
    gather_parts(me_ref[0], "far", (part0_ref, part1_ref, part2_ref, part3_ref), recv_ref)
    _, _, squares, energy = top_levels(recv_ref, top_ref, top_gram_ref)
    theta = jnp.sqrt(squares)
    rho2 = jnp.sqrt(energy - squares)
    rho = rho_ref[:, :1]
    phi = alpha_ref[:, :1] / rho * beta_ref[:, :1]
    v = v_ref[...]
    search = x_ref[...] * inverse_norm(squares) - (theta / rho) * v
    out_ref[...] = (phi / rho) * v - (phi * (theta / rho2) / rho2) * search


def call(kernel, outs, operands, scratch=(), far=(), limit=VMEM_LIMIT):
    spaces = []
    for index, operand in enumerate(operands):
        space = pltpu.SMEM if operand.dtype == jnp.int32 else pltpu.VMEM
        spaces.append(pl.ANY if index in far else space)
    outs = [shape if isinstance(shape, jax.ShapeDtypeStruct) else jax.ShapeDtypeStruct(shape, f32) for shape in outs]
    return pl.pallas_call(
        kernel,
        out_shape=outs,
        in_specs=[pl.BlockSpec(memory_space=space) for space in spaces],
        out_specs=[pl.BlockSpec(memory_space=pltpu.VMEM)] * len(outs),
        scratch_shapes=[
            pltpu.VMEM(shape, f32) if isinstance(shape, tuple) else shape for shape in scratch
        ],
        compiler_params=pltpu.CompilerParams(vmem_limit_bytes=limit),
        cost_estimate=pl.CostEstimate(flops=COST_FLOPS, bytes_accessed=0, transcendentals=0),
    )(*operands)


def device_groups(devices, stride, size):
    out = []
    for base in range(devices):
        if (base // stride) % size == 0:
            out.append([base + k * stride for k in range(size)])
    return out


def local_program(
    devices,
    rhs,
    box_rows,
    dense,
    row_basis,
    col_basis,
    local_col,
    local_row,
    local_couple,
    up_col,
    up_row,
    up_couple,
):
    me = lax.axis_index("leaf").astype(jnp.int32).reshape(1)

    def swap_parts(message, name):
        level, _, count = stage(name)
        parts = [message]
        for k in ORDER[1:count]:
            pairs = [(i, i ^ (k << level)) for i in range(devices)]
            parts.append(lax.ppermute(message, "leaf", pairs))
        return parts

    def swap_mid(message):
        level, _, count = stage("mid")
        groups = device_groups(devices, 1 << level, count)
        return lax.all_to_all(message, "leaf", 0, 0, axis_index_groups=groups)

    tile = (RHS, RANK)
    row_shape = (RHS, LEAF_DEV * LEAF_ROWS)
    col_shape = (RHS, LEAF_DEV * LEAF_COLS)
    single = (RHS + 8, RANK)
    double = (2 * RHS + 8, RANK)

    def longer(shape, rows):
        return (shape[0] + rows, shape[1])

    stat = (8, RANK)
    gram_shape = (RANK, RANK)
    tables = [up_row, up_col, up_couple]

    def nodes_shape(count):
        return jax.ShapeDtypeStruct((2, count) + gram_shape, bf16)

    def path_shape(name):
        return (3 * stage(name)[1],) + tile

    def sibling_shape(name):
        return (stage(name)[1],) + tile

    def nodes_of(name):
        return nodes_shape(node_count(name))

    def node_scratch(name, count=1):
        return [(node_count(name),) + tile] * count

    def received(name, shape):
        return [(stage(name)[2],) + shape]

    groups = stage("mid")[2]

    z, message = call(
        start_kernel,
        [row_shape, (1,) + longer(single, HALF)],
        [me, box_rows, rhs, row_basis, local_row],
        [pltpu.SMEM(box_rows.shape, jnp.int32)]
        + [k.shape for k in (rhs, row_basis, local_row)]
        + [pltpu.SemaphoreType.DMA((4,))],
        range(1, 5),
        START_LIMIT,
    )
    def pair_shape(*shape):
        return jax.ShapeDtypeStruct((2,) + shape, bf16)

    def within(y, earlier):
        operands = [earlier, y, dense, row_basis, col_basis, cross]
        return call(inner_kernel, [col_shape], operands, (), (0,))[0]

    parts = swap_parts(message, "core")
    parts[0] = call(own_kernel, [message.shape], [message])[0]
    message, core_sib, core_nodes = call(
        core_kernel,
        [(1,) + longer(single, HALF), sibling_shape("core"), nodes_of("core")],
        [me] + parts + [up_row],
        received("core", longer(single, HALF)) + node_scratch("core"),
    )
    def products_of(name):
        count = node_count(name)
        return [pair_shape(count, RANK, RANK), (count, RANK, RANK)]

    cross, columns, paths, *products = call(
        paths_kernel,
        [
            pair_shape(LEAF_DEV * RANK, LEAF_DEV * RANK),
            pair_shape(LEAF_DEV * LEAF_COLS, RANK),
            pair_shape(LEAF_DEV * RANK, RANK),
        ]
        + products_of("row"),
        [message, col_basis, local_row, local_col, local_couple, up_row],
        (),
        (0,),
    )
    message, row_sib, row_nodes, near_gain, path = call(
        row_kernel,
        [(groups,) + longer(single, SLICE), sibling_shape("row"), nodes_of("row"), nodes_shape(3), gram_shape],
        [me] + products + swap_parts(message, "row") + tables,
        received("row", longer(single, HALF)) + node_scratch("row") + [(HALF, RANK)],
    )
    message, mid_sib, part, diagonal = call(
        mid_kernel,
        [(1,) + single, sibling_shape("mid"), (HALF, RANK), stat],
        [me, swap_mid(message), up_row],
        node_scratch("mid"),
    )
    (mid_gain,) = call(
        gains_kernel, [nodes_shape(5)], [me, message, up_col, up_couple, path], (), (1,)
    )
    gains = [near_gain, mid_gain]
    x, beta, message, own, inner = call(
        first_kernel,
        [col_shape, tile, (1,) + longer(double, HALF), stat, row_shape],
        [me, box_rows]
        + swap_parts(message, "far")
        + [core_sib, row_sib, mid_sib]
        + gains
        + [part, up_row, dense, row_basis, col_basis, cross, columns, paths, within(z, message)],
        [(2,) + tile] + received("far", single),
    )
    message, core_path, core_own = call(
        core_pair_kernel,
        [(1,) + longer(double, 2 * HALF), path_shape("core"), stat],
        [me] + swap_parts(message, "core") + tables + [core_nodes],
        received("core", longer(double, HALF)) + node_scratch("core", 2),
    )
    images, top, *products = call(
        images_kernel,
        [pair_shape(RANK, LEAF_DEV * LEAF_COLS), pair_shape(4 * RANK, 4 * RANK)] + products_of("mid"),
        [message, box_rows, dense, row_basis, col_basis, cross, paths] + tables,
        (),
        (0,),
    )
    message, row_path, row_own, mid_nodes, gram = call(
        row_pair_kernel,
        [(groups,) + double, path_shape("row"), stat, nodes_of("mid"), (HALF + 8, RANK)],
        [me] + products + swap_parts(message, "row") + tables + [row_nodes, diagonal],
        received("row", longer(double, 2 * HALF)) + node_scratch("row", 2),
    )
    message, mid_path, mid_own = call(
        mid_pair_kernel,
        [(1,) + longer(double, HALF + 8), path_shape("mid"), stat],
        [me, swap_mid(message)] + tables + [mid_nodes, gram],
        node_scratch("mid", 2),
    )
    v, x, alpha, rho, message, top_nodes = call(
        middle_kernel,
        [col_shape, col_shape, tile, tile, (1,) + double, nodes_shape(4)],
        [me, box_rows]
        + swap_parts(message, "far")
        + [core_path, core_own, row_path, row_own, mid_path, mid_own]
        + gains
        + [up_row, top, core_nodes, row_nodes, mid_nodes]
        + [dense, row_basis, col_basis, cross, columns, images, x, own, within(inner, message)],
        [(6,) + tile, (4,) + tile] + received("far", longer(double, HALF + 8)),
    )
    for name, nodes, peers in (
        ("core", core_nodes, 1),
        ("row", row_nodes, groups),
        ("mid", mid_nodes, 1),
    ):
        parts = [swap_mid(message)] if name == "mid" else swap_parts(message, name)
        (message,) = call(
            functools.partial(last_pair_kernel, name),
            [(peers,) + double],
            [me] + parts + tables + [nodes],
            [] if name == "mid" else received(name, double),
        )
    (out,) = call(
        final_kernel,
        [col_shape],
        [me] + swap_parts(message, "far") + [top, top_nodes, beta, alpha, rho, v, x],
        received("far", double),
    )
    return out


def solution(mesh):
    devices = mesh.shape["leaf"]
    return jax.shard_map(
        functools.partial(local_program, devices),
        mesh=mesh,
        in_specs=(
            P(None, "leaf"),
            P("leaf"),
            P("leaf", None, None),
            P("leaf", None, None),
            P("leaf", None, None),
            P("leaf", None, None),
            P("leaf", None, None),
            P("leaf", None, None, None),
            P(),
            P(),
            P(),
        ),
        out_specs=P(None, "leaf"),
        check_vma=False,
    )
```

```python
import functools

import jax
import jax.numpy as jnp
from jax import lax
from jax.experimental import pallas as pl
from jax.experimental.pallas import tpu as pltpu
from jax.sharding import PartitionSpec as P

RHS = 16
RANK = 128
LEAF_DEV = 4
LEAF_ROWS = 512
LEAF_COLS = 256
HALF = RANK // 2
SLICE = 8
COST_FLOPS = 6000000000
TINY = 1.2e-38
ORDER = (0, 1, 3, 2)
NEAR = 8
STAGES = {"core": (0, 1), "row": (1, 2), "mid": (3, 3), "far": (6, 2)}
VMEM_MIB = 24
VMEM_LIMIT = VMEM_MIB * 1024 * 1024
START_LIMIT = 60 * 1024 * 1024

f32 = jnp.float32
bf16 = jnp.bfloat16


def split(v):
    head = v.astype(bf16)
    return head, (v - head.astype(f32)).astype(bf16)


def mm(x, pair, transposed=False):
    xh, xl = x if isinstance(x, tuple) else split(x)
    wh, wl = pair
    dims = (((1,), (1 if transposed else 0,)), ((), ()))
    n = xh.shape[0]
    both = lax.dot_general(jnp.concatenate([xh, xl], 0), wh, dims, preferred_element_type=f32)
    rest = lax.dot_general(xh, wl, dims, preferred_element_type=f32)
    return both[:n] + (both[n:] + rest)


def mm_square(x, pair):
    xh, xl = x
    wh, wl = pair
    upper = jnp.concatenate([wh, wl], 1)
    lower = jnp.concatenate([wh, jnp.zeros_like(wl)], 1)
    out = jnp.dot(
        jnp.concatenate([xh, xl], 1), jnp.concatenate([upper, lower], 0), preferred_element_type=f32
    )
    return out[:, :RANK] + out[:, RANK:]


def mm_narrow(x, pair):
    xh, xl = split(x)
    wh, wl = pair
    out = jnp.dot(xh, jnp.concatenate([wh, wl], 1), preferred_element_type=f32)
    rest = jnp.dot(xl, wh, preferred_element_type=f32)
    return out[:, :RANK] + (out[:, RANK:] + rest)


def mm_inner(a, b):
    ah, al = split(a)
    bh, bl = split(b)
    dims = (((0,), (0,)), ((), ()))
    m = a.shape[1]
    both = lax.dot_general(jnp.concatenate([ah, al], 1), bh, dims, preferred_element_type=f32)
    rest = lax.dot_general(ah, bl, dims, preferred_element_type=f32)
    return both[:m] + (both[m:] + rest)


def gram_of(a):
    high, low = split(a)
    dims = (((0,), (0,)), ((), ()))
    rest = lax.dot_general(high, low, dims, preferred_element_type=f32)
    return lax.dot_general(high, high, dims, preferred_element_type=f32) + (rest + jnp.transpose(rest))


def pair_at(ref, *index):
    if ref.dtype == bf16:
        return ref[(0,) + index], ref[(1,) + index]
    return split(ref[index])


def half_of(ref, j, child):
    return pair_at(ref, j, pl.ds(pl.multiple_of(child * RANK, RANK), RANK))


def eye():
    return (
        lax.broadcasted_iota(jnp.int32, (RHS, RANK), 0)
        == lax.broadcasted_iota(jnp.int32, (RHS, RANK), 1)
    ).astype(f32)


def stat_block(*values):
    rows = lax.broadcasted_iota(jnp.int32, (8, RANK), 0)
    block = jnp.where(rows == 0, values[0], 0.0)
    for k in range(1, len(values)):
        block = jnp.where(rows == k, values[k], block)
    return block


def column_of(row):
    return jnp.sum(row * eye(), axis=1, keepdims=True)


def row_of(column):
    return jnp.sum(column * eye(), axis=0, keepdims=True)


def inverse_norm(squares):
    return jnp.where(squares >= TINY, 1.0 / jnp.sqrt(squares), 1.0)


def sum_squares(v):
    return jnp.sum(v * v, axis=1, keepdims=True)


def send(out_ref, value):
    for peer in range(out_ref.shape[0]):
        out_ref[peer] = value


def stack(blocks):
    return jnp.concatenate(blocks, 0)


def unstack(value, count):
    size = value.shape[0] // count
    return [value[k * size : (k + 1) * size] for k in range(count)]


def climb(blocks, transfer):
    count = len(blocks) // 2
    paired = [jnp.concatenate([blocks[2 * m], blocks[2 * m + 1]], 1) for m in range(count)]
    return unstack(mm(stack(paired), transfer), count)


def descend(blocks, transfer):
    spread = unstack(mm(stack(blocks), transfer, transposed=True), len(blocks))
    out = []
    for block in spread:
        out += [block[:, :RANK], block[:, RANK:]]
    return out


def couple_all(blocks, coupling):
    count = len(blocks) // 2
    even = unstack(mm(stack(blocks[1::2]), coupling[0]), count)
    odd = unstack(mm(stack(blocks[0::2]), coupling[1]), count)
    out = []
    for m in range(count):
        out += [even[m], odd[m]]
    return out


def lanes(value, k):
    return value[:, k * RANK : (k + 1) * RANK]


def live_mask(rows_ref, q):
    slots = lax.broadcasted_iota(jnp.int32, (RHS, LEAF_ROWS), 1)
    return (slots < rows_ref[q]).astype(f32)


def row_part(q):
    return slice(q * LEAF_ROWS, (q + 1) * LEAF_ROWS)


def col_part(q):
    return slice(q * LEAF_COLS, (q + 1) * LEAF_COLS)


def pair_up(parts, local, rows_ref, msg_ref, own_ref, inner_ref, extra):
    dense_ref, row_basis_ref, col_basis_ref, cross_ref, columns_ref, paths_ref, images_ref = local
    squares = sum_squares(parts[0])
    for part in parts[1:]:
        squares = squares + sum_squares(part)
    scale = inverse_norm(squares)
    whole = jnp.concatenate(parts, 1)
    root = mm(whole, pair_at(columns_ref)) * scale
    leaf = [mm(parts[q], pair_at(col_basis_ref, q)) for q in range(LEAF_DEV)]
    down = mm(jnp.concatenate(leaf, 1), pair_at(cross_ref))
    energy = jnp.zeros((RHS, 1), f32)
    rows = []
    for q in range(LEAF_DEV):
        y = mm(parts[q], pair_at(dense_ref, q), transposed=True)
        y = y + mm(lanes(down, q), pair_at(row_basis_ref, q), transposed=True)
        y = y * (live_mask(rows_ref, q) * scale)
        if inner_ref is not None:
            inner_ref[:, row_part(q)] = y
        energy = energy + sum_squares(y)
        if images_ref is None:
            rows.append(mm(y, pair_at(row_basis_ref, q)))
    if images_ref is None:
        row_root = mm(jnp.concatenate(rows, 1), pair_at(paths_ref))
    else:
        row_root = mm(whole * scale, pair_at(images_ref), transposed=True)
    stats = stat_block(row_of(squares), row_of(energy))
    if own_ref is not None:
        own_ref[...] = stats
    send(msg_ref, stack([root, row_root, stats] + extra))


def paths_kernel(
    order_ref,
    col_basis_ref,
    local_row_ref,
    local_col_ref,
    local_couple_ref,
    up_row_ref,
    cross_ref,
    columns_ref,
    paths_ref,
    products_ref,
    turned_ref,
):
    del order_ref
    store_products("row", up_row_ref, products_ref, turned_ref)
    halves = [slice(0, RANK), slice(RANK, 2 * RANK)]

    def store(ref, index, value):
        high, low = split(value)
        ref[(0,) + index] = high
        ref[(1,) + index] = low

    def part(q, size=RANK):
        return slice(q * size, (q + 1) * size)

    for q in range(LEAF_DEV):
        m, i = q // 2, q % 2
        store(cross_ref, (part(q), part(q)), jnp.zeros((RANK, RANK), f32))
        store(cross_ref, (part(q), part(q ^ 1)), local_couple_ref[m, 1 - i])
        gained = mm(local_col_ref[m, halves[i]], pair_at(local_couple_ref, 2, 1 - m))
        spread = mm(gained, pair_at(local_row_ref, 1 - m), transposed=True)
        store(cross_ref, (part(q), slice(2 * (1 - m) * RANK, 2 * (2 - m) * RANK)), spread)
        store(paths_ref, (part(q),), mm(local_row_ref[m, halves[i]], split(local_row_ref[2, halves[m]])))
        path = mm(local_col_ref[m, halves[i]], split(local_col_ref[2, halves[m]]))
        store(columns_ref, (part(q, LEAF_COLS),), mm(col_basis_ref[q], split(path)))


def store_top(up_row_ref, up_col_ref, up_couple_ref, top_ref):
    def store(source, target, value):
        high, low = split(value)
        rows = slice(source * RANK, (source + 1) * RANK)
        cols = slice(target * RANK, target * RANK + value.shape[1])
        top_ref[0, rows, cols] = high
        top_ref[1, rows, cols] = low

    for p in range(4):
        m, i = p // 2, p % 2
        store(p, p, jnp.zeros((RANK, RANK), f32))
        store(p, p ^ 1, up_couple_ref[6, 1 - i])
        half = up_col_ref[6, i * RANK : (i + 1) * RANK]
        gained = mm(half, pair_at(up_couple_ref, 7, 1 - m))
        store(p, 2 * (1 - m), mm(gained, pair_at(up_row_ref, 6), transposed=True))


def images_kernel(
    order_ref,
    rows_ref,
    dense_ref,
    row_basis_ref,
    col_basis_ref,
    cross_ref,
    paths_ref,
    up_row_ref,
    up_col_ref,
    up_couple_ref,
    images_ref,
    top_ref,
    products_ref,
    turned_ref,
):
    del order_ref
    store_products("mid", up_row_ref, products_ref, turned_ref)
    store_top(up_row_ref, up_col_ref, up_couple_ref, top_ref)
    turned = []
    images = []
    moved = []
    for q in range(LEAF_DEV):
        path = pair_at(paths_ref, slice(q * RANK, (q + 1) * RANK))
        turned.append(jnp.transpose(path[0].astype(f32) + path[1].astype(f32)))
        slots = lax.broadcasted_iota(jnp.int32, (LEAF_ROWS, RANK), 0)
        basis = jnp.where(slots < rows_ref[q], row_basis_ref[q], 0.0)
        images.append(mm_inner(basis, dense_ref[q]))
        moved.append(mm(turned[q], split(gram_of(basis))))
    inner = mm(jnp.concatenate(moved, 1), pair_at(cross_ref), transposed=True)
    for q in range(LEAF_DEV):
        image = mm(turned[q], split(images[q]))
        image = image + mm(lanes(inner, q), pair_at(col_basis_ref, q), transposed=True)
        high, low = split(image)
        images_ref[0, :, col_part(q)] = high
        images_ref[1, :, col_part(q)] = low


def inner_kernel(order_ref, y_ref, dense_ref, row_basis_ref, col_basis_ref, cross_ref, x_ref):
    del order_ref
    leaf = [mm(y_ref[:, row_part(q)], pair_at(row_basis_ref, q)) for q in range(LEAF_DEV)]
    down = mm(jnp.concatenate(leaf, 1), pair_at(cross_ref), transposed=True)
    for q in range(LEAF_DEV):
        x = mm(y_ref[:, row_part(q)], pair_at(dense_ref, q))
        x_ref[:, col_part(q)] = x + mm(lanes(down, q), pair_at(col_basis_ref, q), transposed=True)


def both_sides(grams, half):
    full = half[0].astype(f32) + half[1].astype(f32)
    left = mm(jnp.transpose(full), split(jnp.concatenate(grams, 1)))
    columns = [left[:, k * RANK : (k + 1) * RANK] for k in range(len(grams))]
    return unstack(mm(stack(columns), half), len(grams))


def gram_climb(grams, transfer):
    even = both_sides(grams[0::2], (transfer[0][:RANK], transfer[1][:RANK]))
    odd = both_sides(grams[1::2], (transfer[0][RANK:], transfer[1][RANK:]))
    return [a + b for a, b in zip(even, odd)]


def pack(gram):
    row = lax.broadcasted_iota(jnp.int32, (HALF, RANK), 0)
    col = lax.broadcasted_iota(jnp.int32, (HALF, RANK), 1)
    last = gram[HALF:]
    top = jnp.where((col < HALF) & (col > row), pltpu.roll(last, HALF, 1), gram[:HALF])
    diagonal = jnp.sum(jnp.where(col - HALF == row, last, 0.0), axis=0, keepdims=True)
    return top, diagonal


def unpack(top, diagonal):
    row = lax.broadcasted_iota(jnp.int32, (HALF, RANK), 0)
    col = lax.broadcasted_iota(jnp.int32, (HALF, RANK), 1)
    upper = jnp.where((col >= HALF) | (col < row), top, jnp.where(col == row, 0.5 * top, 0.0))
    lower = jnp.where(
        col - HALF > row,
        pltpu.roll(top, HALF, 1),
        jnp.where(col - HALF == row, 0.5 * diagonal, 0.0),
    )
    part = stack([upper, lower])
    return part + jnp.transpose(part)


def stage(name):
    level, heights = STAGES[name]
    return level, heights, 1 << heights


def place_of(me, name):
    level, _, count = stage(name)
    return (me >> level) % count


def bases(name):
    _, heights, count = stage(name)
    return [sum(count >> k for k in range(height)) for height in range(heights)]


def node_count(name):
    return 2 * stage(name)[2] - 2


def gather_parts(me, name, parts, out_ref):
    for k, part in zip(ORDER, parts):
        out_ref[place_of(me, name) ^ k] = part[0]


def store_pair(ref, index, value):
    high, low = split(value)
    ref[0, index] = high
    ref[1, index] = low


def group_grams(name, grams, up_row_ref, nodes_ref):
    for height, base in enumerate(bases(name)):
        for k, value in enumerate(grams):
            store_pair(nodes_ref, base + k, value)
        grams = gram_climb(grams, pair_at(up_row_ref, stage(name)[0] + height))
    return grams[0]


def product_base(height):
    return (2 << height) - 2


def store_products(name, up_row_ref, products_ref, turned_ref):
    level, heights, _ = stage(name)
    products = None
    for height in range(heights):
        halves = [half_of(up_row_ref, level + height, child) for child in range(2)]
        if products is None:
            products = [half[0].astype(f32) + half[1].astype(f32) for half in halves]
        else:
            products = [mm(product, half) for half in halves for product in products]
        for k, product in enumerate(products):
            store_pair(products_ref, product_base(height) + k, product)
            store_pair(turned_ref, product_base(height) + k, jnp.transpose(product))


def member_grams(name, grams, products_ref, turned_ref, nodes_ref):
    _, heights, count = stage(name)
    left = []
    for d in range(count):
        store_pair(nodes_ref, d, grams[d])
        turned = [pair_at(turned_ref, product_base(h) + d % (2 << h)) for h in range(heights)]
        turned = tuple(stack([term[k] for term in turned]) for k in range(2))
        left.append(unstack(mm_square(turned, split(grams[d])), heights))
    for height in range(heights):
        size = 2 << height
        base = product_base(height)
        terms = [pair_at(products_ref, base + t) for t in range(size)]
        table = tuple(stack([term[k] for term in terms]) for k in range(2))
        rows = []
        for n in range(count // size):
            rows.append(jnp.concatenate([left[n * size + t][height] for t in range(size)], 1))
        nodes = unstack(mm_narrow(stack(rows), table), len(rows))
        if height + 1 < heights:
            for k, value in enumerate(nodes):
                store_pair(nodes_ref, bases(name)[height + 1] + k, value)
    return nodes[0]


def start_copies(pairs, sems):
    copies = [
        pltpu.make_async_copy(source, target, sems.at[k])
        for k, (source, target) in enumerate(pairs)
    ]
    for copy in copies:
        copy.start()
    return copies


def start_kernel(
    me_ref,
    rows_hbm,
    rhs_hbm,
    row_basis_hbm,
    local_row_hbm,
    z_ref,
    msg_ref,
    rows_ref,
    rhs_ref,
    row_basis_ref,
    local_row_ref,
    sems,
):
    pairs = [(rows_hbm, rows_ref), (rhs_hbm, rhs_ref)]
    pairs += [(row_basis_hbm, row_basis_ref), (local_row_hbm, local_row_ref)]
    for copy in start_copies(pairs, sems):
        copy.wait()
    squares = jnp.zeros((RHS, 1), f32)
    paths = []
    for q in range(LEAF_DEV):
        m, i = q // 2, q % 2
        top = split(local_row_ref[2, m * RANK : (m + 1) * RANK])
        paths.append(mm(local_row_ref[m, i * RANK : (i + 1) * RANK], top))
    leaf = []
    grams = []
    for q in range(LEAF_DEV):
        part = rhs_ref[:, row_part(q)] * live_mask(rows_ref, q)
        z_ref[:, row_part(q)] = part
        squares = squares + sum_squares(part)
        leaf.append(mm(part, split(row_basis_ref[q])))
    for q in range(LEAF_DEV):
        slots = lax.broadcasted_iota(jnp.int32, (LEAF_ROWS, RANK), 0)
        basis = jnp.where(slots < rows_ref[q], row_basis_ref[q], 0.0)
        grams.append(gram_of(basis))
    root = mm(jnp.concatenate(leaf, 1), split(stack(paths)))
    row = row_of(squares)
    left = [mm_square(split(jnp.transpose(paths[q])), split(grams[q])) for q in range(LEAF_DEV)]
    gram = mm_narrow(jnp.concatenate(left, 1), split(stack(paths)))
    top, diagonal = pack(gram)
    send(msg_ref, stack([root, stat_block(row, row, diagonal), top]))


def sum_stats(recv_ref):
    stats = recv_ref[0, RHS : RHS + 8]
    for d in range(1, recv_ref.shape[0]):
        stats = stats + recv_ref[d, RHS : RHS + 8]
    return stats


def climb_group(name, me_ref, recv_ref, climb_ref, sib_ref, scratch_ref):
    level = stage(name)[0]
    place = place_of(me_ref[0], name)
    summaries = [recv_ref[d, :RHS] for d in range(recv_ref.shape[0])]
    for height, base in enumerate(bases(name)):
        for m, value in enumerate(summaries):
            scratch_ref[base + m] = value
        sib_ref[height] = scratch_ref[base + ((place >> height) ^ 1)]
        summaries = climb(summaries, pair_at(climb_ref, level + height))
    return summaries[0]


def received_grams(recv_ref):
    base = RHS + 8
    count = recv_ref.shape[0]
    return [unpack(recv_ref[d, base:], recv_ref[d, RHS + 2 : RHS + 3]) for d in range(count)]


def own_kernel(message_ref, out_ref):
    out_ref[...] = message_ref[...]


def path_product(me, level, path, up_col_ref):
    half = half_of(up_col_ref, level, (me >> level) & 1)
    return mm(path, half)


def sibling_gain(me, level, path, up_couple_ref):
    child = 1 - ((me >> level) & 1)
    return mm(path, pair_at(up_couple_ref, level, child))


def core_kernel(
    me_ref,
    part0_ref,
    part1_ref,
    up_row_ref,
    msg_ref,
    sib_ref,
    nodes_ref,
    recv_ref,
    scratch_ref,
):
    gather_parts(me_ref[0], "core", (part0_ref, part1_ref), recv_ref)
    summary = climb_group("core", me_ref, recv_ref, up_row_ref, sib_ref, scratch_ref)
    top, diagonal = pack(group_grams("core", received_grams(recv_ref), up_row_ref, nodes_ref))
    stats = sum_stats(recv_ref)
    send(msg_ref, stack([summary, stat_block(stats[:1], stats[1:2], diagonal), top]))


def row_kernel(
    me_ref,
    products_ref,
    turned_ref,
    part0_ref,
    part1_ref,
    part2_ref,
    part3_ref,
    up_row_ref,
    order_ref,
    msg_ref,
    sib_ref,
    nodes_ref,
    recv_ref,
    scratch_ref,
    slice_ref,
):
    del order_ref
    me = me_ref[0]
    gather_parts(me, "row", (part0_ref, part1_ref, part2_ref, part3_ref), recv_ref)
    summary = climb_group("row", me_ref, recv_ref, up_row_ref, sib_ref, scratch_ref)
    gram = member_grams("row", received_grams(recv_ref), products_ref, turned_ref, nodes_ref)
    top, diagonal = pack(gram)
    slice_ref[...] = top
    part = slice_ref[pl.ds(pl.multiple_of((me % NEAR) * SLICE, SLICE), SLICE), :]
    stats = sum_stats(recv_ref)
    send(msg_ref, stack([summary, stat_block(stats[:1], stats[1:2], diagonal), part]))


def mid_kernel(
    me_ref,
    recv_ref,
    up_row_ref,
    msg_ref,
    sib_ref,
    part_ref,
    diagonal_ref,
    scratch_ref,
):
    count = stage("mid")[2]
    summary = climb_group("mid", me_ref, recv_ref, up_row_ref, sib_ref, scratch_ref)
    for d in range(count):
        part_ref[d * SLICE : (d + 1) * SLICE] = recv_ref[d, RHS + 8 :]
        diagonal_ref[d : d + 1] = recv_ref[d, RHS + 2 : RHS + 3]
    send(msg_ref, stack([summary, sum_stats(recv_ref)]))


def gains_kernel(me_ref, order_ref, up_col_ref, up_couple_ref, gain_ref):
    del order_ref
    me = me_ref[0]
    store_pair(gain_ref, 0, up_couple_ref[0, 1 - (me & 1)])
    path = up_col_ref[0, pl.ds(pl.multiple_of((me & 1) * RANK, RANK), RANK), :]
    for j in range(1, 8):
        store_pair(gain_ref, j, sibling_gain(me, j, path, up_couple_ref))
        if j < 7:
            path = path_product(me, j, path, up_col_ref)


def from_siblings(siblings, gain_ref):
    gains = [pair_at(gain_ref, j) for j in range(8)]
    gains = tuple(jnp.concatenate([g[k] for g in gains], 1) for k in range(2))
    return mm(jnp.concatenate(siblings, 1), gains, transposed=True)


def first_kernel(
    me_ref,
    rows_ref,
    part0_ref,
    part1_ref,
    part2_ref,
    part3_ref,
    core_sib_ref,
    row_sib_ref,
    mid_sib_ref,
    gain_ref,
    part_ref,
    up_row_ref,
    dense_ref,
    row_basis_ref,
    col_basis_ref,
    cross_ref,
    columns_ref,
    paths_ref,
    within_ref,
    x_ref,
    beta_ref,
    msg_ref,
    own_ref,
    inner_ref,
    scratch_ref,
    recv_ref,
):
    me = me_ref[0]
    gather_parts(me, "far", (part0_ref, part1_ref, part2_ref, part3_ref), recv_ref)
    place = place_of(me, "far")
    summaries = [recv_ref[d, :RHS] for d in range(recv_ref.shape[0])]
    siblings = [core_sib_ref[0]] + [row_sib_ref[j] for j in range(2)] + [mid_sib_ref[j] for j in range(3)]
    siblings.append(recv_ref[place ^ 1, :RHS])
    summaries = climb(summaries, pair_at(up_row_ref, 6))
    for m, value in enumerate(summaries):
        scratch_ref[m] = value
    siblings.append(scratch_ref[(place >> 1) ^ 1])
    potential = from_siblings(siblings, gain_ref)
    beta = jnp.sqrt(column_of(sum_stats(recv_ref)[:1]))
    inverse = 1.0 / beta
    beta_ref[...] = jnp.broadcast_to(beta, (RHS, RANK))
    spread = mm(potential, pair_at(columns_ref), transposed=True)
    parts = []
    for q in range(LEAF_DEV):
        x = (within_ref[:, col_part(q)] + spread[:, col_part(q)]) * inverse
        x_ref[:, col_part(q)] = x
        parts.append(x)
    local = (dense_ref, row_basis_ref, col_basis_ref, cross_ref, columns_ref, paths_ref, None)
    pair_up(parts, local, rows_ref, msg_ref, own_ref, inner_ref, [part_ref[...]])


def rescale(recv_ref):
    base = 2 * RHS
    squares = stack([recv_ref[d, base : base + 1] for d in range(recv_ref.shape[0])])
    energy = stack([recv_ref[d, base + 1 : base + 2] for d in range(recv_ref.shape[0])])
    total = jnp.sum(squares, axis=0, keepdims=True)
    factor = inverse_norm(total) / inverse_norm(squares)
    energy = jnp.sum(energy * factor * factor, axis=0, keepdims=True)
    first = []
    second = []
    for d in range(recv_ref.shape[0]):
        column = column_of(factor[d : d + 1])
        first.append(recv_ref[d, :RHS] * column)
        second.append(recv_ref[d, RHS : 2 * RHS] * column)
    return first, second, factor, total, energy


def pair_group(name, me_ref, recv_ref, tables, nodes_ref, keep):
    up_row_ref, up_col_ref, up_couple_ref = tables
    level = stage(name)[0]
    place = place_of(me_ref[0], name)
    first, second, _, total, energy = rescale(recv_ref)
    cross = jnp.zeros((RHS, RANK), f32)
    for height, base in enumerate(bases(name)):
        j = level + height
        gained = couple_all(first, (pair_at(up_couple_ref, j, 0), pair_at(up_couple_ref, j, 1)))
        summed = []
        for k in range(len(first)):
            moved = mm(gained[k], pair_at(nodes_ref, base + k))
            cross = cross + gained[k] * (2.0 * second[k] + moved)
            summed.append(second[k] + moved)
        if keep is not None:
            path_ref, gain_ref, below_ref = keep
            for k in range(len(first)):
                gain_ref[base + k] = gained[k]
                below_ref[base + k] = second[k]
            own = base + (place >> height)
            other = base + ((place >> height) ^ 1)
            path_ref[3 * height] = gain_ref[own]
            path_ref[3 * height + 1] = gain_ref[other]
            path_ref[3 * height + 2] = below_ref[other]
        first = climb(first, pair_at(up_col_ref, j))
        second = climb(summed, pair_at(up_row_ref, j))
    energy = energy + row_of(jnp.sum(cross, axis=1, keepdims=True))
    return first[0], second[0], stat_block(total, energy)


def core_pair_kernel(
    me_ref,
    part0_ref,
    part1_ref,
    up_row_ref,
    up_col_ref,
    up_couple_ref,
    nodes_ref,
    msg_ref,
    path_ref,
    own_ref,
    recv_ref,
    gain_ref,
    below_ref,
):
    gather_parts(me_ref[0], "core", (part0_ref, part1_ref), recv_ref)
    tables = (up_row_ref, up_col_ref, up_couple_ref)
    keep = (path_ref, gain_ref, below_ref)
    first, second, stats = pair_group("core", me_ref, recv_ref, tables, nodes_ref, keep)
    own_ref[...] = stats
    base = 2 * RHS + 8
    send(msg_ref, stack([first, second, stats, recv_ref[0, base:], recv_ref[1, base:]]))


def row_pair_kernel(
    me_ref,
    products_ref,
    turned_ref,
    part0_ref,
    part1_ref,
    part2_ref,
    part3_ref,
    up_row_ref,
    up_col_ref,
    up_couple_ref,
    nodes_ref,
    diagonal_ref,
    msg_ref,
    path_ref,
    own_ref,
    mid_nodes_ref,
    gram_ref,
    recv_ref,
    gain_ref,
    below_ref,
):
    gather_parts(me_ref[0], "row", (part0_ref, part1_ref, part2_ref, part3_ref), recv_ref)
    tables = (up_row_ref, up_col_ref, up_couple_ref)
    keep = (path_ref, gain_ref, below_ref)
    first, second, stats = pair_group("row", me_ref, recv_ref, tables, nodes_ref, keep)
    own_ref[...] = stats
    send(msg_ref, stack([first, second, stats]))
    base = 2 * RHS + 8
    grams = []
    for d in range(stage("mid")[2]):
        slices = []
        for p in range(NEAR):
            low = base + (p % 2) * HALF + d * SLICE
            slices.append(recv_ref[p // 2, low : low + SLICE])
        grams.append(unpack(stack(slices), diagonal_ref[d : d + 1]))
    top, diagonal = pack(member_grams("mid", grams, products_ref, turned_ref, mid_nodes_ref))
    gram_ref[...] = stack([top, stat_block(diagonal)])


def mid_pair_kernel(
    me_ref,
    recv_ref,
    up_row_ref,
    up_col_ref,
    up_couple_ref,
    nodes_ref,
    gram_ref,
    msg_ref,
    path_ref,
    own_ref,
    gain_ref,
    below_ref,
):
    tables = (up_row_ref, up_col_ref, up_couple_ref)
    keep = (path_ref, gain_ref, below_ref)
    first, second, stats = pair_group("mid", me_ref, recv_ref, tables, nodes_ref, keep)
    own_ref[...] = stats
    send(msg_ref, stack([first, second, stats, gram_ref[...]]))


def last_pair_kernel(name, me_ref, *refs):
    if name == "mid":
        recv_ref, up_row_ref, up_col_ref, up_couple_ref, nodes_ref, msg_ref = refs
    else:
        count = stage(name)[2]
        up_row_ref, up_col_ref, up_couple_ref, nodes_ref, msg_ref, recv_ref = refs[count:]
        gather_parts(me_ref[0], name, refs[:count], recv_ref)
    tables = (up_row_ref, up_col_ref, up_couple_ref)
    send(msg_ref, stack(pair_group(name, me_ref, recv_ref, tables, nodes_ref, None)))


def top_levels(recv_ref, top_ref, gram_ref):
    first, second, _, total, energy = rescale(recv_ref)
    potential = mm(jnp.concatenate(first, 1), pair_at(top_ref))
    potential = [lanes(potential, d) for d in range(recv_ref.shape[0])]
    cross = jnp.zeros((RHS, RANK), f32)
    summed = []
    for d in range(recv_ref.shape[0]):
        moved = mm(potential[d], pair_at(gram_ref, d))
        cross = cross + potential[d] * (2.0 * second[d] + moved)
        summed.append(second[d] + moved)
    energy = column_of(energy) + jnp.sum(cross, axis=1, keepdims=True)
    return potential, summed, column_of(total), energy


def middle_kernel(
    me_ref,
    rows_ref,
    part0_ref,
    part1_ref,
    part2_ref,
    part3_ref,
    core_path_ref,
    core_own_ref,
    row_path_ref,
    row_own_ref,
    mid_path_ref,
    mid_own_ref,
    gain_ref,
    up_row_ref,
    top_ref,
    core_nodes_ref,
    row_nodes_ref,
    mid_nodes_ref,
    dense_ref,
    row_basis_ref,
    col_basis_ref,
    cross_ref,
    columns_ref,
    images_ref,
    x_ref,
    own_in_ref,
    within_ref,
    v_ref,
    next_ref,
    alpha_ref,
    rho_ref,
    msg_ref,
    top_gram_ref,
    a_ref,
    b_ref,
    recv_ref,
):
    me = me_ref[0]
    gather_parts(me, "far", (part0_ref, part1_ref, part2_ref, part3_ref), recv_ref)
    place = place_of(me, "far")
    base = 2 * RHS + 8
    for d in range(recv_ref.shape[0]):
        gram = unpack(recv_ref[d, base : base + HALF], recv_ref[d, base + HALF : base + HALF + 1])
        store_pair(top_gram_ref, d, gram)
    potential, summed, squares, energy = top_levels(recv_ref, top_ref, top_gram_ref)
    alpha = jnp.sqrt(squares)
    rho = jnp.sqrt(energy)
    alpha_ref[...] = jnp.broadcast_to(alpha, (RHS, RANK))
    rho_ref[...] = jnp.broadcast_to(rho, (RHS, RANK))
    scale = inverse_norm(squares)
    for d in range(recv_ref.shape[0]):
        a_ref[d] = potential[d]
        b_ref[d] = summed[d]
    forward = a_ref[place]
    siblings = {6: b_ref[place ^ 1]}
    for k, value in enumerate(climb(summed, pair_at(up_row_ref, 6))):
        a_ref[4 + k] = value
    siblings[7] = a_ref[4 + ((place >> 1) ^ 1)]
    for name, path_ref, part_ref, nodes_ref in (
        ("mid", mid_path_ref, mid_own_ref, mid_nodes_ref),
        ("row", row_path_ref, row_own_ref, row_nodes_ref),
        ("core", core_path_ref, core_own_ref, core_nodes_ref),
    ):
        level, heights, _ = stage(name)
        factor = scale / inverse_norm(column_of(part_ref[:1]))
        inside = place_of(me, name)
        for height in reversed(range(heights)):
            j = level + height
            child = (me >> j) & 1
            spread = mm(forward, pair_at(up_row_ref, j), transposed=True)
            low = spread[:, :RANK]
            high = spread[:, RANK:]
            forward = path_ref[3 * height] * factor + jnp.where(child == 0, low, high)
            other = path_ref[3 * height + 1] * factor + jnp.where(child == 0, high, low)
            gram = pair_at(nodes_ref, bases(name)[height] + ((inside >> height) ^ 1))
            siblings[j] = path_ref[3 * height + 2] * factor + mm(other, gram)
    backward = from_siblings([siblings[j] for j in range(8)], gain_ref)
    own_factor = scale / inverse_norm(column_of(own_in_ref[:1]))
    inverse = 1.0 / rho
    spread = mm(backward, pair_at(columns_ref), transposed=True)
    spread = spread + mm(forward, pair_at(images_ref))
    parts = []
    for q in range(LEAF_DEV):
        v = x_ref[:, col_part(q)] * scale
        v_ref[:, col_part(q)] = v
        x = spread[:, col_part(q)] + within_ref[:, col_part(q)] * own_factor
        x = x * inverse - rho * v
        next_ref[:, col_part(q)] = x
        parts.append(x)
    local = (dense_ref, row_basis_ref, col_basis_ref, cross_ref, columns_ref, None, images_ref)
    pair_up(parts, local, rows_ref, msg_ref, None, None, [])


def final_kernel(
    me_ref,
    part0_ref,
    part1_ref,
    part2_ref,
    part3_ref,
    top_ref,
    top_gram_ref,
    beta_ref,
    alpha_ref,
    rho_ref,
    v_ref,
    x_ref,
    out_ref,
    recv_ref,
):
    gather_parts(me_ref[0], "far", (part0_ref, part1_ref, part2_ref, part3_ref), recv_ref)
    _, _, squares, energy = top_levels(recv_ref, top_ref, top_gram_ref)
    theta = jnp.sqrt(squares)
    rho2 = jnp.sqrt(energy - squares)
    rho = rho_ref[:, :1]
    phi = alpha_ref[:, :1] / rho * beta_ref[:, :1]
    v = v_ref[...]
    search = x_ref[...] * inverse_norm(squares) - (theta / rho) * v
    out_ref[...] = (phi / rho) * v - (phi * (theta / rho2) / rho2) * search


def call(kernel, outs, operands, scratch=(), far=(), limit=VMEM_LIMIT):
    spaces = []
    for index, operand in enumerate(operands):
        space = pltpu.SMEM if operand.dtype == jnp.int32 else pltpu.VMEM
        spaces.append(pl.ANY if index in far else space)
    outs = [shape if isinstance(shape, jax.ShapeDtypeStruct) else jax.ShapeDtypeStruct(shape, f32) for shape in outs]
    return pl.pallas_call(
        kernel,
        out_shape=outs,
        in_specs=[pl.BlockSpec(memory_space=space) for space in spaces],
        out_specs=[pl.BlockSpec(memory_space=pltpu.VMEM)] * len(outs),
        scratch_shapes=[
            pltpu.VMEM(shape, f32) if isinstance(shape, tuple) else shape for shape in scratch
        ],
        compiler_params=pltpu.CompilerParams(vmem_limit_bytes=limit),
        cost_estimate=pl.CostEstimate(flops=COST_FLOPS, bytes_accessed=0, transcendentals=0),
    )(*operands)


def device_groups(devices, stride, size):
    out = []
    for base in range(devices):
        if (base // stride) % size == 0:
            out.append([base + k * stride for k in range(size)])
    return out


def local_program(
    devices,
    rhs,
    box_rows,
    dense,
    row_basis,
    col_basis,
    local_col,
    local_row,
    local_couple,
    up_col,
    up_row,
    up_couple,
):
    me = lax.axis_index("leaf").astype(jnp.int32).reshape(1)

    def swap_parts(message, name):
        level, _, count = stage(name)
        parts = [message]
        for k in ORDER[1:count]:
            pairs = [(i, i ^ (k << level)) for i in range(devices)]
            parts.append(lax.ppermute(message, "leaf", pairs))
        return parts

    def swap_mid(message):
        level, _, count = stage("mid")
        groups = device_groups(devices, 1 << level, count)
        return lax.all_to_all(message, "leaf", 0, 0, axis_index_groups=groups)

    tile = (RHS, RANK)
    row_shape = (RHS, LEAF_DEV * LEAF_ROWS)
    col_shape = (RHS, LEAF_DEV * LEAF_COLS)
    single = (RHS + 8, RANK)
    double = (2 * RHS + 8, RANK)

    def longer(shape, rows):
        return (shape[0] + rows, shape[1])

    stat = (8, RANK)
    gram_shape = (RANK, RANK)
    tables = [up_row, up_col, up_couple]

    def nodes_shape(count):
        return jax.ShapeDtypeStruct((2, count) + gram_shape, bf16)

    def path_shape(name):
        return (3 * stage(name)[1],) + tile

    def sibling_shape(name):
        return (stage(name)[1],) + tile

    def nodes_of(name):
        return nodes_shape(node_count(name))

    def node_scratch(name, count=1):
        return [(node_count(name),) + tile] * count

    def received(name, shape):
        return [(stage(name)[2],) + shape]

    groups = stage("mid")[2]

    z, message = call(
        start_kernel,
        [row_shape, (1,) + longer(single, HALF)],
        [me, box_rows, rhs, row_basis, local_row],
        [pltpu.SMEM(box_rows.shape, jnp.int32)]
        + [k.shape for k in (rhs, row_basis, local_row)]
        + [pltpu.SemaphoreType.DMA((4,))],
        range(1, 5),
        START_LIMIT,
    )
    def pair_shape(*shape):
        return jax.ShapeDtypeStruct((2,) + shape, bf16)

    def within(y, earlier):
        operands = [earlier, y, dense, row_basis, col_basis, cross]
        return call(inner_kernel, [col_shape], operands, (), (0,))[0]

    parts = swap_parts(message, "core")
    parts[0] = call(own_kernel, [message.shape], [message])[0]
    message, core_sib, core_nodes = call(
        core_kernel,
        [(1,) + longer(single, HALF), sibling_shape("core"), nodes_of("core")],
        [me] + parts + [up_row],
        received("core", longer(single, HALF)) + node_scratch("core"),
    )
    def products_of(name):
        count = node_count(name)
        return [pair_shape(count, RANK, RANK)] * 2

    cross, columns, paths, *products = call(
        paths_kernel,
        [
            pair_shape(LEAF_DEV * RANK, LEAF_DEV * RANK),
            pair_shape(LEAF_DEV * LEAF_COLS, RANK),
            pair_shape(LEAF_DEV * RANK, RANK),
        ]
        + products_of("row"),
        [message, col_basis, local_row, local_col, local_couple, up_row],
        (),
        (0,),
    )
    (gain,) = call(gains_kernel, [nodes_shape(8)], [me, paths, up_col, up_couple], (), (1,))
    message, row_sib, row_nodes = call(
        row_kernel,
        [(groups,) + longer(single, SLICE), sibling_shape("row"), nodes_of("row")],
        [me] + products + swap_parts(message, "row") + [up_row, gain],
        received("row", longer(single, HALF)) + node_scratch("row") + [(HALF, RANK)],
        (8,),
    )
    message, mid_sib, part, diagonal = call(
        mid_kernel,
        [(1,) + single, sibling_shape("mid"), (HALF, RANK), stat],
        [me, swap_mid(message), up_row],
        node_scratch("mid"),
    )
    x, beta, message, own, inner = call(
        first_kernel,
        [col_shape, tile, (1,) + longer(double, HALF), stat, row_shape],
        [me, box_rows]
        + swap_parts(message, "far")
        + [core_sib, row_sib, mid_sib]
        + [gain]
        + [part, up_row, dense, row_basis, col_basis, cross, columns, paths, within(z, message)],
        [(2,) + tile] + received("far", single),
    )
    message, core_path, core_own = call(
        core_pair_kernel,
        [(1,) + longer(double, 2 * HALF), path_shape("core"), stat],
        [me] + swap_parts(message, "core") + tables + [core_nodes],
        received("core", longer(double, HALF)) + node_scratch("core", 2),
    )
    images, top, *products = call(
        images_kernel,
        [pair_shape(RANK, LEAF_DEV * LEAF_COLS), pair_shape(4 * RANK, 4 * RANK)] + products_of("mid"),
        [message, box_rows, dense, row_basis, col_basis, cross, paths] + tables,
        (),
        (0,),
    )
    message, row_path, row_own, mid_nodes, gram = call(
        row_pair_kernel,
        [(groups,) + double, path_shape("row"), stat, nodes_of("mid"), (HALF + 8, RANK)],
        [me] + products + swap_parts(message, "row") + tables + [row_nodes, diagonal],
        received("row", longer(double, 2 * HALF)) + node_scratch("row", 2),
    )
    message, mid_path, mid_own = call(
        mid_pair_kernel,
        [(1,) + longer(double, HALF + 8), path_shape("mid"), stat],
        [me, swap_mid(message)] + tables + [mid_nodes, gram],
        node_scratch("mid", 2),
    )
    v, x, alpha, rho, message, top_nodes = call(
        middle_kernel,
        [col_shape, col_shape, tile, tile, (1,) + double, nodes_shape(4)],
        [me, box_rows]
        + swap_parts(message, "far")
        + [core_path, core_own, row_path, row_own, mid_path, mid_own]
        + [gain]
        + [up_row, top, core_nodes, row_nodes, mid_nodes]
        + [dense, row_basis, col_basis, cross, columns, images, x, own, within(inner, message)],
        [(6,) + tile, (4,) + tile] + received("far", longer(double, HALF + 8)),
    )
    for name, nodes, peers in (
        ("core", core_nodes, 1),
        ("row", row_nodes, groups),
        ("mid", mid_nodes, 1),
    ):
        parts = [swap_mid(message)] if name == "mid" else swap_parts(message, name)
        (message,) = call(
            functools.partial(last_pair_kernel, name),
            [(peers,) + double],
            [me] + parts + tables + [nodes],
            [] if name == "mid" else received(name, double),
        )
    (out,) = call(
        final_kernel,
        [col_shape],
        [me] + swap_parts(message, "far") + [top, top_nodes, beta, alpha, rho, v, x],
        received("far", double),
    )
    return out


def solution(mesh):
    devices = mesh.shape["leaf"]
    return jax.shard_map(
        functools.partial(local_program, devices),
        mesh=mesh,
        in_specs=(
            P(None, "leaf"),
            P("leaf"),
            P("leaf", None, None),
            P("leaf", None, None),
            P("leaf", None, None),
            P("leaf", None, None),
            P("leaf", None, None),
            P("leaf", None, None, None),
            P(),
            P(),
            P(),
        ),
        out_specs=P(None, "leaf"),
        check_vma=False,
    )
```

```python
import functools

import jax
import jax.numpy as jnp
from jax import lax
from jax.experimental import pallas as pl
from jax.experimental.pallas import tpu as pltpu
from jax.sharding import PartitionSpec as P

RHS = 16
RANK = 128
LEAF_DEV = 4
LEAF_ROWS = 512
LEAF_COLS = 256
HALF = RANK // 2
SLICE = 8
COST_FLOPS = 6000000000
TINY = 1.2e-38
ORDER = (0, 1, 3, 2)
NEAR = 8
STAGES = {"core": (0, 1), "row": (1, 2), "mid": (3, 3), "far": (6, 2)}
VMEM_MIB = 24
VMEM_LIMIT = VMEM_MIB * 1024 * 1024
START_LIMIT = 60 * 1024 * 1024

f32 = jnp.float32
bf16 = jnp.bfloat16


def split(v):
    head = v.astype(bf16)
    return head, (v - head.astype(f32)).astype(bf16)


def mm(x, pair, transposed=False):
    xh, xl = x if isinstance(x, tuple) else split(x)
    wh, wl = pair
    dims = (((1,), (1 if transposed else 0,)), ((), ()))
    n = xh.shape[0]
    both = lax.dot_general(jnp.concatenate([xh, xl], 0), wh, dims, preferred_element_type=f32)
    rest = lax.dot_general(xh, wl, dims, preferred_element_type=f32)
    return both[:n] + (both[n:] + rest)


def mm_square(x, pair):
    xh, xl = x
    wh, wl = pair
    upper = jnp.concatenate([wh, wl], 1)
    lower = jnp.concatenate([wh, jnp.zeros_like(wl)], 1)
    out = jnp.dot(
        jnp.concatenate([xh, xl], 1), jnp.concatenate([upper, lower], 0), preferred_element_type=f32
    )
    return out[:, :RANK] + out[:, RANK:]


def mm_narrow(x, pair):
    xh, xl = split(x)
    wh, wl = pair
    out = jnp.dot(xh, jnp.concatenate([wh, wl], 1), preferred_element_type=f32)
    rest = jnp.dot(xl, wh, preferred_element_type=f32)
    return out[:, :RANK] + (out[:, RANK:] + rest)


def mm_inner(a, b):
    ah, al = split(a)
    bh, bl = split(b)
    dims = (((0,), (0,)), ((), ()))
    m = a.shape[1]
    both = lax.dot_general(jnp.concatenate([ah, al], 1), bh, dims, preferred_element_type=f32)
    rest = lax.dot_general(ah, bl, dims, preferred_element_type=f32)
    return both[:m] + (both[m:] + rest)


def gram_of(a):
    high, low = split(a)
    dims = (((0,), (0,)), ((), ()))
    rest = lax.dot_general(high, low, dims, preferred_element_type=f32)
    return lax.dot_general(high, high, dims, preferred_element_type=f32) + (rest + jnp.transpose(rest))


def pair_at(ref, *index):
    if ref.dtype == bf16:
        return ref[(0,) + index], ref[(1,) + index]
    return split(ref[index])


def half_of(ref, j, child):
    return pair_at(ref, j, pl.ds(pl.multiple_of(child * RANK, RANK), RANK))


def eye():
    return (
        lax.broadcasted_iota(jnp.int32, (RHS, RANK), 0)
        == lax.broadcasted_iota(jnp.int32, (RHS, RANK), 1)
    ).astype(f32)


def stat_block(*values):
    rows = lax.broadcasted_iota(jnp.int32, (8, RANK), 0)
    block = jnp.where(rows == 0, values[0], 0.0)
    for k in range(1, len(values)):
        block = jnp.where(rows == k, values[k], block)
    return block


def column_of(row):
    return jnp.sum(row * eye(), axis=1, keepdims=True)


def row_of(column):
    return jnp.sum(column * eye(), axis=0, keepdims=True)


def inverse_norm(squares):
    return jnp.where(squares >= TINY, 1.0 / jnp.sqrt(squares), 1.0)


def sum_squares(v):
    return jnp.sum(v * v, axis=1, keepdims=True)


def send(out_ref, value):
    for peer in range(out_ref.shape[0]):
        out_ref[peer] = value


def stack(blocks):
    return jnp.concatenate(blocks, 0)


def unstack(value, count):
    size = value.shape[0] // count
    return [value[k * size : (k + 1) * size] for k in range(count)]


def climb(blocks, transfer):
    count = len(blocks) // 2
    paired = [jnp.concatenate([blocks[2 * m], blocks[2 * m + 1]], 1) for m in range(count)]
    return unstack(mm(stack(paired), transfer), count)


def descend(blocks, transfer):
    spread = unstack(mm(stack(blocks), transfer, transposed=True), len(blocks))
    out = []
    for block in spread:
        out += [block[:, :RANK], block[:, RANK:]]
    return out


def couple_all(blocks, coupling):
    count = len(blocks) // 2
    even = unstack(mm(stack(blocks[1::2]), coupling[0]), count)
    odd = unstack(mm(stack(blocks[0::2]), coupling[1]), count)
    out = []
    for m in range(count):
        out += [even[m], odd[m]]
    return out


def lanes(value, k):
    return value[:, k * RANK : (k + 1) * RANK]


def live_mask(rows_ref, q):
    slots = lax.broadcasted_iota(jnp.int32, (RHS, LEAF_ROWS), 1)
    return (slots < rows_ref[q]).astype(f32)


def row_part(q):
    return slice(q * LEAF_ROWS, (q + 1) * LEAF_ROWS)


def col_part(q):
    return slice(q * LEAF_COLS, (q + 1) * LEAF_COLS)


def pair_up(parts, local, rows_ref, msg_ref, own_ref, inner_ref, extra):
    dense_ref, row_basis_ref, col_basis_ref, cross_ref, columns_ref, paths_ref, images_ref = local
    squares = sum_squares(parts[0])
    for part in parts[1:]:
        squares = squares + sum_squares(part)
    scale = inverse_norm(squares)
    whole = jnp.concatenate(parts, 1)
    root = mm(whole, pair_at(columns_ref)) * scale
    leaf = [mm(parts[q], pair_at(col_basis_ref, q)) for q in range(LEAF_DEV)]
    down = mm(jnp.concatenate(leaf, 1), pair_at(cross_ref))
    energy = jnp.zeros((RHS, 1), f32)
    rows = []
    for q in range(LEAF_DEV):
        y = mm(parts[q], pair_at(dense_ref, q), transposed=True)
        y = y + mm(lanes(down, q), pair_at(row_basis_ref, q), transposed=True)
        y = y * (live_mask(rows_ref, q) * scale)
        if inner_ref is not None:
            inner_ref[:, row_part(q)] = y
        energy = energy + sum_squares(y)
        if images_ref is None:
            rows.append(mm(y, pair_at(row_basis_ref, q)))
    if images_ref is None:
        row_root = mm(jnp.concatenate(rows, 1), pair_at(paths_ref))
    else:
        row_root = mm(whole * scale, pair_at(images_ref), transposed=True)
    stats = stat_block(row_of(squares), row_of(energy))
    if own_ref is not None:
        own_ref[...] = stats
    send(msg_ref, stack([root, row_root, stats] + extra))


def paths_kernel(
    order_ref,
    col_basis_ref,
    local_row_ref,
    local_col_ref,
    local_couple_ref,
    up_row_ref,
    cross_ref,
    columns_ref,
    paths_ref,
    products_ref,
    turned_ref,
):
    del order_ref
    store_products("row", up_row_ref, products_ref, turned_ref)
    halves = [slice(0, RANK), slice(RANK, 2 * RANK)]

    def store(ref, index, value):
        high, low = split(value)
        ref[(0,) + index] = high
        ref[(1,) + index] = low

    def part(q, size=RANK):
        return slice(q * size, (q + 1) * size)

    for q in range(LEAF_DEV):
        m, i = q // 2, q % 2
        store(cross_ref, (part(q), part(q)), jnp.zeros((RANK, RANK), f32))
        store(cross_ref, (part(q), part(q ^ 1)), local_couple_ref[m, 1 - i])
        gained = mm_square(pair_at(local_col_ref, m, halves[i]), pair_at(local_couple_ref, 2, 1 - m))
        spread = mm(gained, pair_at(local_row_ref, 1 - m), transposed=True)
        store(cross_ref, (part(q), slice(2 * (1 - m) * RANK, 2 * (2 - m) * RANK)), spread)
        row_path = mm_square(pair_at(local_row_ref, m, halves[i]), pair_at(local_row_ref, 2, halves[m]))
        store(paths_ref, (part(q),), row_path)
        path = mm_square(pair_at(local_col_ref, m, halves[i]), pair_at(local_col_ref, 2, halves[m]))
        store(columns_ref, (part(q, LEAF_COLS),), mm_square(pair_at(col_basis_ref, q), split(path)))


def store_top(up_row_ref, up_col_ref, up_couple_ref, top_ref):
    def store(source, target, value):
        high, low = split(value)
        rows = slice(source * RANK, (source + 1) * RANK)
        cols = slice(target * RANK, target * RANK + value.shape[1])
        top_ref[0, rows, cols] = high
        top_ref[1, rows, cols] = low

    for p in range(4):
        m, i = p // 2, p % 2
        store(p, p, jnp.zeros((RANK, RANK), f32))
        store(p, p ^ 1, up_couple_ref[6, 1 - i])
        half = up_col_ref[6, i * RANK : (i + 1) * RANK]
        gained = mm(half, pair_at(up_couple_ref, 7, 1 - m))
        store(p, 2 * (1 - m), mm(gained, pair_at(up_row_ref, 6), transposed=True))


def images_kernel(
    order_ref,
    rows_ref,
    dense_ref,
    row_basis_ref,
    col_basis_ref,
    cross_ref,
    paths_ref,
    up_row_ref,
    up_col_ref,
    up_couple_ref,
    images_ref,
    top_ref,
    products_ref,
    turned_ref,
):
    del order_ref
    store_products("mid", up_row_ref, products_ref, turned_ref)
    store_top(up_row_ref, up_col_ref, up_couple_ref, top_ref)
    turned = []
    images = []
    moved = []
    for q in range(LEAF_DEV):
        path = pair_at(paths_ref, slice(q * RANK, (q + 1) * RANK))
        turned.append(jnp.transpose(path[0].astype(f32) + path[1].astype(f32)))
        slots = lax.broadcasted_iota(jnp.int32, (LEAF_ROWS, RANK), 0)
        basis = jnp.where(slots < rows_ref[q], row_basis_ref[q], 0.0)
        images.append(mm_inner(basis, dense_ref[q]))
        moved.append(mm_square(split(turned[q]), split(gram_of(basis))))
    inner = mm(jnp.concatenate(moved, 1), pair_at(cross_ref), transposed=True)
    for q in range(LEAF_DEV):
        image = mm(turned[q], split(images[q]))
        image = image + mm(lanes(inner, q), pair_at(col_basis_ref, q), transposed=True)
        high, low = split(image)
        images_ref[0, :, col_part(q)] = high
        images_ref[1, :, col_part(q)] = low


def inner_kernel(order_ref, y_ref, dense_ref, row_basis_ref, col_basis_ref, cross_ref, x_ref):
    del order_ref
    leaf = [mm(y_ref[:, row_part(q)], pair_at(row_basis_ref, q)) for q in range(LEAF_DEV)]
    down = mm(jnp.concatenate(leaf, 1), pair_at(cross_ref), transposed=True)
    for q in range(LEAF_DEV):
        x = mm(y_ref[:, row_part(q)], pair_at(dense_ref, q))
        x_ref[:, col_part(q)] = x + mm(lanes(down, q), pair_at(col_basis_ref, q), transposed=True)


def both_sides(grams, half):
    full = half[0].astype(f32) + half[1].astype(f32)
    left = mm(jnp.transpose(full), split(jnp.concatenate(grams, 1)))
    columns = [left[:, k * RANK : (k + 1) * RANK] for k in range(len(grams))]
    return unstack(mm(stack(columns), half), len(grams))


def gram_climb(grams, transfer):
    even = both_sides(grams[0::2], (transfer[0][:RANK], transfer[1][:RANK]))
    odd = both_sides(grams[1::2], (transfer[0][RANK:], transfer[1][RANK:]))
    return [a + b for a, b in zip(even, odd)]


def pack(gram):
    row = lax.broadcasted_iota(jnp.int32, (HALF, RANK), 0)
    col = lax.broadcasted_iota(jnp.int32, (HALF, RANK), 1)
    last = gram[HALF:]
    top = jnp.where((col < HALF) & (col > row), pltpu.roll(last, HALF, 1), gram[:HALF])
    diagonal = jnp.sum(jnp.where(col - HALF == row, last, 0.0), axis=0, keepdims=True)
    return top, diagonal


def unpack(top, diagonal):
    row = lax.broadcasted_iota(jnp.int32, (HALF, RANK), 0)
    col = lax.broadcasted_iota(jnp.int32, (HALF, RANK), 1)
    upper = jnp.where((col >= HALF) | (col < row), top, jnp.where(col == row, 0.5 * top, 0.0))
    lower = jnp.where(
        col - HALF > row,
        pltpu.roll(top, HALF, 1),
        jnp.where(col - HALF == row, 0.5 * diagonal, 0.0),
    )
    part = stack([upper, lower])
    return part + jnp.transpose(part)


def stage(name):
    level, heights = STAGES[name]
    return level, heights, 1 << heights


def place_of(me, name):
    level, _, count = stage(name)
    return (me >> level) % count


def bases(name):
    _, heights, count = stage(name)
    return [sum(count >> k for k in range(height)) for height in range(heights)]


def node_count(name):
    return 2 * stage(name)[2] - 2


def gather_parts(me, name, parts, out_ref):
    for k, part in zip(ORDER, parts):
        out_ref[place_of(me, name) ^ k] = part[0]


def store_pair(ref, index, value):
    high, low = split(value)
    ref[0, index] = high
    ref[1, index] = low


def group_grams(name, grams, up_row_ref, nodes_ref):
    for height, base in enumerate(bases(name)):
        for k, value in enumerate(grams):
            store_pair(nodes_ref, base + k, value)
        grams = gram_climb(grams, pair_at(up_row_ref, stage(name)[0] + height))
    return grams[0]


def product_base(height):
    return (2 << height) - 2


def store_products(name, up_row_ref, products_ref, turned_ref):
    level, heights, _ = stage(name)
    products = None
    for height in range(heights):
        halves = [half_of(up_row_ref, level + height, child) for child in range(2)]
        if products is None:
            products = [half[0].astype(f32) + half[1].astype(f32) for half in halves]
        else:
            products = [mm_square(split(product), half) for half in halves for product in products]
        for k, product in enumerate(products):
            store_pair(products_ref, product_base(height) + k, product)
            store_pair(turned_ref, product_base(height) + k, jnp.transpose(product))


def member_grams(name, grams, products_ref, turned_ref, nodes_ref):
    _, heights, count = stage(name)
    left = []
    for d in range(count):
        store_pair(nodes_ref, d, grams[d])
        turned = [pair_at(turned_ref, product_base(h) + d % (2 << h)) for h in range(heights)]
        turned = tuple(stack([term[k] for term in turned]) for k in range(2))
        left.append(unstack(mm_square(turned, split(grams[d])), heights))
    for height in range(heights):
        size = 2 << height
        base = product_base(height)
        terms = [pair_at(products_ref, base + t) for t in range(size)]
        table = tuple(stack([term[k] for term in terms]) for k in range(2))
        rows = []
        for n in range(count // size):
            rows.append(jnp.concatenate([left[n * size + t][height] for t in range(size)], 1))
        nodes = unstack(mm_narrow(stack(rows), table), len(rows))
        if height + 1 < heights:
            for k, value in enumerate(nodes):
                store_pair(nodes_ref, bases(name)[height + 1] + k, value)
    return nodes[0]


def start_copies(pairs, sems):
    copies = [
        pltpu.make_async_copy(source, target, sems.at[k])
        for k, (source, target) in enumerate(pairs)
    ]
    for copy in copies:
        copy.start()
    return copies


def start_kernel(
    me_ref,
    rows_hbm,
    rhs_hbm,
    row_basis_hbm,
    local_row_hbm,
    z_ref,
    msg_ref,
    rows_ref,
    rhs_ref,
    row_basis_ref,
    local_row_ref,
    sems,
):
    pairs = [(rows_hbm, rows_ref), (rhs_hbm, rhs_ref)]
    pairs += [(row_basis_hbm, row_basis_ref), (local_row_hbm, local_row_ref)]
    for copy in start_copies(pairs, sems):
        copy.wait()
    squares = jnp.zeros((RHS, 1), f32)
    paths = []
    for q in range(LEAF_DEV):
        m, i = q // 2, q % 2
        top = split(local_row_ref[2, m * RANK : (m + 1) * RANK])
        paths.append(mm(local_row_ref[m, i * RANK : (i + 1) * RANK], top))
    leaf = []
    grams = []
    for q in range(LEAF_DEV):
        part = rhs_ref[:, row_part(q)] * live_mask(rows_ref, q)
        z_ref[:, row_part(q)] = part
        squares = squares + sum_squares(part)
        leaf.append(mm(part, split(row_basis_ref[q])))
    for q in range(LEAF_DEV):
        slots = lax.broadcasted_iota(jnp.int32, (LEAF_ROWS, RANK), 0)
        basis = jnp.where(slots < rows_ref[q], row_basis_ref[q], 0.0)
        grams.append(gram_of(basis))
    root = mm(jnp.concatenate(leaf, 1), split(stack(paths)))
    row = row_of(squares)
    left = [mm_square(split(jnp.transpose(paths[q])), split(grams[q])) for q in range(LEAF_DEV)]
    gram = mm_narrow(jnp.concatenate(left, 1), split(stack(paths)))
    top, diagonal = pack(gram)
    send(msg_ref, stack([root, stat_block(row, row, diagonal), top]))


def sum_stats(recv_ref):
    stats = recv_ref[0, RHS : RHS + 8]
    for d in range(1, recv_ref.shape[0]):
        stats = stats + recv_ref[d, RHS : RHS + 8]
    return stats


def climb_group(name, me_ref, recv_ref, climb_ref, sib_ref, scratch_ref):
    level = stage(name)[0]
    place = place_of(me_ref[0], name)
    summaries = [recv_ref[d, :RHS] for d in range(recv_ref.shape[0])]
    for height, base in enumerate(bases(name)):
        for m, value in enumerate(summaries):
            scratch_ref[base + m] = value
        sib_ref[height] = scratch_ref[base + ((place >> height) ^ 1)]
        summaries = climb(summaries, pair_at(climb_ref, level + height))
    return summaries[0]


def received_grams(recv_ref):
    base = RHS + 8
    count = recv_ref.shape[0]
    return [unpack(recv_ref[d, base:], recv_ref[d, RHS + 2 : RHS + 3]) for d in range(count)]


def own_kernel(message_ref, out_ref):
    out_ref[...] = message_ref[...]


def path_product(me, level, path, up_col_ref):
    half = half_of(up_col_ref, level, (me >> level) & 1)
    return mm_square(split(path), half)


def sibling_gain(me, level, path, up_couple_ref):
    child = 1 - ((me >> level) & 1)
    return mm_square(split(path), pair_at(up_couple_ref, level, child))


def core_kernel(
    me_ref,
    part0_ref,
    part1_ref,
    up_row_ref,
    msg_ref,
    sib_ref,
    nodes_ref,
    recv_ref,
    scratch_ref,
):
    gather_parts(me_ref[0], "core", (part0_ref, part1_ref), recv_ref)
    summary = climb_group("core", me_ref, recv_ref, up_row_ref, sib_ref, scratch_ref)
    top, diagonal = pack(group_grams("core", received_grams(recv_ref), up_row_ref, nodes_ref))
    stats = sum_stats(recv_ref)
    send(msg_ref, stack([summary, stat_block(stats[:1], stats[1:2], diagonal), top]))


def row_kernel(
    me_ref,
    products_ref,
    turned_ref,
    part0_ref,
    part1_ref,
    part2_ref,
    part3_ref,
    up_row_ref,
    order_ref,
    msg_ref,
    sib_ref,
    nodes_ref,
    recv_ref,
    scratch_ref,
    slice_ref,
):
    del order_ref
    me = me_ref[0]
    gather_parts(me, "row", (part0_ref, part1_ref, part2_ref, part3_ref), recv_ref)
    summary = climb_group("row", me_ref, recv_ref, up_row_ref, sib_ref, scratch_ref)
    gram = member_grams("row", received_grams(recv_ref), products_ref, turned_ref, nodes_ref)
    top, diagonal = pack(gram)
    slice_ref[...] = top
    part = slice_ref[pl.ds(pl.multiple_of((me % NEAR) * SLICE, SLICE), SLICE), :]
    stats = sum_stats(recv_ref)
    send(msg_ref, stack([summary, stat_block(stats[:1], stats[1:2], diagonal), part]))


def mid_kernel(
    me_ref,
    recv_ref,
    up_row_ref,
    msg_ref,
    sib_ref,
    part_ref,
    diagonal_ref,
    scratch_ref,
):
    count = stage("mid")[2]
    summary = climb_group("mid", me_ref, recv_ref, up_row_ref, sib_ref, scratch_ref)
    for d in range(count):
        part_ref[d * SLICE : (d + 1) * SLICE] = recv_ref[d, RHS + 8 :]
        diagonal_ref[d : d + 1] = recv_ref[d, RHS + 2 : RHS + 3]
    send(msg_ref, stack([summary, sum_stats(recv_ref)]))


def gains_kernel(me_ref, order_ref, up_col_ref, up_couple_ref, gain_ref):
    del order_ref
    me = me_ref[0]
    store_pair(gain_ref, 0, up_couple_ref[0, 1 - (me & 1)])
    path = up_col_ref[0, pl.ds(pl.multiple_of((me & 1) * RANK, RANK), RANK), :]
    for j in range(1, 8):
        store_pair(gain_ref, j, sibling_gain(me, j, path, up_couple_ref))
        if j < 7:
            path = path_product(me, j, path, up_col_ref)


def from_siblings(siblings, gain_ref):
    gains = [pair_at(gain_ref, j) for j in range(8)]
    gains = tuple(jnp.concatenate([g[k] for g in gains], 1) for k in range(2))
    return mm(jnp.concatenate(siblings, 1), gains, transposed=True)


def first_kernel(
    me_ref,
    rows_ref,
    part0_ref,
    part1_ref,
    part2_ref,
    part3_ref,
    core_sib_ref,
    row_sib_ref,
    mid_sib_ref,
    gain_ref,
    part_ref,
    up_row_ref,
    dense_ref,
    row_basis_ref,
    col_basis_ref,
    cross_ref,
    columns_ref,
    paths_ref,
    within_ref,
    x_ref,
    beta_ref,
    msg_ref,
    own_ref,
    inner_ref,
    scratch_ref,
    recv_ref,
):
    me = me_ref[0]
    gather_parts(me, "far", (part0_ref, part1_ref, part2_ref, part3_ref), recv_ref)
    place = place_of(me, "far")
    summaries = [recv_ref[d, :RHS] for d in range(recv_ref.shape[0])]
    siblings = [core_sib_ref[0]] + [row_sib_ref[j] for j in range(2)] + [mid_sib_ref[j] for j in range(3)]
    siblings.append(recv_ref[place ^ 1, :RHS])
    summaries = climb(summaries, pair_at(up_row_ref, 6))
    for m, value in enumerate(summaries):
        scratch_ref[m] = value
    siblings.append(scratch_ref[(place >> 1) ^ 1])
    potential = from_siblings(siblings, gain_ref)
    beta = jnp.sqrt(column_of(sum_stats(recv_ref)[:1]))
    inverse = 1.0 / beta
    beta_ref[...] = jnp.broadcast_to(beta, (RHS, RANK))
    spread = mm(potential, pair_at(columns_ref), transposed=True)
    parts = []
    for q in range(LEAF_DEV):
        x = (within_ref[:, col_part(q)] + spread[:, col_part(q)]) * inverse
        x_ref[:, col_part(q)] = x
        parts.append(x)
    local = (dense_ref, row_basis_ref, col_basis_ref, cross_ref, columns_ref, paths_ref, None)
    pair_up(parts, local, rows_ref, msg_ref, own_ref, inner_ref, [part_ref[...]])


def rescale(recv_ref):
    base = 2 * RHS
    squares = stack([recv_ref[d, base : base + 1] for d in range(recv_ref.shape[0])])
    energy = stack([recv_ref[d, base + 1 : base + 2] for d in range(recv_ref.shape[0])])
    total = jnp.sum(squares, axis=0, keepdims=True)
    factor = inverse_norm(total) / inverse_norm(squares)
    energy = jnp.sum(energy * factor * factor, axis=0, keepdims=True)
    first = []
    second = []
    for d in range(recv_ref.shape[0]):
        column = column_of(factor[d : d + 1])
        first.append(recv_ref[d, :RHS] * column)
        second.append(recv_ref[d, RHS : 2 * RHS] * column)
    return first, second, factor, total, energy


def pair_group(name, me_ref, recv_ref, tables, nodes_ref, keep):
    up_row_ref, up_col_ref, up_couple_ref = tables
    level = stage(name)[0]
    place = place_of(me_ref[0], name)
    first, second, _, total, energy = rescale(recv_ref)
    cross = jnp.zeros((RHS, RANK), f32)
    for height, base in enumerate(bases(name)):
        j = level + height
        gained = couple_all(first, (pair_at(up_couple_ref, j, 0), pair_at(up_couple_ref, j, 1)))
        summed = []
        for k in range(len(first)):
            moved = mm(gained[k], pair_at(nodes_ref, base + k))
            cross = cross + gained[k] * (2.0 * second[k] + moved)
            summed.append(second[k] + moved)
        if keep is not None:
            path_ref, gain_ref, below_ref = keep
            for k in range(len(first)):
                gain_ref[base + k] = gained[k]
                below_ref[base + k] = second[k]
            own = base + (place >> height)
            other = base + ((place >> height) ^ 1)
            path_ref[3 * height] = gain_ref[own]
            path_ref[3 * height + 1] = gain_ref[other]
            path_ref[3 * height + 2] = below_ref[other]
        first = climb(first, pair_at(up_col_ref, j))
        second = climb(summed, pair_at(up_row_ref, j))
    energy = energy + row_of(jnp.sum(cross, axis=1, keepdims=True))
    return first[0], second[0], stat_block(total, energy)


def core_pair_kernel(
    me_ref,
    part0_ref,
    part1_ref,
    up_row_ref,
    up_col_ref,
    up_couple_ref,
    nodes_ref,
    msg_ref,
    path_ref,
    own_ref,
    recv_ref,
    gain_ref,
    below_ref,
):
    gather_parts(me_ref[0], "core", (part0_ref, part1_ref), recv_ref)
    tables = (up_row_ref, up_col_ref, up_couple_ref)
    keep = (path_ref, gain_ref, below_ref)
    first, second, stats = pair_group("core", me_ref, recv_ref, tables, nodes_ref, keep)
    own_ref[...] = stats
    base = 2 * RHS + 8
    send(msg_ref, stack([first, second, stats, recv_ref[0, base:], recv_ref[1, base:]]))


def row_pair_kernel(
    me_ref,
    products_ref,
    turned_ref,
    part0_ref,
    part1_ref,
    part2_ref,
    part3_ref,
    up_row_ref,
    up_col_ref,
    up_couple_ref,
    nodes_ref,
    diagonal_ref,
    msg_ref,
    path_ref,
    own_ref,
    mid_nodes_ref,
    gram_ref,
    recv_ref,
    gain_ref,
    below_ref,
):
    gather_parts(me_ref[0], "row", (part0_ref, part1_ref, part2_ref, part3_ref), recv_ref)
    tables = (up_row_ref, up_col_ref, up_couple_ref)
    keep = (path_ref, gain_ref, below_ref)
    first, second, stats = pair_group("row", me_ref, recv_ref, tables, nodes_ref, keep)
    own_ref[...] = stats
    send(msg_ref, stack([first, second, stats]))
    base = 2 * RHS + 8
    grams = []
    for d in range(stage("mid")[2]):
        slices = []
        for p in range(NEAR):
            low = base + (p % 2) * HALF + d * SLICE
            slices.append(recv_ref[p // 2, low : low + SLICE])
        grams.append(unpack(stack(slices), diagonal_ref[d : d + 1]))
    top, diagonal = pack(member_grams("mid", grams, products_ref, turned_ref, mid_nodes_ref))
    gram_ref[...] = stack([top, stat_block(diagonal)])


def mid_pair_kernel(
    me_ref,
    recv_ref,
    up_row_ref,
    up_col_ref,
    up_couple_ref,
    nodes_ref,
    gram_ref,
    msg_ref,
    path_ref,
    own_ref,
    gain_ref,
    below_ref,
):
    tables = (up_row_ref, up_col_ref, up_couple_ref)
    keep = (path_ref, gain_ref, below_ref)
    first, second, stats = pair_group("mid", me_ref, recv_ref, tables, nodes_ref, keep)
    own_ref[...] = stats
    send(msg_ref, stack([first, second, stats, gram_ref[...]]))


def last_pair_kernel(name, me_ref, *refs):
    if name == "mid":
        recv_ref, up_row_ref, up_col_ref, up_couple_ref, nodes_ref, msg_ref = refs
    else:
        count = stage(name)[2]
        up_row_ref, up_col_ref, up_couple_ref, nodes_ref, msg_ref, recv_ref = refs[count:]
        gather_parts(me_ref[0], name, refs[:count], recv_ref)
    tables = (up_row_ref, up_col_ref, up_couple_ref)
    send(msg_ref, stack(pair_group(name, me_ref, recv_ref, tables, nodes_ref, None)))


def top_levels(recv_ref, top_ref, gram_ref):
    first, second, _, total, energy = rescale(recv_ref)
    potential = mm(jnp.concatenate(first, 1), pair_at(top_ref))
    potential = [lanes(potential, d) for d in range(recv_ref.shape[0])]
    cross = jnp.zeros((RHS, RANK), f32)
    summed = []
    for d in range(recv_ref.shape[0]):
        moved = mm(potential[d], pair_at(gram_ref, d))
        cross = cross + potential[d] * (2.0 * second[d] + moved)
        summed.append(second[d] + moved)
    energy = column_of(energy) + jnp.sum(cross, axis=1, keepdims=True)
    return potential, summed, column_of(total), energy


def middle_kernel(
    me_ref,
    rows_ref,
    part0_ref,
    part1_ref,
    part2_ref,
    part3_ref,
    core_path_ref,
    core_own_ref,
    row_path_ref,
    row_own_ref,
    mid_path_ref,
    mid_own_ref,
    gain_ref,
    up_row_ref,
    top_ref,
    core_nodes_ref,
    row_nodes_ref,
    mid_nodes_ref,
    dense_ref,
    row_basis_ref,
    col_basis_ref,
    cross_ref,
    columns_ref,
    images_ref,
    x_ref,
    own_in_ref,
    within_ref,
    v_ref,
    next_ref,
    alpha_ref,
    rho_ref,
    msg_ref,
    top_gram_ref,
    a_ref,
    b_ref,
    recv_ref,
):
    me = me_ref[0]
    gather_parts(me, "far", (part0_ref, part1_ref, part2_ref, part3_ref), recv_ref)
    place = place_of(me, "far")
    base = 2 * RHS + 8
    for d in range(recv_ref.shape[0]):
        gram = unpack(recv_ref[d, base : base + HALF], recv_ref[d, base + HALF : base + HALF + 1])
        store_pair(top_gram_ref, d, gram)
    potential, summed, squares, energy = top_levels(recv_ref, top_ref, top_gram_ref)
    alpha = jnp.sqrt(squares)
    rho = jnp.sqrt(energy)
    alpha_ref[...] = jnp.broadcast_to(alpha, (RHS, RANK))
    rho_ref[...] = jnp.broadcast_to(rho, (RHS, RANK))
    scale = inverse_norm(squares)
    for d in range(recv_ref.shape[0]):
        a_ref[d] = potential[d]
        b_ref[d] = summed[d]
    forward = a_ref[place]
    siblings = {6: b_ref[place ^ 1]}
    for k, value in enumerate(climb(summed, pair_at(up_row_ref, 6))):
        a_ref[4 + k] = value
    siblings[7] = a_ref[4 + ((place >> 1) ^ 1)]
    for name, path_ref, part_ref, nodes_ref in (
        ("mid", mid_path_ref, mid_own_ref, mid_nodes_ref),
        ("row", row_path_ref, row_own_ref, row_nodes_ref),
        ("core", core_path_ref, core_own_ref, core_nodes_ref),
    ):
        level, heights, _ = stage(name)
        factor = scale / inverse_norm(column_of(part_ref[:1]))
        inside = place_of(me, name)
        for height in reversed(range(heights)):
            j = level + height
            child = (me >> j) & 1
            spread = mm(forward, pair_at(up_row_ref, j), transposed=True)
            low = spread[:, :RANK]
            high = spread[:, RANK:]
            forward = path_ref[3 * height] * factor + jnp.where(child == 0, low, high)
            other = path_ref[3 * height + 1] * factor + jnp.where(child == 0, high, low)
            gram = pair_at(nodes_ref, bases(name)[height] + ((inside >> height) ^ 1))
            siblings[j] = path_ref[3 * height + 2] * factor + mm(other, gram)
    backward = from_siblings([siblings[j] for j in range(8)], gain_ref)
    own_factor = scale / inverse_norm(column_of(own_in_ref[:1]))
    inverse = 1.0 / rho
    spread = mm(backward, pair_at(columns_ref), transposed=True)
    spread = spread + mm(forward, pair_at(images_ref))
    parts = []
    for q in range(LEAF_DEV):
        v = x_ref[:, col_part(q)] * scale
        v_ref[:, col_part(q)] = v
        x = spread[:, col_part(q)] + within_ref[:, col_part(q)] * own_factor
        x = x * inverse - rho * v
        next_ref[:, col_part(q)] = x
        parts.append(x)
    local = (dense_ref, row_basis_ref, col_basis_ref, cross_ref, columns_ref, None, images_ref)
    pair_up(parts, local, rows_ref, msg_ref, None, None, [])


def final_kernel(
    me_ref,
    part0_ref,
    part1_ref,
    part2_ref,
    part3_ref,
    top_ref,
    top_gram_ref,
    beta_ref,
    alpha_ref,
    rho_ref,
    v_ref,
    x_ref,
    out_ref,
    recv_ref,
):
    gather_parts(me_ref[0], "far", (part0_ref, part1_ref, part2_ref, part3_ref), recv_ref)
    _, _, squares, energy = top_levels(recv_ref, top_ref, top_gram_ref)
    theta = jnp.sqrt(squares)
    rho2 = jnp.sqrt(energy - squares)
    rho = rho_ref[:, :1]
    phi = alpha_ref[:, :1] / rho * beta_ref[:, :1]
    v = v_ref[...]
    search = x_ref[...] * inverse_norm(squares) - (theta / rho) * v
    out_ref[...] = (phi / rho) * v - (phi * (theta / rho2) / rho2) * search


def call(kernel, outs, operands, scratch=(), far=(), limit=VMEM_LIMIT):
    spaces = []
    for index, operand in enumerate(operands):
        space = pltpu.SMEM if operand.dtype == jnp.int32 else pltpu.VMEM
        spaces.append(pl.ANY if index in far else space)
    outs = [shape if isinstance(shape, jax.ShapeDtypeStruct) else jax.ShapeDtypeStruct(shape, f32) for shape in outs]
    return pl.pallas_call(
        kernel,
        out_shape=outs,
        in_specs=[pl.BlockSpec(memory_space=space) for space in spaces],
        out_specs=[pl.BlockSpec(memory_space=pltpu.VMEM)] * len(outs),
        scratch_shapes=[
            pltpu.VMEM(shape, f32) if isinstance(shape, tuple) else shape for shape in scratch
        ],
        compiler_params=pltpu.CompilerParams(vmem_limit_bytes=limit),
        cost_estimate=pl.CostEstimate(flops=COST_FLOPS, bytes_accessed=0, transcendentals=0),
    )(*operands)


def device_groups(devices, stride, size):
    out = []
    for base in range(devices):
        if (base // stride) % size == 0:
            out.append([base + k * stride for k in range(size)])
    return out


def local_program(
    devices,
    rhs,
    box_rows,
    dense,
    row_basis,
    col_basis,
    local_col,
    local_row,
    local_couple,
    up_col,
    up_row,
    up_couple,
):
    me = lax.axis_index("leaf").astype(jnp.int32).reshape(1)

    def swap_parts(message, name):
        level, _, count = stage(name)
        parts = [message]
        for k in ORDER[1:count]:
            pairs = [(i, i ^ (k << level)) for i in range(devices)]
            parts.append(lax.ppermute(message, "leaf", pairs))
        return parts

    def swap_mid(message):
        level, _, count = stage("mid")
        groups = device_groups(devices, 1 << level, count)
        return lax.all_to_all(message, "leaf", 0, 0, axis_index_groups=groups)

    tile = (RHS, RANK)
    row_shape = (RHS, LEAF_DEV * LEAF_ROWS)
    col_shape = (RHS, LEAF_DEV * LEAF_COLS)
    single = (RHS + 8, RANK)
    double = (2 * RHS + 8, RANK)

    def longer(shape, rows):
        return (shape[0] + rows, shape[1])

    stat = (8, RANK)
    gram_shape = (RANK, RANK)
    tables = [up_row, up_col, up_couple]

    def nodes_shape(count):
        return jax.ShapeDtypeStruct((2, count) + gram_shape, bf16)

    def path_shape(name):
        return (3 * stage(name)[1],) + tile

    def sibling_shape(name):
        return (stage(name)[1],) + tile

    def nodes_of(name):
        return nodes_shape(node_count(name))

    def node_scratch(name, count=1):
        return [(node_count(name),) + tile] * count

    def received(name, shape):
        return [(stage(name)[2],) + shape]

    groups = stage("mid")[2]

    z, message = call(
        start_kernel,
        [row_shape, (1,) + longer(single, HALF)],
        [me, box_rows, rhs, row_basis, local_row],
        [pltpu.SMEM(box_rows.shape, jnp.int32)]
        + [k.shape for k in (rhs, row_basis, local_row)]
        + [pltpu.SemaphoreType.DMA((4,))],
        range(1, 5),
        START_LIMIT,
    )
    def pair_shape(*shape):
        return jax.ShapeDtypeStruct((2,) + shape, bf16)

    def within(y, earlier):
        operands = [earlier, y, dense, row_basis, col_basis, cross]
        return call(inner_kernel, [col_shape], operands, (), (0,))[0]

    parts = swap_parts(message, "core")
    parts[0] = call(own_kernel, [message.shape], [message])[0]
    message, core_sib, core_nodes = call(
        core_kernel,
        [(1,) + longer(single, HALF), sibling_shape("core"), nodes_of("core")],
        [me] + parts + [up_row],
        received("core", longer(single, HALF)) + node_scratch("core"),
    )
    def products_of(name):
        count = node_count(name)
        return [pair_shape(count, RANK, RANK)] * 2

    cross, columns, paths, *products = call(
        paths_kernel,
        [
            pair_shape(LEAF_DEV * RANK, LEAF_DEV * RANK),
            pair_shape(LEAF_DEV * LEAF_COLS, RANK),
            pair_shape(LEAF_DEV * RANK, RANK),
        ]
        + products_of("row"),
        [message, col_basis, local_row, local_col, local_couple, up_row],
        (),
        (0,),
    )
    (gain,) = call(gains_kernel, [nodes_shape(8)], [me, paths, up_col, up_couple], (), (1,))
    message, row_sib, row_nodes = call(
        row_kernel,
        [(groups,) + longer(single, SLICE), sibling_shape("row"), nodes_of("row")],
        [me] + products + swap_parts(message, "row") + [up_row, gain],
        received("row", longer(single, HALF)) + node_scratch("row") + [(HALF, RANK)],
        (8,),
    )
    message, mid_sib, part, diagonal = call(
        mid_kernel,
        [(1,) + single, sibling_shape("mid"), (HALF, RANK), stat],
        [me, swap_mid(message), up_row],
        node_scratch("mid"),
    )
    x, beta, message, own, inner = call(
        first_kernel,
        [col_shape, tile, (1,) + longer(double, HALF), stat, row_shape],
        [me, box_rows]
        + swap_parts(message, "far")
        + [core_sib, row_sib, mid_sib]
        + [gain]
        + [part, up_row, dense, row_basis, col_basis, cross, columns, paths, within(z, message)],
        [(2,) + tile] + received("far", single),
    )
    message, core_path, core_own = call(
        core_pair_kernel,
        [(1,) + longer(double, 2 * HALF), path_shape("core"), stat],
        [me] + swap_parts(message, "core") + tables + [core_nodes],
        received("core", longer(double, HALF)) + node_scratch("core", 2),
    )
    images, top, *products = call(
        images_kernel,
        [pair_shape(RANK, LEAF_DEV * LEAF_COLS), pair_shape(4 * RANK, 4 * RANK)] + products_of("mid"),
        [message, box_rows, dense, row_basis, col_basis, cross, paths] + tables,
        (),
        (0,),
    )
    message, row_path, row_own, mid_nodes, gram = call(
        row_pair_kernel,
        [(groups,) + double, path_shape("row"), stat, nodes_of("mid"), (HALF + 8, RANK)],
        [me] + products + swap_parts(message, "row") + tables + [row_nodes, diagonal],
        received("row", longer(double, 2 * HALF)) + node_scratch("row", 2),
    )
    message, mid_path, mid_own = call(
        mid_pair_kernel,
        [(1,) + longer(double, HALF + 8), path_shape("mid"), stat],
        [me, swap_mid(message)] + tables + [mid_nodes, gram],
        node_scratch("mid", 2),
    )
    v, x, alpha, rho, message, top_nodes = call(
        middle_kernel,
        [col_shape, col_shape, tile, tile, (1,) + double, nodes_shape(4)],
        [me, box_rows]
        + swap_parts(message, "far")
        + [core_path, core_own, row_path, row_own, mid_path, mid_own]
        + [gain]
        + [up_row, top, core_nodes, row_nodes, mid_nodes]
        + [dense, row_basis, col_basis, cross, columns, images, x, own, within(inner, message)],
        [(6,) + tile, (4,) + tile] + received("far", longer(double, HALF + 8)),
    )
    for name, nodes, peers in (
        ("core", core_nodes, 1),
        ("row", row_nodes, groups),
        ("mid", mid_nodes, 1),
    ):
        parts = [swap_mid(message)] if name == "mid" else swap_parts(message, name)
        (message,) = call(
            functools.partial(last_pair_kernel, name),
            [(peers,) + double],
            [me] + parts + tables + [nodes],
            [] if name == "mid" else received(name, double),
        )
    (out,) = call(
        final_kernel,
        [col_shape],
        [me] + swap_parts(message, "far") + [top, top_nodes, beta, alpha, rho, v, x],
        received("far", double),
    )
    return out


def solution(mesh):
    devices = mesh.shape["leaf"]
    return jax.shard_map(
        functools.partial(local_program, devices),
        mesh=mesh,
        in_specs=(
            P(None, "leaf"),
            P("leaf"),
            P("leaf", None, None),
            P("leaf", None, None),
            P("leaf", None, None),
            P("leaf", None, None),
            P("leaf", None, None),
            P("leaf", None, None, None),
            P(),
            P(),
            P(),
        ),
        out_specs=P(None, "leaf"),
        check_vma=False,
    )
```

```python
import functools

import jax
import jax.numpy as jnp
from jax import lax
from jax.experimental import pallas as pl
from jax.experimental.pallas import tpu as pltpu
from jax.sharding import PartitionSpec as P

RHS = 16
RANK = 128
LEAF_DEV = 4
LEAF_ROWS = 512
LEAF_COLS = 256
HALF = RANK // 2
SLICE = 8
COST_FLOPS = 6000000000
TINY = 1.2e-38
ORDER = (0, 1, 3, 2)
NEAR = 8
STAGES = {"core": (0, 1), "row": (1, 2), "mid": (3, 3), "far": (6, 2)}
VMEM_MIB = 24
VMEM_LIMIT = VMEM_MIB * 1024 * 1024
START_LIMIT = 60 * 1024 * 1024

f32 = jnp.float32
bf16 = jnp.bfloat16


def split(v):
    head = v.astype(bf16)
    return head, (v - head.astype(f32)).astype(bf16)


def mm(x, pair, transposed=False):
    xh, xl = x if isinstance(x, tuple) else split(x)
    wh, wl = pair
    dims = (((1,), (1 if transposed else 0,)), ((), ()))
    n = xh.shape[0]
    both = lax.dot_general(jnp.concatenate([xh, xl], 0), wh, dims, preferred_element_type=f32)
    rest = lax.dot_general(xh, wl, dims, preferred_element_type=f32)
    return both[:n] + (both[n:] + rest)


def mm_square(x, pair):
    xh, xl = x
    wh, wl = pair
    upper = jnp.concatenate([wh, wl], 1)
    lower = jnp.concatenate([wh, jnp.zeros_like(wl)], 1)
    out = jnp.dot(
        jnp.concatenate([xh, xl], 1), jnp.concatenate([upper, lower], 0), preferred_element_type=f32
    )
    return out[:, :RANK] + out[:, RANK:]


def mm_narrow(x, pair):
    xh, xl = split(x)
    wh, wl = pair
    out = jnp.dot(xh, jnp.concatenate([wh, wl], 1), preferred_element_type=f32)
    rest = jnp.dot(xl, wh, preferred_element_type=f32)
    return out[:, :RANK] + (out[:, RANK:] + rest)


def mm_inner(a, b):
    ah, al = split(a)
    bh, bl = split(b)
    dims = (((0,), (0,)), ((), ()))
    m = a.shape[1]
    both = lax.dot_general(jnp.concatenate([ah, al], 1), bh, dims, preferred_element_type=f32)
    rest = lax.dot_general(ah, bl, dims, preferred_element_type=f32)
    return both[:m] + (both[m:] + rest)


def gram_of(a):
    high, low = split(a)
    dims = (((0,), (0,)), ((), ()))
    rest = lax.dot_general(high, low, dims, preferred_element_type=f32)
    return lax.dot_general(high, high, dims, preferred_element_type=f32) + (rest + jnp.transpose(rest))


def pair_at(ref, *index):
    if ref.dtype == bf16:
        return ref[(0,) + index], ref[(1,) + index]
    return split(ref[index])


def half_of(ref, j, child):
    return pair_at(ref, j, pl.ds(pl.multiple_of(child * RANK, RANK), RANK))


def eye():
    return (
        lax.broadcasted_iota(jnp.int32, (RHS, RANK), 0)
        == lax.broadcasted_iota(jnp.int32, (RHS, RANK), 1)
    ).astype(f32)


def stat_block(*values):
    rows = lax.broadcasted_iota(jnp.int32, (8, RANK), 0)
    block = jnp.where(rows == 0, values[0], 0.0)
    for k in range(1, len(values)):
        block = jnp.where(rows == k, values[k], block)
    return block


def column_of(row):
    return jnp.sum(row * eye(), axis=1, keepdims=True)


def row_of(column):
    return jnp.sum(column * eye(), axis=0, keepdims=True)


def inverse_norm(squares):
    return jnp.where(squares >= TINY, 1.0 / jnp.sqrt(squares), 1.0)


def sum_squares(v):
    return jnp.sum(v * v, axis=1, keepdims=True)


def send(out_ref, value):
    for peer in range(out_ref.shape[0]):
        out_ref[peer] = value


def stack(blocks):
    return jnp.concatenate(blocks, 0)


def unstack(value, count):
    size = value.shape[0] // count
    return [value[k * size : (k + 1) * size] for k in range(count)]


def climb(blocks, transfer):
    count = len(blocks) // 2
    paired = [jnp.concatenate([blocks[2 * m], blocks[2 * m + 1]], 1) for m in range(count)]
    return unstack(mm(stack(paired), transfer), count)


def descend(blocks, transfer):
    spread = unstack(mm(stack(blocks), transfer, transposed=True), len(blocks))
    out = []
    for block in spread:
        out += [block[:, :RANK], block[:, RANK:]]
    return out


def couple_all(blocks, coupling):
    count = len(blocks) // 2
    even = unstack(mm(stack(blocks[1::2]), coupling[0]), count)
    odd = unstack(mm(stack(blocks[0::2]), coupling[1]), count)
    out = []
    for m in range(count):
        out += [even[m], odd[m]]
    return out


def lanes(value, k):
    return value[:, k * RANK : (k + 1) * RANK]


def live_mask(rows_ref, q):
    slots = lax.broadcasted_iota(jnp.int32, (RHS, LEAF_ROWS), 1)
    return (slots < rows_ref[q]).astype(f32)


def row_part(q):
    return slice(q * LEAF_ROWS, (q + 1) * LEAF_ROWS)


def col_part(q):
    return slice(q * LEAF_COLS, (q + 1) * LEAF_COLS)


def pair_up(parts, local, rows_ref, msg_ref, own_ref, inner_ref, extra):
    dense_ref, row_basis_ref, col_basis_ref, cross_ref, columns_ref, paths_ref, images_ref = local
    squares = sum_squares(parts[0])
    for part in parts[1:]:
        squares = squares + sum_squares(part)
    scale = inverse_norm(squares)
    whole = jnp.concatenate(parts, 1)
    root = mm(whole, pair_at(columns_ref)) * scale
    leaf = [mm(parts[q], pair_at(col_basis_ref, q)) for q in range(LEAF_DEV)]
    down = mm(jnp.concatenate(leaf, 1), pair_at(cross_ref))
    energy = jnp.zeros((RHS, 1), f32)
    rows = []
    for q in range(LEAF_DEV):
        y = mm(parts[q], pair_at(dense_ref, q), transposed=True)
        y = y + mm(lanes(down, q), pair_at(row_basis_ref, q), transposed=True)
        y = y * (live_mask(rows_ref, q) * scale)
        if inner_ref is not None:
            inner_ref[:, row_part(q)] = y
        energy = energy + sum_squares(y)
        if images_ref is None:
            rows.append(mm(y, pair_at(row_basis_ref, q)))
    if images_ref is None:
        row_root = mm(jnp.concatenate(rows, 1), pair_at(paths_ref))
    else:
        row_root = mm(whole * scale, pair_at(images_ref), transposed=True)
    stats = stat_block(row_of(squares), row_of(energy))
    if own_ref is not None:
        own_ref[...] = stats
    send(msg_ref, stack([root, row_root, stats] + extra))


def paths_kernel(
    order_ref,
    col_basis_ref,
    local_row_ref,
    local_col_ref,
    local_couple_ref,
    up_row_ref,
    cross_ref,
    columns_ref,
    paths_ref,
    products_ref,
    turned_ref,
):
    del order_ref
    store_products("row", up_row_ref, products_ref, turned_ref)
    halves = [slice(0, RANK), slice(RANK, 2 * RANK)]

    def store(ref, index, value):
        high, low = split(value)
        ref[(0,) + index] = high
        ref[(1,) + index] = low

    def part(q, size=RANK):
        return slice(q * size, (q + 1) * size)

    for q in range(LEAF_DEV):
        m, i = q // 2, q % 2
        store(cross_ref, (part(q), part(q)), jnp.zeros((RANK, RANK), f32))
        store(cross_ref, (part(q), part(q ^ 1)), local_couple_ref[m, 1 - i])
        gained = mm_square(pair_at(local_col_ref, m, halves[i]), pair_at(local_couple_ref, 2, 1 - m))
        spread = mm(gained, pair_at(local_row_ref, 1 - m), transposed=True)
        store(cross_ref, (part(q), slice(2 * (1 - m) * RANK, 2 * (2 - m) * RANK)), spread)
        row_path = mm_square(pair_at(local_row_ref, m, halves[i]), pair_at(local_row_ref, 2, halves[m]))
        store(paths_ref, (part(q),), row_path)
        path = mm_square(pair_at(local_col_ref, m, halves[i]), pair_at(local_col_ref, 2, halves[m]))
        store(columns_ref, (part(q, LEAF_COLS),), mm_square(pair_at(col_basis_ref, q), split(path)))


def store_top(up_row_ref, up_col_ref, up_couple_ref, top_ref):
    def store(source, target, value):
        high, low = split(value)
        rows = slice(source * RANK, (source + 1) * RANK)
        cols = slice(target * RANK, target * RANK + value.shape[1])
        top_ref[0, rows, cols] = high
        top_ref[1, rows, cols] = low

    for p in range(4):
        m, i = p // 2, p % 2
        store(p, p, jnp.zeros((RANK, RANK), f32))
        store(p, p ^ 1, up_couple_ref[6, 1 - i])
        half = up_col_ref[6, i * RANK : (i + 1) * RANK]
        gained = mm(half, pair_at(up_couple_ref, 7, 1 - m))
        store(p, 2 * (1 - m), mm(gained, pair_at(up_row_ref, 6), transposed=True))


def images_kernel(
    order_ref,
    rows_ref,
    dense_ref,
    row_basis_ref,
    col_basis_ref,
    cross_ref,
    paths_ref,
    up_row_ref,
    up_col_ref,
    up_couple_ref,
    images_ref,
    top_ref,
    products_ref,
    turned_ref,
):
    del order_ref
    store_products("mid", up_row_ref, products_ref, turned_ref)
    store_top(up_row_ref, up_col_ref, up_couple_ref, top_ref)
    turned = []
    images = []
    moved = []
    for q in range(LEAF_DEV):
        path = pair_at(paths_ref, slice(q * RANK, (q + 1) * RANK))
        turned.append(jnp.transpose(path[0].astype(f32) + path[1].astype(f32)))
        slots = lax.broadcasted_iota(jnp.int32, (LEAF_ROWS, RANK), 0)
        basis = jnp.where(slots < rows_ref[q], row_basis_ref[q], 0.0)
        images.append(mm_inner(basis, dense_ref[q]))
        moved.append(mm_square(split(turned[q]), split(gram_of(basis))))
    inner = mm(jnp.concatenate(moved, 1), pair_at(cross_ref), transposed=True)
    for q in range(LEAF_DEV):
        image = mm(turned[q], split(images[q]))
        image = image + mm(lanes(inner, q), pair_at(col_basis_ref, q), transposed=True)
        high, low = split(image)
        images_ref[0, :, col_part(q)] = high
        images_ref[1, :, col_part(q)] = low


def inner_kernel(order_ref, y_ref, dense_ref, row_basis_ref, col_basis_ref, cross_ref, x_ref):
    del order_ref
    leaf = [mm(y_ref[:, row_part(q)], pair_at(row_basis_ref, q)) for q in range(LEAF_DEV)]
    down = mm(jnp.concatenate(leaf, 1), pair_at(cross_ref), transposed=True)
    for q in range(LEAF_DEV):
        x = mm(y_ref[:, row_part(q)], pair_at(dense_ref, q))
        x_ref[:, col_part(q)] = x + mm(lanes(down, q), pair_at(col_basis_ref, q), transposed=True)


def both_sides(grams, half):
    turned = split(jnp.transpose(half[0].astype(f32) + half[1].astype(f32)))
    return [mm_square(split(mm_square(turned, split(gram))), half) for gram in grams]


def gram_climb(grams, transfer):
    even = both_sides(grams[0::2], (transfer[0][:RANK], transfer[1][:RANK]))
    odd = both_sides(grams[1::2], (transfer[0][RANK:], transfer[1][RANK:]))
    return [a + b for a, b in zip(even, odd)]


def pack(gram):
    row = lax.broadcasted_iota(jnp.int32, (HALF, RANK), 0)
    col = lax.broadcasted_iota(jnp.int32, (HALF, RANK), 1)
    last = gram[HALF:]
    top = jnp.where((col < HALF) & (col > row), pltpu.roll(last, HALF, 1), gram[:HALF])
    diagonal = jnp.sum(jnp.where(col - HALF == row, last, 0.0), axis=0, keepdims=True)
    return top, diagonal


def unpack(top, diagonal):
    row = lax.broadcasted_iota(jnp.int32, (HALF, RANK), 0)
    col = lax.broadcasted_iota(jnp.int32, (HALF, RANK), 1)
    upper = jnp.where((col >= HALF) | (col < row), top, jnp.where(col == row, 0.5 * top, 0.0))
    lower = jnp.where(
        col - HALF > row,
        pltpu.roll(top, HALF, 1),
        jnp.where(col - HALF == row, 0.5 * diagonal, 0.0),
    )
    part = stack([upper, lower])
    return part + jnp.transpose(part)


def stage(name):
    level, heights = STAGES[name]
    return level, heights, 1 << heights


def place_of(me, name):
    level, _, count = stage(name)
    return (me >> level) % count


def bases(name):
    _, heights, count = stage(name)
    return [sum(count >> k for k in range(height)) for height in range(heights)]


def node_count(name):
    return 2 * stage(name)[2] - 2


def gather_parts(me, name, parts, out_ref):
    for k, part in zip(ORDER, parts):
        out_ref[place_of(me, name) ^ k] = part[0]


def store_pair(ref, index, value):
    high, low = split(value)
    ref[0, index] = high
    ref[1, index] = low


def group_grams(name, grams, up_row_ref, nodes_ref):
    for height, base in enumerate(bases(name)):
        for k, value in enumerate(grams):
            store_pair(nodes_ref, base + k, value)
        grams = gram_climb(grams, pair_at(up_row_ref, stage(name)[0] + height))
    return grams[0]


def product_base(height):
    return (2 << height) - 2


def store_products(name, up_row_ref, products_ref, turned_ref):
    level, heights, _ = stage(name)
    products = None
    for height in range(heights):
        halves = [half_of(up_row_ref, level + height, child) for child in range(2)]
        if products is None:
            products = [half[0].astype(f32) + half[1].astype(f32) for half in halves]
        else:
            products = [mm_square(split(product), half) for half in halves for product in products]
        for k, product in enumerate(products):
            store_pair(products_ref, product_base(height) + k, product)
            store_pair(turned_ref, product_base(height) + k, jnp.transpose(product))


def member_grams(name, grams, products_ref, turned_ref, nodes_ref):
    _, heights, count = stage(name)
    left = []
    for d in range(count):
        store_pair(nodes_ref, d, grams[d])
        turned = [pair_at(turned_ref, product_base(h) + d % (2 << h)) for h in range(heights)]
        turned = tuple(stack([term[k] for term in turned]) for k in range(2))
        left.append(unstack(mm_square(turned, split(grams[d])), heights))
    for height in range(heights):
        size = 2 << height
        base = product_base(height)
        terms = [pair_at(products_ref, base + t) for t in range(size)]
        table = tuple(stack([term[k] for term in terms]) for k in range(2))
        rows = []
        for n in range(count // size):
            rows.append(jnp.concatenate([left[n * size + t][height] for t in range(size)], 1))
        nodes = unstack(mm_narrow(stack(rows), table), len(rows))
        if height + 1 < heights:
            for k, value in enumerate(nodes):
                store_pair(nodes_ref, bases(name)[height + 1] + k, value)
    return nodes[0]


def start_copies(pairs, sems):
    copies = [
        pltpu.make_async_copy(source, target, sems.at[k])
        for k, (source, target) in enumerate(pairs)
    ]
    for copy in copies:
        copy.start()
    return copies


def start_kernel(
    me_ref,
    rows_hbm,
    rhs_hbm,
    row_basis_hbm,
    local_row_hbm,
    z_ref,
    msg_ref,
    rows_ref,
    rhs_ref,
    row_basis_ref,
    local_row_ref,
    sems,
):
    pairs = [(rows_hbm, rows_ref), (rhs_hbm, rhs_ref)]
    pairs += [(row_basis_hbm, row_basis_ref), (local_row_hbm, local_row_ref)]
    for copy in start_copies(pairs, sems):
        copy.wait()
    squares = jnp.zeros((RHS, 1), f32)
    paths = []
    for q in range(LEAF_DEV):
        m, i = q // 2, q % 2
        top = split(local_row_ref[2, m * RANK : (m + 1) * RANK])
        paths.append(mm_square(pair_at(local_row_ref, m, slice(i * RANK, (i + 1) * RANK)), top))
    leaf = []
    grams = []
    for q in range(LEAF_DEV):
        part = rhs_ref[:, row_part(q)] * live_mask(rows_ref, q)
        z_ref[:, row_part(q)] = part
        squares = squares + sum_squares(part)
        leaf.append(mm(part, split(row_basis_ref[q])))
    for q in range(LEAF_DEV):
        slots = lax.broadcasted_iota(jnp.int32, (LEAF_ROWS, RANK), 0)
        basis = jnp.where(slots < rows_ref[q], row_basis_ref[q], 0.0)
        grams.append(gram_of(basis))
    root = mm(jnp.concatenate(leaf, 1), split(stack(paths)))
    row = row_of(squares)
    left = [mm_square(split(jnp.transpose(paths[q])), split(grams[q])) for q in range(LEAF_DEV)]
    gram = mm_narrow(jnp.concatenate(left, 1), split(stack(paths)))
    top, diagonal = pack(gram)
    send(msg_ref, stack([root, stat_block(row, row, diagonal), top]))


def sum_stats(recv_ref):
    stats = recv_ref[0, RHS : RHS + 8]
    for d in range(1, recv_ref.shape[0]):
        stats = stats + recv_ref[d, RHS : RHS + 8]
    return stats


def climb_group(name, me_ref, recv_ref, climb_ref, sib_ref, scratch_ref):
    level = stage(name)[0]
    place = place_of(me_ref[0], name)
    summaries = [recv_ref[d, :RHS] for d in range(recv_ref.shape[0])]
    for height, base in enumerate(bases(name)):
        for m, value in enumerate(summaries):
            scratch_ref[base + m] = value
        sib_ref[height] = scratch_ref[base + ((place >> height) ^ 1)]
        summaries = climb(summaries, pair_at(climb_ref, level + height))
    return summaries[0]


def received_grams(recv_ref):
    base = RHS + 8
    count = recv_ref.shape[0]
    return [unpack(recv_ref[d, base:], recv_ref[d, RHS + 2 : RHS + 3]) for d in range(count)]


def own_kernel(message_ref, out_ref):
    out_ref[...] = message_ref[...]


def path_product(me, level, path, up_col_ref):
    half = half_of(up_col_ref, level, (me >> level) & 1)
    return mm_square(split(path), half)


def sibling_gain(me, level, path, up_couple_ref):
    child = 1 - ((me >> level) & 1)
    return mm_square(split(path), pair_at(up_couple_ref, level, child))


def core_kernel(
    me_ref,
    part0_ref,
    part1_ref,
    up_row_ref,
    msg_ref,
    sib_ref,
    nodes_ref,
    recv_ref,
    scratch_ref,
):
    gather_parts(me_ref[0], "core", (part0_ref, part1_ref), recv_ref)
    summary = climb_group("core", me_ref, recv_ref, up_row_ref, sib_ref, scratch_ref)
    top, diagonal = pack(group_grams("core", received_grams(recv_ref), up_row_ref, nodes_ref))
    stats = sum_stats(recv_ref)
    send(msg_ref, stack([summary, stat_block(stats[:1], stats[1:2], diagonal), top]))


def row_kernel(
    me_ref,
    products_ref,
    turned_ref,
    part0_ref,
    part1_ref,
    part2_ref,
    part3_ref,
    up_row_ref,
    order_ref,
    msg_ref,
    sib_ref,
    nodes_ref,
    recv_ref,
    scratch_ref,
    slice_ref,
):
    del order_ref
    me = me_ref[0]
    gather_parts(me, "row", (part0_ref, part1_ref, part2_ref, part3_ref), recv_ref)
    summary = climb_group("row", me_ref, recv_ref, up_row_ref, sib_ref, scratch_ref)
    gram = member_grams("row", received_grams(recv_ref), products_ref, turned_ref, nodes_ref)
    top, diagonal = pack(gram)
    slice_ref[...] = top
    part = slice_ref[pl.ds(pl.multiple_of((me % NEAR) * SLICE, SLICE), SLICE), :]
    stats = sum_stats(recv_ref)
    send(msg_ref, stack([summary, stat_block(stats[:1], stats[1:2], diagonal), part]))


def mid_kernel(
    me_ref,
    recv_ref,
    up_row_ref,
    msg_ref,
    sib_ref,
    part_ref,
    diagonal_ref,
    scratch_ref,
):
    count = stage("mid")[2]
    summary = climb_group("mid", me_ref, recv_ref, up_row_ref, sib_ref, scratch_ref)
    for d in range(count):
        part_ref[d * SLICE : (d + 1) * SLICE] = recv_ref[d, RHS + 8 :]
        diagonal_ref[d : d + 1] = recv_ref[d, RHS + 2 : RHS + 3]
    send(msg_ref, stack([summary, sum_stats(recv_ref)]))


def gains_kernel(me_ref, order_ref, up_col_ref, up_couple_ref, gain_ref):
    del order_ref
    me = me_ref[0]
    store_pair(gain_ref, 0, up_couple_ref[0, 1 - (me & 1)])
    path = up_col_ref[0, pl.ds(pl.multiple_of((me & 1) * RANK, RANK), RANK), :]
    for j in range(1, 8):
        store_pair(gain_ref, j, sibling_gain(me, j, path, up_couple_ref))
        if j < 7:
            path = path_product(me, j, path, up_col_ref)


def from_siblings(siblings, gain_ref):
    gains = [pair_at(gain_ref, j) for j in range(8)]
    gains = tuple(jnp.concatenate([g[k] for g in gains], 1) for k in range(2))
    return mm(jnp.concatenate(siblings, 1), gains, transposed=True)


def first_kernel(
    me_ref,
    rows_ref,
    part0_ref,
    part1_ref,
    part2_ref,
    part3_ref,
    core_sib_ref,
    row_sib_ref,
    mid_sib_ref,
    gain_ref,
    part_ref,
    up_row_ref,
    dense_ref,
    row_basis_ref,
    col_basis_ref,
    cross_ref,
    columns_ref,
    paths_ref,
    within_ref,
    x_ref,
    beta_ref,
    msg_ref,
    own_ref,
    inner_ref,
    scratch_ref,
    recv_ref,
):
    me = me_ref[0]
    gather_parts(me, "far", (part0_ref, part1_ref, part2_ref, part3_ref), recv_ref)
    place = place_of(me, "far")
    summaries = [recv_ref[d, :RHS] for d in range(recv_ref.shape[0])]
    siblings = [core_sib_ref[0]] + [row_sib_ref[j] for j in range(2)] + [mid_sib_ref[j] for j in range(3)]
    siblings.append(recv_ref[place ^ 1, :RHS])
    summaries = climb(summaries, pair_at(up_row_ref, 6))
    for m, value in enumerate(summaries):
        scratch_ref[m] = value
    siblings.append(scratch_ref[(place >> 1) ^ 1])
    potential = from_siblings(siblings, gain_ref)
    beta = jnp.sqrt(column_of(sum_stats(recv_ref)[:1]))
    inverse = 1.0 / beta
    beta_ref[...] = jnp.broadcast_to(beta, (RHS, RANK))
    spread = mm(potential, pair_at(columns_ref), transposed=True)
    parts = []
    for q in range(LEAF_DEV):
        x = (within_ref[:, col_part(q)] + spread[:, col_part(q)]) * inverse
        x_ref[:, col_part(q)] = x
        parts.append(x)
    local = (dense_ref, row_basis_ref, col_basis_ref, cross_ref, columns_ref, paths_ref, None)
    pair_up(parts, local, rows_ref, msg_ref, own_ref, inner_ref, [part_ref[...]])


def rescale(recv_ref):
    base = 2 * RHS
    squares = stack([recv_ref[d, base : base + 1] for d in range(recv_ref.shape[0])])
    energy = stack([recv_ref[d, base + 1 : base + 2] for d in range(recv_ref.shape[0])])
    total = jnp.sum(squares, axis=0, keepdims=True)
    factor = inverse_norm(total) / inverse_norm(squares)
    energy = jnp.sum(energy * factor * factor, axis=0, keepdims=True)
    first = []
    second = []
    for d in range(recv_ref.shape[0]):
        column = column_of(factor[d : d + 1])
        first.append(recv_ref[d, :RHS] * column)
        second.append(recv_ref[d, RHS : 2 * RHS] * column)
    return first, second, factor, total, energy


def pair_group(name, me_ref, recv_ref, tables, nodes_ref, keep):
    up_row_ref, up_col_ref, up_couple_ref = tables
    level = stage(name)[0]
    place = place_of(me_ref[0], name)
    first, second, _, total, energy = rescale(recv_ref)
    cross = jnp.zeros((RHS, RANK), f32)
    for height, base in enumerate(bases(name)):
        j = level + height
        gained = couple_all(first, (pair_at(up_couple_ref, j, 0), pair_at(up_couple_ref, j, 1)))
        summed = []
        for k in range(len(first)):
            moved = mm(gained[k], pair_at(nodes_ref, base + k))
            cross = cross + gained[k] * (2.0 * second[k] + moved)
            summed.append(second[k] + moved)
        if keep is not None:
            path_ref, gain_ref, below_ref = keep
            for k in range(len(first)):
                gain_ref[base + k] = gained[k]
                below_ref[base + k] = second[k]
            own = base + (place >> height)
            other = base + ((place >> height) ^ 1)
            path_ref[3 * height] = gain_ref[own]
            path_ref[3 * height + 1] = gain_ref[other]
            path_ref[3 * height + 2] = below_ref[other]
        first = climb(first, pair_at(up_col_ref, j))
        second = climb(summed, pair_at(up_row_ref, j))
    energy = energy + row_of(jnp.sum(cross, axis=1, keepdims=True))
    return first[0], second[0], stat_block(total, energy)


def core_pair_kernel(
    me_ref,
    part0_ref,
    part1_ref,
    up_row_ref,
    up_col_ref,
    up_couple_ref,
    nodes_ref,
    msg_ref,
    path_ref,
    own_ref,
    recv_ref,
    gain_ref,
    below_ref,
):
    gather_parts(me_ref[0], "core", (part0_ref, part1_ref), recv_ref)
    tables = (up_row_ref, up_col_ref, up_couple_ref)
    keep = (path_ref, gain_ref, below_ref)
    first, second, stats = pair_group("core", me_ref, recv_ref, tables, nodes_ref, keep)
    own_ref[...] = stats
    base = 2 * RHS + 8
    send(msg_ref, stack([first, second, stats, recv_ref[0, base:], recv_ref[1, base:]]))


def row_pair_kernel(
    me_ref,
    products_ref,
    turned_ref,
    part0_ref,
    part1_ref,
    part2_ref,
    part3_ref,
    up_row_ref,
    up_col_ref,
    up_couple_ref,
    nodes_ref,
    diagonal_ref,
    msg_ref,
    path_ref,
    own_ref,
    mid_nodes_ref,
    gram_ref,
    recv_ref,
    gain_ref,
    below_ref,
):
    gather_parts(me_ref[0], "row", (part0_ref, part1_ref, part2_ref, part3_ref), recv_ref)
    tables = (up_row_ref, up_col_ref, up_couple_ref)
    keep = (path_ref, gain_ref, below_ref)
    first, second, stats = pair_group("row", me_ref, recv_ref, tables, nodes_ref, keep)
    own_ref[...] = stats
    send(msg_ref, stack([first, second, stats]))
    base = 2 * RHS + 8
    grams = []
    for d in range(stage("mid")[2]):
        slices = []
        for p in range(NEAR):
            low = base + (p % 2) * HALF + d * SLICE
            slices.append(recv_ref[p // 2, low : low + SLICE])
        grams.append(unpack(stack(slices), diagonal_ref[d : d + 1]))
    top, diagonal = pack(member_grams("mid", grams, products_ref, turned_ref, mid_nodes_ref))
    gram_ref[...] = stack([top, stat_block(diagonal)])


def mid_pair_kernel(
    me_ref,
    recv_ref,
    up_row_ref,
    up_col_ref,
    up_couple_ref,
    nodes_ref,
    gram_ref,
    msg_ref,
    path_ref,
    own_ref,
    gain_ref,
    below_ref,
):
    tables = (up_row_ref, up_col_ref, up_couple_ref)
    keep = (path_ref, gain_ref, below_ref)
    first, second, stats = pair_group("mid", me_ref, recv_ref, tables, nodes_ref, keep)
    own_ref[...] = stats
    send(msg_ref, stack([first, second, stats, gram_ref[...]]))


def last_pair_kernel(name, me_ref, *refs):
    if name == "mid":
        recv_ref, up_row_ref, up_col_ref, up_couple_ref, nodes_ref, msg_ref = refs
    else:
        count = stage(name)[2]
        up_row_ref, up_col_ref, up_couple_ref, nodes_ref, msg_ref, recv_ref = refs[count:]
        gather_parts(me_ref[0], name, refs[:count], recv_ref)
    tables = (up_row_ref, up_col_ref, up_couple_ref)
    send(msg_ref, stack(pair_group(name, me_ref, recv_ref, tables, nodes_ref, None)))


def top_levels(recv_ref, top_ref, gram_ref):
    first, second, _, total, energy = rescale(recv_ref)
    potential = mm(jnp.concatenate(first, 1), pair_at(top_ref))
    potential = [lanes(potential, d) for d in range(recv_ref.shape[0])]
    cross = jnp.zeros((RHS, RANK), f32)
    summed = []
    for d in range(recv_ref.shape[0]):
        moved = mm(potential[d], pair_at(gram_ref, d))
        cross = cross + potential[d] * (2.0 * second[d] + moved)
        summed.append(second[d] + moved)
    energy = column_of(energy) + jnp.sum(cross, axis=1, keepdims=True)
    return potential, summed, column_of(total), energy


def middle_kernel(
    me_ref,
    rows_ref,
    part0_ref,
    part1_ref,
    part2_ref,
    part3_ref,
    core_path_ref,
    core_own_ref,
    row_path_ref,
    row_own_ref,
    mid_path_ref,
    mid_own_ref,
    gain_ref,
    up_row_ref,
    top_ref,
    core_nodes_ref,
    row_nodes_ref,
    mid_nodes_ref,
    dense_ref,
    row_basis_ref,
    col_basis_ref,
    cross_ref,
    columns_ref,
    images_ref,
    x_ref,
    own_in_ref,
    within_ref,
    v_ref,
    next_ref,
    alpha_ref,
    rho_ref,
    msg_ref,
    top_gram_ref,
    a_ref,
    b_ref,
    recv_ref,
):
    me = me_ref[0]
    gather_parts(me, "far", (part0_ref, part1_ref, part2_ref, part3_ref), recv_ref)
    place = place_of(me, "far")
    base = 2 * RHS + 8
    for d in range(recv_ref.shape[0]):
        gram = unpack(recv_ref[d, base : base + HALF], recv_ref[d, base + HALF : base + HALF + 1])
        store_pair(top_gram_ref, d, gram)
    potential, summed, squares, energy = top_levels(recv_ref, top_ref, top_gram_ref)
    alpha = jnp.sqrt(squares)
    rho = jnp.sqrt(energy)
    alpha_ref[...] = jnp.broadcast_to(alpha, (RHS, RANK))
    rho_ref[...] = jnp.broadcast_to(rho, (RHS, RANK))
    scale = inverse_norm(squares)
    for d in range(recv_ref.shape[0]):
        a_ref[d] = potential[d]
        b_ref[d] = summed[d]
    forward = a_ref[place]
    siblings = {6: b_ref[place ^ 1]}
    for k, value in enumerate(climb(summed, pair_at(up_row_ref, 6))):
        a_ref[4 + k] = value
    siblings[7] = a_ref[4 + ((place >> 1) ^ 1)]
    for name, path_ref, part_ref, nodes_ref in (
        ("mid", mid_path_ref, mid_own_ref, mid_nodes_ref),
        ("row", row_path_ref, row_own_ref, row_nodes_ref),
        ("core", core_path_ref, core_own_ref, core_nodes_ref),
    ):
        level, heights, _ = stage(name)
        factor = scale / inverse_norm(column_of(part_ref[:1]))
        inside = place_of(me, name)
        for height in reversed(range(heights)):
            j = level + height
            child = (me >> j) & 1
            spread = mm(forward, pair_at(up_row_ref, j), transposed=True)
            low = spread[:, :RANK]
            high = spread[:, RANK:]
            forward = path_ref[3 * height] * factor + jnp.where(child == 0, low, high)
            other = path_ref[3 * height + 1] * factor + jnp.where(child == 0, high, low)
            gram = pair_at(nodes_ref, bases(name)[height] + ((inside >> height) ^ 1))
            siblings[j] = path_ref[3 * height + 2] * factor + mm(other, gram)
    backward = from_siblings([siblings[j] for j in range(8)], gain_ref)
    own_factor = scale / inverse_norm(column_of(own_in_ref[:1]))
    inverse = 1.0 / rho
    spread = mm(backward, pair_at(columns_ref), transposed=True)
    spread = spread + mm(forward, pair_at(images_ref))
    parts = []
    for q in range(LEAF_DEV):
        v = x_ref[:, col_part(q)] * scale
        v_ref[:, col_part(q)] = v
        x = spread[:, col_part(q)] + within_ref[:, col_part(q)] * own_factor
        x = x * inverse - rho * v
        next_ref[:, col_part(q)] = x
        parts.append(x)
    local = (dense_ref, row_basis_ref, col_basis_ref, cross_ref, columns_ref, None, images_ref)
    pair_up(parts, local, rows_ref, msg_ref, None, None, [])


def final_kernel(
    me_ref,
    part0_ref,
    part1_ref,
    part2_ref,
    part3_ref,
    top_ref,
    top_gram_ref,
    beta_ref,
    alpha_ref,
    rho_ref,
    v_ref,
    x_ref,
    out_ref,
    recv_ref,
):
    gather_parts(me_ref[0], "far", (part0_ref, part1_ref, part2_ref, part3_ref), recv_ref)
    _, _, squares, energy = top_levels(recv_ref, top_ref, top_gram_ref)
    theta = jnp.sqrt(squares)
    rho2 = jnp.sqrt(energy - squares)
    rho = rho_ref[:, :1]
    phi = alpha_ref[:, :1] / rho * beta_ref[:, :1]
    v = v_ref[...]
    search = x_ref[...] * inverse_norm(squares) - (theta / rho) * v
    out_ref[...] = (phi / rho) * v - (phi * (theta / rho2) / rho2) * search


def call(kernel, outs, operands, scratch=(), far=(), limit=VMEM_LIMIT):
    spaces = []
    for index, operand in enumerate(operands):
        space = pltpu.SMEM if operand.dtype == jnp.int32 else pltpu.VMEM
        spaces.append(pl.ANY if index in far else space)
    outs = [shape if isinstance(shape, jax.ShapeDtypeStruct) else jax.ShapeDtypeStruct(shape, f32) for shape in outs]
    return pl.pallas_call(
        kernel,
        out_shape=outs,
        in_specs=[pl.BlockSpec(memory_space=space) for space in spaces],
        out_specs=[pl.BlockSpec(memory_space=pltpu.VMEM)] * len(outs),
        scratch_shapes=[
            pltpu.VMEM(shape, f32) if isinstance(shape, tuple) else shape for shape in scratch
        ],
        compiler_params=pltpu.CompilerParams(vmem_limit_bytes=limit),
        cost_estimate=pl.CostEstimate(flops=COST_FLOPS, bytes_accessed=0, transcendentals=0),
    )(*operands)


def device_groups(devices, stride, size):
    out = []
    for base in range(devices):
        if (base // stride) % size == 0:
            out.append([base + k * stride for k in range(size)])
    return out


def local_program(
    devices,
    rhs,
    box_rows,
    dense,
    row_basis,
    col_basis,
    local_col,
    local_row,
    local_couple,
    up_col,
    up_row,
    up_couple,
):
    me = lax.axis_index("leaf").astype(jnp.int32).reshape(1)

    def swap_parts(message, name):
        level, _, count = stage(name)
        parts = [message]
        for k in ORDER[1:count]:
            pairs = [(i, i ^ (k << level)) for i in range(devices)]
            parts.append(lax.ppermute(message, "leaf", pairs))
        return parts

    def swap_mid(message):
        level, _, count = stage("mid")
        groups = device_groups(devices, 1 << level, count)
        return lax.all_to_all(message, "leaf", 0, 0, axis_index_groups=groups)

    tile = (RHS, RANK)
    row_shape = (RHS, LEAF_DEV * LEAF_ROWS)
    col_shape = (RHS, LEAF_DEV * LEAF_COLS)
    single = (RHS + 8, RANK)
    double = (2 * RHS + 8, RANK)

    def longer(shape, rows):
        return (shape[0] + rows, shape[1])

    stat = (8, RANK)
    gram_shape = (RANK, RANK)
    tables = [up_row, up_col, up_couple]

    def nodes_shape(count):
        return jax.ShapeDtypeStruct((2, count) + gram_shape, bf16)

    def path_shape(name):
        return (3 * stage(name)[1],) + tile

    def sibling_shape(name):
        return (stage(name)[1],) + tile

    def nodes_of(name):
        return nodes_shape(node_count(name))

    def node_scratch(name, count=1):
        return [(node_count(name),) + tile] * count

    def received(name, shape):
        return [(stage(name)[2],) + shape]

    groups = stage("mid")[2]

    z, message = call(
        start_kernel,
        [row_shape, (1,) + longer(single, HALF)],
        [me, box_rows, rhs, row_basis, local_row],
        [pltpu.SMEM(box_rows.shape, jnp.int32)]
        + [k.shape for k in (rhs, row_basis, local_row)]
        + [pltpu.SemaphoreType.DMA((4,))],
        range(1, 5),
        START_LIMIT,
    )
    def pair_shape(*shape):
        return jax.ShapeDtypeStruct((2,) + shape, bf16)

    def within(y, earlier):
        operands = [earlier, y, dense, row_basis, col_basis, cross]
        return call(inner_kernel, [col_shape], operands, (), (0,))[0]

    parts = swap_parts(message, "core")
    parts[0] = call(own_kernel, [message.shape], [message])[0]
    message, core_sib, core_nodes = call(
        core_kernel,
        [(1,) + longer(single, HALF), sibling_shape("core"), nodes_of("core")],
        [me] + parts + [up_row],
        received("core", longer(single, HALF)) + node_scratch("core"),
    )
    def products_of(name):
        count = node_count(name)
        return [pair_shape(count, RANK, RANK)] * 2

    cross, columns, paths, *products = call(
        paths_kernel,
        [
            pair_shape(LEAF_DEV * RANK, LEAF_DEV * RANK),
            pair_shape(LEAF_DEV * LEAF_COLS, RANK),
            pair_shape(LEAF_DEV * RANK, RANK),
        ]
        + products_of("row"),
        [message, col_basis, local_row, local_col, local_couple, up_row],
        (),
        (0,),
    )
    (gain,) = call(gains_kernel, [nodes_shape(8)], [me, paths, up_col, up_couple], (), (1,))
    message, row_sib, row_nodes = call(
        row_kernel,
        [(groups,) + longer(single, SLICE), sibling_shape("row"), nodes_of("row")],
        [me] + products + swap_parts(message, "row") + [up_row, gain],
        received("row", longer(single, HALF)) + node_scratch("row") + [(HALF, RANK)],
        (8,),
    )
    message, mid_sib, part, diagonal = call(
        mid_kernel,
        [(1,) + single, sibling_shape("mid"), (HALF, RANK), stat],
        [me, swap_mid(message), up_row],
        node_scratch("mid"),
    )
    x, beta, message, own, inner = call(
        first_kernel,
        [col_shape, tile, (1,) + longer(double, HALF), stat, row_shape],
        [me, box_rows]
        + swap_parts(message, "far")
        + [core_sib, row_sib, mid_sib]
        + [gain]
        + [part, up_row, dense, row_basis, col_basis, cross, columns, paths, within(z, message)],
        [(2,) + tile] + received("far", single),
    )
    message, core_path, core_own = call(
        core_pair_kernel,
        [(1,) + longer(double, 2 * HALF), path_shape("core"), stat],
        [me] + swap_parts(message, "core") + tables + [core_nodes],
        received("core", longer(double, HALF)) + node_scratch("core", 2),
    )
    images, top, *products = call(
        images_kernel,
        [pair_shape(RANK, LEAF_DEV * LEAF_COLS), pair_shape(4 * RANK, 4 * RANK)] + products_of("mid"),
        [message, box_rows, dense, row_basis, col_basis, cross, paths] + tables,
        (),
        (0,),
    )
    message, row_path, row_own, mid_nodes, gram = call(
        row_pair_kernel,
        [(groups,) + double, path_shape("row"), stat, nodes_of("mid"), (HALF + 8, RANK)],
        [me] + products + swap_parts(message, "row") + tables + [row_nodes, diagonal],
        received("row", longer(double, 2 * HALF)) + node_scratch("row", 2),
    )
    message, mid_path, mid_own = call(
        mid_pair_kernel,
        [(1,) + longer(double, HALF + 8), path_shape("mid"), stat],
        [me, swap_mid(message)] + tables + [mid_nodes, gram],
        node_scratch("mid", 2),
    )
    v, x, alpha, rho, message, top_nodes = call(
        middle_kernel,
        [col_shape, col_shape, tile, tile, (1,) + double, nodes_shape(4)],
        [me, box_rows]
        + swap_parts(message, "far")
        + [core_path, core_own, row_path, row_own, mid_path, mid_own]
        + [gain]
        + [up_row, top, core_nodes, row_nodes, mid_nodes]
        + [dense, row_basis, col_basis, cross, columns, images, x, own, within(inner, message)],
        [(6,) + tile, (4,) + tile] + received("far", longer(double, HALF + 8)),
    )
    for name, nodes, peers in (
        ("core", core_nodes, 1),
        ("row", row_nodes, groups),
        ("mid", mid_nodes, 1),
    ):
        parts = [swap_mid(message)] if name == "mid" else swap_parts(message, name)
        (message,) = call(
            functools.partial(last_pair_kernel, name),
            [(peers,) + double],
            [me] + parts + tables + [nodes],
            [] if name == "mid" else received(name, double),
        )
    (out,) = call(
        final_kernel,
        [col_shape],
        [me] + swap_parts(message, "far") + [top, top_nodes, beta, alpha, rho, v, x],
        received("far", double),
    )
    return out


def solution(mesh):
    devices = mesh.shape["leaf"]
    return jax.shard_map(
        functools.partial(local_program, devices),
        mesh=mesh,
        in_specs=(
            P(None, "leaf"),
            P("leaf"),
            P("leaf", None, None),
            P("leaf", None, None),
            P("leaf", None, None),
            P("leaf", None, None),
            P("leaf", None, None),
            P("leaf", None, None, None),
            P(),
            P(),
            P(),
        ),
        out_specs=P(None, "leaf"),
        check_vma=False,
    )
```
